32 devices in a mesh: dp: 16 (over z, y, x), tensor: 2 (over core).
Axes of the slice: x: 2, y: 2, z: 4, core: 2. Of those that a mesh axis runs over, the one named last changes fastest.
Arguments:
- tokens: bfloat16 [4096, 2048], P(('dp', 'tensor')), may hold values from -6 to 6
- norm1_gain: float32 [2048], replicated, may hold values from 0.1 to 1.9
- w_query: bfloat16 [2048, 2048], P(None, 'tensor'), may hold values from -0.125 to 0.125
- w_key: bfloat16 [2048, 2048], P(None, 'tensor'), may hold values from -0.125 to 0.125
- w_value: bfloat16 [2048, 2048], P(None, 'tensor'), may hold values from -0.125 to 0.125
- w_beta: bfloat16 [2048, 16], P(None, 'tensor'), may hold values from -0.125 to 0.125
- w_gate_out: bfloat16 [2048, 2048], P(None, 'tensor'), may hold values from -0.125 to 0.125
- conv_weights: float32 [3, 4, 2048], P(None, None, 'tensor'), may hold values from -3 to 3
- head_gain: float32 [128], replicated, may hold values from 0.1 to 1.9
- w_out: bfloat16 [2048, 2048], P('tensor'), may hold values from -0.1875 to 0.1875
- norm2_gain: float32 [2048], replicated, may hold values from 0.1 to 1.9
- w_gate: bfloat16 [2048, 5632], P(None, 'tensor'), may hold values from -0.125 to 0.125
- w_up: bfloat16 [2048, 5632], P(None, 'tensor'), may hold values from -0.125 to 0.125
- w_down: bfloat16 [5632, 2048], P('tensor'), may hold values from -0.109375 to 0.109375
- cotangent: bfloat16 [4096, 2048], P(('dp', 'tensor')), may hold values from -6 to 6
Outputs:
- block_out: bfloat16 [4096, 2048], P(('dp', 'tensor'))
- input_grad: float32 [4096, 2048], P(('dp', 'tensor'))
- grad_norm1: float32 [2048], replicated
- grad_query: float32 [2048, 2048], P('dp', 'tensor')
- grad_key: float32 [2048, 2048], P('dp', 'tensor')
- grad_value: float32 [2048, 2048], P('dp', 'tensor')
- grad_beta: float32 [2048, 16], P('dp', 'tensor')
- grad_gate_out: float32 [2048, 2048], P('dp', 'tensor')
- grad_conv: float32 [3, 4, 2048], P(None, None, 'tensor')
- grad_head_gain: float32 [128], replicated
- grad_out: float32 [2048, 2048], P('tensor', 'dp')
- grad_norm2: float32 [2048], replicated
- grad_gate: float32 [2048, 5632], P('dp', 'tensor')
- grad_up: float32 [2048, 5632], P('dp', 'tensor')
- grad_down: float32 [5632, 2048], P('tensor', 'dp')
The draws below stay inside these ranges and needn't reach their ends.
All inputs are finite; a program needn't handle non-finite values.
Results may differ from the reference program's by a relative error of at most 0.017.
Values may be sent and summed in bfloat16 or wider, within the bound.
A program may use at most 320 MiB of HBM per device.

```python
import jax
import jax.numpy as jnp
from jax import lax

D = 2048
HEADS = 16
HEAD_DIM = 128
FF = 5632
SPAN = 64
CONV = 4
LEN = 256
TOKENS = 4096


def strengthened(values, stream_key, source, target, blocks, factor):
    owner, partner = [(jnp.arange(values.shape[axis_at]) // (values.shape[axis_at] // blocks)).reshape([-1 if axis == axis_at else 1 for axis in range(values.ndim)]) for axis_at in (source, target)]
    chosen = jax.random.permutation(stream_key, blocks)[partner]
    strong = (owner == chosen) | (owner == (partner + blocks // 2) % blocks)
    return jnp.where(strong, factor * values, values)


def block_scale(stream_key, shape, shards, least, largest):
    factor_of, own = 1.0, jax.random.fold_in(stream_key, 6)
    for dim, parts in shards:
        steps = jnp.exp(jax.random.uniform(jax.random.fold_in(own, dim), (parts,), jnp.float32, least / len(shards), largest / len(shards)))
        factor_of = factor_of * jnp.repeat(steps, shape[dim] // parts).reshape([-1 if axis == dim else 1 for axis in range(len(shape))])
    return factor_of


def normal_values(key, dims, deviation, most, shards=(), dtype=jnp.bfloat16):
    gain = block_scale(key, dims, shards, -0.22, 0.18) if shards else 1.0
    values = jax.random.normal(key, dims, jnp.float32) * deviation * gain
    return jnp.minimum(jnp.maximum(values, -most), most).astype(dtype)


def heavy_noise(own_key, shape, spread, most, cuts, heavy, held_as=jnp.bfloat16):
    array = spread * jax.random.normal(own_key, shape, jnp.float32)
    if cuts:
        array = array * block_scale(own_key, shape, cuts, -0.22, 0.18)
    return jnp.clip(strengthened(array, jax.random.fold_in(own_key, 3), *heavy), -most, most).astype(held_as)


def setup_inputs(seed: int = 0) -> dict:
    streams_of = jax.random.split(jax.random.key(seed), 16)
    tokens = heavy_noise(streams_of[0], (TOKENS, D), 1.0, 6.0, ((0, 32),), (0, 1, 32, 2.75))
    norm1_gain = jnp.clip(1.0 + 0.18 * jax.random.normal(streams_of[1], (D,), jnp.float32), 0.1, 1.9)
    w_query = normal_values(streams_of[2], (D, HEADS * HEAD_DIM), D ** -0.5, 0.125, ((1, 2),))
    w_key = normal_values(streams_of[3], (D, HEADS * HEAD_DIM), D ** -0.5, 0.125, ((1, 2),))
    w_value = normal_values(streams_of[4], (D, HEADS * HEAD_DIM), D ** -0.5, 0.125, ((1, 2),))
    w_beta = normal_values(streams_of[5], (D, HEADS), D ** -0.5, 0.125, ((1, 2),))
    w_gate_out = normal_values(streams_of[6], (D, HEADS * HEAD_DIM), D ** -0.5, 0.125, ((1, 2),))
    conv_weights = normal_values(streams_of[7], (3, CONV, HEADS * HEAD_DIM), CONV ** -0.5, 3.0, ((2, 2),), jnp.float32)
    head_gain = jnp.clip(1.0 + 0.18 * jax.random.normal(streams_of[8], (HEAD_DIM,), jnp.float32), 0.1, 1.9)
    w_out = normal_values(streams_of[9], (HEADS * HEAD_DIM, D), (HEADS * HEAD_DIM // 2) ** -0.5, 0.1875, ((0, 2),))
    norm2_gain = jnp.clip(1.0 + 0.18 * jax.random.normal(streams_of[10], (D,), jnp.float32), 0.1, 1.9)
    w_gate = normal_values(streams_of[11], (D, FF), D ** -0.5, 0.125, ((1, 2),))
    w_up = normal_values(streams_of[12], (D, FF), D ** -0.5, 0.125, ((1, 2),))
    w_down = normal_values(streams_of[13], (FF, D), (FF // 2) ** -0.5, 0.109375, ((0, 2),))
    cotangent = heavy_noise(streams_of[14], (TOKENS, D), 1.0, 6.0, ((0, 32),), (0, 1, 32, 2.75))
    return {"tokens": tokens, "norm1_gain": norm1_gain, "w_query": w_query, "w_key": w_key, "w_value": w_value, "w_beta": w_beta, "w_gate_out": w_gate_out, "conv_weights": conv_weights, "head_gain": head_gain, "w_out": w_out, "norm2_gain": norm2_gain, "w_gate": w_gate, "w_up": w_up, "w_down": w_down, "cotangent": cotangent}


highest = lax.Precision.HIGHEST
norm_eps = 1e-06
unit_eps = 1e-06

@jax.custom_vjp
def low(v):
    return lax.optimization_barrier(v.astype(jnp.bfloat16)).astype(jnp.float32)

@jax.custom_vjp
def low_back(v):
    return v

def low_keep(v):
    return (low(v), None)

def low_pass(kept, grad):
    return (grad,)

def back_keep(v):
    return (v, None)

def back_low(kept, grad):
    return (low(grad),)
low.defvjp(low_keep, low_pass)
low_back.defvjp(back_keep, back_low)

def matmul(left, right):
    return jnp.dot(left.astype(jnp.float32), right.astype(jnp.float32), preferred_element_type=jnp.float32, precision=highest)

def root_scaled(matrix):
    return matrix * lax.rsqrt(lax.optimization_barrier(jnp.mean(matrix * matrix, -1, keepdims=True)) + norm_eps)

def causal_conv(matrix, conv_taps):
    padded = jnp.pad(matrix, ((CONV - 1, 0), (0, 0)))
    summed = jnp.zeros_like(matrix)
    for offset in range(CONV):
        summed = summed + padded[offset:offset + matrix.shape[0]] * conv_taps[offset]
    return summed

def unit_rows(matrix):
    return matrix * lax.rsqrt(lax.optimization_barrier(jnp.sum(matrix * matrix, -1, keepdims=True)) + unit_eps)

def block_step(carried_state, pieces):
    queries, keys, values_h, beta_rates = pieces
    block_rows = keys.shape[1]
    row_index = lax.broadcasted_iota(jnp.int32, (block_rows, block_rows), 0)
    col_index = lax.broadcasted_iota(jnp.int32, (block_rows, block_rows), 1)
    weighted_keys = keys * beta_rates[..., None]
    weighted_values = values_h * beta_rates[..., None]
    key_inner = jnp.einsum('hid,hjd->hij', weighted_keys, keys, precision=highest)
    lower_part = jnp.where(row_index > col_index, key_inner, 0.0)
    solved = jax.scipy.linalg.solve_triangular(lower_part, jnp.concatenate([weighted_keys, weighted_values], -1), lower=True, unit_diagonal=True)
    head_width = keys.shape[-1]
    corrected = solved[..., head_width:] - jnp.einsum('hid,hde->hie', solved[..., :head_width], carried_state, precision=highest)
    scores = jnp.einsum('hid,hjd->hij', queries, keys, precision=highest)
    scores = jnp.where(row_index >= col_index, scores, 0.0)
    output = jnp.einsum('hid,hde->hie', queries, carried_state, precision=highest) + jnp.einsum('hij,hje->hie', scores, corrected, precision=highest)
    carried_state = carried_state + jnp.einsum('hid,hie->hde', keys, corrected, precision=highest)
    return (carried_state, output)

def delta_rule(queries, keys, values_h, beta_rates):
    length, head_count, head_width = queries.shape
    blocks = length // SPAN

    def to_blocks(matrix):
        return matrix.reshape(blocks, SPAN, head_count, head_width).transpose(0, 2, 1, 3)
    beta_blocks = beta_rates.reshape(blocks, SPAN, head_count).transpose(0, 2, 1)
    initial = jnp.zeros((head_count, head_width, head_width), jnp.float32)
    _, outputs = lax.scan(jax.checkpoint(block_step), initial, (to_blocks(queries), to_blocks(keys), to_blocks(values_h), beta_blocks))
    return outputs.transpose(0, 2, 1, 3).reshape(length, head_count, head_width)

def delta_mixer(query_in, key_in, value_in, beta_in, gate_in, conv_weights, head_gain):
    length = query_in.shape[0]
    head_count = beta_in.shape[1]
    queries = jax.nn.silu(causal_conv(query_in, conv_weights[0])).reshape(length, head_count, HEAD_DIM)
    keys = jax.nn.silu(causal_conv(key_in, conv_weights[1])).reshape(length, head_count, HEAD_DIM)
    values_h = jax.nn.silu(causal_conv(value_in, conv_weights[2])).reshape(length, head_count, HEAD_DIM)
    queries = unit_rows(queries) * HEAD_DIM ** (-0.5)
    keys = unit_rows(keys)
    beta_rates = jax.nn.sigmoid(beta_in)
    delta_out = delta_rule(queries, keys, values_h, beta_rates)
    normed = delta_out * lax.rsqrt(lax.optimization_barrier(jnp.mean(delta_out * delta_out, -1, keepdims=True)) + norm_eps) * head_gain
    return normed.reshape(length, -1) * jax.nn.silu(gate_in)

def block_forward(params, single):
    norm1_gain, w_query, w_key, w_value, w_beta, w_gate_out, conv_weights, head_gain, w_out, norm2_gain, w_gate, w_up, w_down = params
    first_normed = low(root_scaled(single) * norm1_gain)
    query_in = low_back(matmul(first_normed, w_query))
    key_in = low_back(matmul(first_normed, w_key))
    value_in = low_back(matmul(first_normed, w_value))
    beta_in = low_back(matmul(first_normed, w_beta))
    gate_in = low_back(matmul(first_normed, w_gate_out))
    mixed = low(delta_mixer(query_in, key_in, value_in, beta_in, gate_in, conv_weights, head_gain))
    hidden_state = single + low_back(matmul(mixed, w_out))
    second_normed = low(root_scaled(hidden_state) * norm2_gain)
    gate_pre = low_back(matmul(second_normed, w_gate))
    up_pre = low_back(matmul(second_normed, w_up))
    product = low(jax.nn.silu(gate_pre) * up_pre)
    return hidden_state + matmul(product, w_down)

def reference(tokens, norm1_gain, w_query, w_key, w_value, w_beta, w_gate_out, conv_weights, head_gain, w_out, norm2_gain, w_gate, w_up, w_down, cotangent):
    params = tuple((item.astype(jnp.float32) for item in (norm1_gain, w_query, w_key, w_value, w_beta, w_gate_out, conv_weights, head_gain, w_out, norm2_gain, w_gate, w_up, w_down)))
    inputs = tokens.astype(jnp.float32)

    def forward(params, inputs):
        sequences = inputs.reshape(-1, LEN, D)

        def visit_one(carried, single):
            return (carried, jax.checkpoint(block_forward)(params, single))
        _, outputs = lax.scan(visit_one, jnp.zeros((), jnp.float32), sequences)
        return outputs.reshape(-1, D)
    result, pullback = jax.vjp(forward, params, inputs)
    gradients, input_grad = pullback(cotangent.astype(jnp.float32))
    grad_norm1, grad_query, grad_key, grad_value, grad_beta, grad_gate_out, grad_conv, grad_head_gain, grad_out, grad_norm2, grad_gate, grad_up, grad_down = gradients
    return (result.astype(jnp.bfloat16), input_grad, grad_norm1, grad_query, grad_key, grad_value, grad_beta, grad_gate_out, grad_conv, grad_head_gain, grad_out, grad_norm2, grad_gate, grad_up, grad_down)
```

```python
import functools

import jax
import jax.numpy as jnp
from jax import lax
from jax.experimental import pallas as pl
from jax.experimental.pallas import tpu as pltpu
from jax.sharding import PartitionSpec as P

HEAD = 128
CONV = 4
PAIR = 2 * HEAD
F32 = jnp.float32
BF16 = jnp.bfloat16
norm_eps = 1e-06
unit_eps = 1e-06
VMEM_LIMIT = 56 * 1024 * 1024

NN = (((1,), (0,)), ((), ()))
NT = (((1,), (1,)), ((), ()))
TN = (((0,), (0,)), ((), ()))


def dot(left, right, dims=NN):
    return lax.dot_general(left, right, dims, preferred_element_type=F32)


def halves(value):
    high = value.astype(BF16)
    return high, (value - high.astype(F32)).astype(BF16)


def dot3(left, right, dims=NN):
    left_high, left_low = halves(left)
    right_high, right_low = halves(right)
    return (
        dot(left_high, right_low, dims) + dot(left_low, right_high, dims)
    ) + dot(left_high, right_high, dims)


def rows_down(value, shift):
    if shift == 0:
        return value
    row = lax.broadcasted_iota(jnp.int32, value.shape, 0)
    return jnp.where(row >= shift, pltpu.roll(value, shift, 0), 0.0)


def rows_up(value, shift):
    if shift == 0:
        return value
    rows = value.shape[0]
    row = lax.broadcasted_iota(jnp.int32, value.shape, 0)
    return jnp.where(row < rows - shift, pltpu.roll(value, rows - shift, 0), 0.0)


def causal_conv(value, taps):
    total = value * taps[CONV - 1 : CONV]
    for offset in range(CONV - 1):
        total = total + rows_down(value, CONV - 1 - offset) * taps[offset : offset + 1]
    return total


def sigmoid(value):
    return 1.0 / (1.0 + jnp.exp(-value))


def tri_mask(rows, strict):
    row = lax.broadcasted_iota(jnp.int32, (rows, rows), 0)
    col = lax.broadcasted_iota(jnp.int32, (rows, rows), 1)
    return row > col if strict else row >= col


def unit_lower_inverse(lower):
    size = lower.shape[0]
    row = lax.broadcasted_iota(jnp.int32, (size, size), 0)
    col = lax.broadcasted_iota(jnp.int32, (size, size), 1)
    level, inverse = 0, None
    while (1 << level) < size:
        mask = (
            ((row >> (level + 1)) == (col >> (level + 1)))
            & (((row >> level) & 1) == 1)
            & (((col >> level) & 1) == 0)
        )
        part = jnp.where(mask, lower, 0.0)
        if inverse is None:
            inverse = jnp.where(row == col, 1.0, 0.0) - part
        else:
            inverse = inverse - dot3(inverse, dot3(part, inverse))
        level += 1
    return inverse


def head_column(values, head):
    lane = lax.broadcasted_iota(jnp.int32, values.shape, 1)
    return jnp.sum(jnp.where(lane == head, values, 0.0), -1, keepdims=True)


def mixer_forward(
    xn_ref, wq_ref, wk_ref, wv_ref, wg_ref, wb_ref, conv_ref, gain_ref, wo_ref,
    mixed_ref, part_ref, q_ref, k_ref, v_ref, g_ref, beta_ref, inv_ref, u_ref, o_ref,
    total,
):
    step = pl.program_id(0)
    xn = xn_ref[...]
    rows = xn.shape[0]
    half = rows // 2

    @pl.when(step == 0)
    def _():
        beta_ref[...] = dot(xn, wb_ref[...])
        total[...] = jnp.zeros_like(total)

    query_in = dot(xn, wq_ref[...])
    key_in = dot(xn, wk_ref[...])
    value_in = dot(xn, wv_ref[...])
    gate_in = dot(xn, wg_ref[...])
    q_ref[...] = query_in
    k_ref[...] = key_in
    v_ref[...] = value_in
    g_ref[...] = gate_in
    beta_all = sigmoid(beta_ref[...])
    conv_q = causal_conv(query_in, conv_ref[0])
    conv_k = causal_conv(key_in, conv_ref[1])
    conv_v = causal_conv(value_in, conv_ref[2])
    query_act = conv_q * sigmoid(conv_q)
    key_act = conv_k * sigmoid(conv_k)
    value_act = conv_v * sigmoid(conv_v)
    gate_act = gate_in * sigmoid(gate_in)
    strict = tri_mask(rows, True)
    causal = tri_mask(rows, False)
    for head in range(2):
        cols = slice(head * HEAD, (head + 1) * HEAD)
        queries = query_act[:, cols]
        queries = queries * lax.rsqrt(jnp.sum(queries * queries, -1, keepdims=True) + unit_eps)
        queries = queries * HEAD**-0.5
        keys = key_act[:, cols]
        keys = keys * lax.rsqrt(jnp.sum(keys * keys, -1, keepdims=True) + unit_eps)
        values = value_act[:, cols]
        beta = head_column(beta_all, 2 * step + head)
        lower = jnp.where(strict, dot3(keys, keys, NT) * beta, 0.0)
        first = unit_lower_inverse(lower[:half, :half])
        second = unit_lower_inverse(lower[half:, half:])
        inv_ref[head, 0] = first
        inv_ref[head, 1] = second
        weighted = values * beta
        upper_u = dot3(first, weighted[:half])
        lower_u = dot3(second, weighted[half:] - dot3(lower[half:, :half], upper_u))
        updates = jnp.concatenate([upper_u, lower_u], 0)
        u_ref[:, cols] = updates
        scores = jnp.where(causal, dot3(queries, keys, NT), 0.0)
        output = dot3(scores, updates)
        o_ref[:, cols] = output
        normed = output * lax.rsqrt(jnp.mean(output * output, -1, keepdims=True) + norm_eps)
        mixed_ref[0, :, cols] = (normed * gain_ref[...] * gate_act[:, cols]).astype(BF16)
    total[...] += dot(mixed_ref[0], wo_ref[...])

    @pl.when(step == pl.num_programs(0) - 1)
    def _():
        part_ref[...] = total[...].astype(BF16)


def call_mixer_forward(xn, wq, wk, wv, wg, wb, conv, gain, wo):
    rows, width = xn.shape
    cols = wq.shape[1]
    pairs = cols // PAIR
    heads = wb.shape[1]
    whole = lambda *shape: pl.BlockSpec(shape, lambda i: (0,) * len(shape))
    column = pl.BlockSpec((rows, PAIR), lambda i: (0, i))
    weight = pl.BlockSpec((width, PAIR), lambda i: (0, i))
    wide = jax.ShapeDtypeStruct((rows, cols), F32)
    return pl.pallas_call(
        mixer_forward,
        grid=(pairs,),
        in_specs=[
            whole(rows, width), weight, weight, weight, weight, whole(width, heads),
            pl.BlockSpec((3, CONV, PAIR), lambda i: (0, 0, i)), whole(1, HEAD),
            pl.BlockSpec((PAIR, width), lambda i: (i, 0)),
        ],
        out_specs=[
            pl.BlockSpec((1, rows, PAIR), lambda i: (i // (pairs // 2), 0, i % (pairs // 2))),
            whole(rows, width), column, column, column, column, whole(rows, heads),
            pl.BlockSpec((2, 2, rows // 2, rows // 2), lambda i: (i, 0, 0, 0)), column, column,
        ],
        out_shape=[
            jax.ShapeDtypeStruct((2, rows, cols // 2), BF16),
            jax.ShapeDtypeStruct((rows, width), BF16),
            wide, wide, wide, wide, jax.ShapeDtypeStruct((rows, heads), F32),
            jax.ShapeDtypeStruct((heads, 2, rows // 2, rows // 2), F32), wide, wide,
        ],
        scratch_shapes=[pltpu.VMEM((rows, width), F32)],
        compiler_params=pltpu.CompilerParams(vmem_limit_bytes=VMEM_LIMIT),
        cost_estimate=pl.CostEstimate(
            flops=2 * rows * width * cols * 5 + 10**10, bytes_accessed=5 * width * cols * 2 + 10**7,
            transcendentals=0,
        ),
        name="mixer_forward",
    )(xn, wq, wk, wv, wg, wb, conv, gain, wo)


def silu_slope(value, sig):
    return sig * (1.0 + value * (1.0 - sig))


def mixer_backward(
    dh_ref, wq_ref, wk_ref, wv_ref, wg_ref, wb_ref, conv_ref, gain_ref, wo_ref,
    q_ref, k_ref, v_ref, g_ref, beta_ref, inv_ref, u_ref, o_ref,
    low_ref, bl_ref, part_ref, dconv_ref, dgain_ref,
    total, beta_total,
):
    step = pl.program_id(0)
    rows = dh_ref.shape[0]
    half = rows // 2

    @pl.when(step == 0)
    def _():
        total[...] = jnp.zeros_like(total)
        beta_total[...] = jnp.zeros_like(beta_total)
        dgain_ref[...] = jnp.zeros_like(dgain_ref)

    mixed_grad = dot(dh_ref[...], wo_ref[...], NT)
    query_in = q_ref[...]
    key_in = k_ref[...]
    value_in = v_ref[...]
    gate_in = g_ref[...]
    beta_all = sigmoid(beta_ref[...])
    lane = lax.broadcasted_iota(jnp.int32, beta_all.shape, 1)
    conv_q = causal_conv(query_in, conv_ref[0])
    conv_k = causal_conv(key_in, conv_ref[1])
    conv_v = causal_conv(value_in, conv_ref[2])
    sig_q, sig_k, sig_v = sigmoid(conv_q), sigmoid(conv_k), sigmoid(conv_v)
    sig_g = sigmoid(gate_in)
    query_act = conv_q * sig_q
    key_act = conv_k * sig_k
    value_act = conv_v * sig_v
    gate_act = gate_in * sig_g
    strict = tri_mask(rows, True)
    causal = tri_mask(rows, False)
    grads_q, grads_k, grads_v, grads_g = [], [], [], []
    gain = gain_ref[...]
    for head in range(2):
        cols = slice(head * HEAD, (head + 1) * HEAD)
        raw_q, raw_k, values = query_act[:, cols], key_act[:, cols], value_act[:, cols]
        scale_q = lax.rsqrt(jnp.sum(raw_q * raw_q, -1, keepdims=True) + unit_eps)
        scale_k = lax.rsqrt(jnp.sum(raw_k * raw_k, -1, keepdims=True) + unit_eps)
        queries = raw_q * scale_q * HEAD**-0.5
        keys = raw_k * scale_k
        beta = head_column(beta_all, 2 * step + head)
        updates = u_ref[:, cols]
        output = o_ref[:, cols]
        upstream = mixed_grad[:, cols]
        scale_o = lax.rsqrt(jnp.mean(output * output, -1, keepdims=True) + norm_eps)
        unit_out = output * scale_o
        grads_g.append(upstream * (unit_out * gain))
        d_normed = upstream * gate_act[:, cols]
        dgain_ref[...] += jnp.sum(d_normed * unit_out, 0, keepdims=True)
        d_unit = d_normed * gain
        d_output = scale_o * (d_unit - unit_out * jnp.mean(d_unit * unit_out, -1, keepdims=True))
        inner = dot3(keys, keys, NT)
        lower_21 = inner[half:, :half] * beta[half:]
        scores = jnp.where(causal, dot3(queries, keys, NT), 0.0)
        d_scores = jnp.where(causal, dot3(d_output, updates, NT), 0.0)
        d_updates = dot3(scores, d_output, TN)
        d_right_2 = dot3(inv_ref[head, 1], d_updates[half:], TN)
        d_right_1 = dot3(
            inv_ref[head, 0], d_updates[:half] - dot3(lower_21, d_right_2, TN), TN
        )
        d_right = jnp.concatenate([d_right_1, d_right_2], 0)
        d_lower = jnp.where(strict, -dot3(d_right, updates, NT), 0.0)
        d_beta = jnp.sum(d_lower * inner, -1, keepdims=True) + jnp.sum(
            d_right * values, -1, keepdims=True
        )
        grads_v.append(d_right * beta)
        d_inner = d_lower * beta
        d_keys = dot3(d_scores, queries, TN) + dot3(d_inner, keys) + dot3(d_inner, keys, TN)
        d_queries = dot3(d_scores, keys) * HEAD**-0.5
        grads_q.append(
            scale_q
            * (d_queries - raw_q * (scale_q * scale_q) * jnp.sum(d_queries * raw_q, -1, keepdims=True))
        )
        grads_k.append(
            scale_k
            * (d_keys - raw_k * (scale_k * scale_k) * jnp.sum(d_keys * raw_k, -1, keepdims=True))
        )
        d_beta_in = d_beta * beta * (1.0 - beta)
        beta_total[...] += jnp.where(lane == 2 * step + head, d_beta_in, 0.0)
    for kind, (grads, pre, conv, sig) in enumerate(
        (
            (grads_q, query_in, conv_q, sig_q),
            (grads_k, key_in, conv_k, sig_k),
            (grads_v, value_in, conv_v, sig_v),
        )
    ):
        d_conv = jnp.concatenate(grads, 1) * silu_slope(conv, sig)
        taps = conv_ref[kind]
        d_pre = d_conv * taps[CONV - 1 : CONV]
        for offset in range(CONV):
            shift = CONV - 1 - offset
            dconv_ref[kind, offset : offset + 1, :] = jnp.sum(
                d_conv * rows_down(pre, shift), 0, keepdims=True
            )
            if shift:
                d_pre = d_pre + rows_up(d_conv, shift) * taps[offset : offset + 1]
        low_ref[0, kind] = d_pre.astype(BF16)
    low_ref[0, 3] = (jnp.concatenate(grads_g, 1) * silu_slope(gate_in, sig_g)).astype(BF16)
    total[...] += (
        dot(low_ref[0, 0], wq_ref[...], NT)
        + dot(low_ref[0, 1], wk_ref[...], NT)
        + dot(low_ref[0, 2], wv_ref[...], NT)
        + dot(low_ref[0, 3], wg_ref[...], NT)
    )

    @pl.when(step == pl.num_programs(0) - 1)
    def _():
        bl_ref[...] = beta_total[...].astype(BF16)
        part_ref[...] = (total[...] + dot(bl_ref[...], wb_ref[...], NT)).astype(BF16)


def call_mixer_backward(dh, wq, wk, wv, wg, wb, conv, gain, wo, q, k, v, g, beta, inv, u, o):
    rows, width = dh.shape
    cols = wq.shape[1]
    pairs = cols // PAIR
    heads = wb.shape[1]
    whole = lambda *shape: pl.BlockSpec(shape, lambda i: (0,) * len(shape))
    column = pl.BlockSpec((rows, PAIR), lambda i: (0, i))
    weight = pl.BlockSpec((width, PAIR), lambda i: (0, i))
    taps = pl.BlockSpec((3, CONV, PAIR), lambda i: (0, 0, i))
    return pl.pallas_call(
        mixer_backward,
        grid=(pairs,),
        in_specs=[
            whole(rows, width), weight, weight, weight, weight, whole(width, heads), taps,
            whole(1, HEAD), pl.BlockSpec((PAIR, width), lambda i: (i, 0)),
            column, column, column, column, whole(rows, heads),
            pl.BlockSpec((2, 2, rows // 2, rows // 2), lambda i: (i, 0, 0, 0)), column, column,
        ],
        out_specs=[
            pl.BlockSpec((1, 4, rows, PAIR), lambda i: (i // (pairs // 2), 0, 0, i % (pairs // 2))),
            whole(rows, heads), whole(rows, width), taps, whole(1, HEAD),
        ],
        out_shape=[
            jax.ShapeDtypeStruct((2, 4, rows, cols // 2), BF16),
            jax.ShapeDtypeStruct((rows, heads), BF16),
            jax.ShapeDtypeStruct((rows, width), BF16), jax.ShapeDtypeStruct(conv.shape, F32),
            jax.ShapeDtypeStruct((1, HEAD), F32),
        ],
        scratch_shapes=[pltpu.VMEM((rows, width), F32), pltpu.VMEM((rows, heads), F32)],
        compiler_params=pltpu.CompilerParams(vmem_limit_bytes=VMEM_LIMIT),
        cost_estimate=pl.CostEstimate(
            flops=2 * rows * width * cols * 5 + 2 * 10**10,
            bytes_accessed=5 * width * cols * 2 + 10**7,
            transcendentals=0,
        ),
        name="mixer_backward",
    )(dh, wq, wk, wv, wg, wb, conv, gain, wo, q, k, v, g, beta, inv, u, o)


def mlp_kernel(
    yn_ref, dy_ref, wg_ref, wu_ref, wd_ref,
    low_ref, down_ref, back_ref,
    wg_buf, wu_buf, wd_buf, down_total, back_total, sems,
):
    step = pl.program_id(0)
    steps = pl.num_programs(0)
    hidden = wg_ref.shape[1] // 2

    def copies(index, slot):
        for part in range(2):
            start = pl.multiple_of(part * hidden + index * HEAD, HEAD)
            lanes = pl.ds(part * HEAD, HEAD)
            yield pltpu.make_async_copy(
                wg_ref.at[:, pl.ds(start, HEAD)], wg_buf.at[slot, :, lanes], sems.at[slot, part]
            )
            yield pltpu.make_async_copy(
                wu_ref.at[:, pl.ds(start, HEAD)], wu_buf.at[slot, :, lanes], sems.at[slot, 2 + part]
            )
            yield pltpu.make_async_copy(
                wd_ref.at[pl.ds(start, HEAD), :], wd_buf.at[slot, lanes, :], sems.at[slot, 4 + part]
            )

    slot = lax.rem(step, 2)

    @pl.when(step == 0)
    def _():
        for copy in copies(step, slot):
            copy.start()
        down_total[...] = jnp.zeros_like(down_total)
        back_total[...] = jnp.zeros_like(back_total)

    @pl.when(step + 1 < steps)
    def _():
        for copy in copies(step + 1, 1 - slot):
            copy.start()

    for copy in copies(step, slot):
        copy.wait()
    yn, dy = yn_ref[...], dy_ref[...]
    w_gate, w_up, w_down = wg_buf[slot], wu_buf[slot], wd_buf[slot]
    gate = dot(yn, w_gate)
    up = dot(yn, w_up)
    d_product = dot(dy, w_down, NT)
    sig = sigmoid(gate)
    act = gate * sig
    product = (act * up).astype(BF16)
    gate_grad = (d_product * up * silu_slope(gate, sig)).astype(BF16)
    up_grad = (d_product * act).astype(BF16)
    down_total[...] += dot(product, w_down)
    back_total[...] += dot(gate_grad, w_gate, NT) + dot(up_grad, w_up, NT)
    for kind, value in enumerate((product, gate_grad, up_grad)):
        low_ref[0, kind] = value[:, :HEAD]
        low_ref[1, kind] = value[:, HEAD:]

    @pl.when(step == steps - 1)
    def _():
        down_ref[...] = down_total[...].astype(BF16)
        back_ref[...] = back_total[...].astype(BF16)


def call_mlp(yn, dy, w_gate, w_up, w_down):
    rows, width = yn.shape
    hidden = w_gate.shape[1] // 2
    whole = lambda *shape: pl.BlockSpec(shape, lambda i: (0,) * len(shape))
    anywhere = pl.BlockSpec(memory_space=pl.ANY)
    tile = pl.BlockSpec((2, 3, rows, HEAD), lambda i: (0, 0, 0, i))
    return pl.pallas_call(
        mlp_kernel,
        grid=(hidden // HEAD,),
        in_specs=[whole(rows, width), whole(rows, width), anywhere, anywhere, anywhere],
        out_specs=[tile, whole(rows, width), whole(rows, width)],
        out_shape=[
            jax.ShapeDtypeStruct((2, 3, rows, hidden), BF16),
            jax.ShapeDtypeStruct((rows, width), BF16),
            jax.ShapeDtypeStruct((rows, width), BF16),
        ],
        scratch_shapes=[
            pltpu.VMEM((2, width, PAIR), BF16), pltpu.VMEM((2, width, PAIR), BF16),
            pltpu.VMEM((2, PAIR, width), BF16), pltpu.VMEM((rows, width), F32),
            pltpu.VMEM((rows, width), F32), pltpu.SemaphoreType.DMA((2, 6)),
        ],
        compiler_params=pltpu.CompilerParams(vmem_limit_bytes=VMEM_LIMIT),
        cost_estimate=pl.CostEstimate(
            flops=12 * rows * width * w_gate.shape[1], bytes_accessed=6 * width * w_gate.shape[1],
            transcendentals=0,
        ),
        name="mlp",
    )(yn, dy, w_gate, w_up, w_down)


def norm_back(upstream, inputs, scale_rows, gain_row):
    scaled_grad = upstream * gain_row
    return scale_rows * (
        scaled_grad
        - inputs * scale_rows * scale_rows * jnp.mean(scaled_grad * inputs, -1, keepdims=True)
    )


def take(value, axis, index):
    return lax.dynamic_index_in_dim(value, index, axis, keepdims=False)


def sibling(value):
    return lax.ppermute(value, "tensor", [(0, 1), (1, 0)])


def both_rows(mine, other, core):
    axis = mine.ndim - 2
    return jnp.where(
        core == 0, jnp.concatenate([mine, other], axis), jnp.concatenate([other, mine], axis)
    )


def swap_sum(partial, core):
    parts = partial.reshape(2, -1, partial.shape[-1])
    received = sibling(take(parts, 0, 1 - core))
    return take(parts, 0, core).astype(F32) + received.astype(F32)


BIT_X, BIT_Y, BIT_ZA, BIT_ZB = 1, 2, 4, 8
GATHER_1, GATHER_2, REDUCE_1, REDUCE_2 = BIT_X, BIT_ZA, BIT_Y, BIT_ZB
CHIPS = 16
MESH = pl.DeviceIdType.MESH
KINDS = ((1, 0, 2), (0, 0, 0), (0, 1, 1), (0, 2, 1), (1, 1, 3), (1, 2, 3), (1, 3, 3), (1, 4, 3))
CROSSED = (0, 1)


def block_place(block):
    bit = lambda mask: int((block & mask) != 0)
    return bit(GATHER_1), bit(REDUCE_1) * 4 + bit(REDUCE_2) * 2 + bit(GATHER_2)


def trade(value, bit):
    return lax.ppermute(value, "dp", [(index, index ^ bit) for index in range(CHIPS)])


def grads_kernel(
    cot_ref, second_ref, state_ref, first_ref, wide_ref, mixed_ref, low_ref,
    *rest,
):
    outs, rest = rest[:8], rest[8:]
    own, left, gw, gn, s1w, s1n, r1w, r1n, k2w, k2n, s2w, s2n, r2w, r2n, sfw, sfn, rfw, rfn = rest[:18]
    ow, on, ct_w, ct_n, left_sems, right_sems, own_sems, sum_sems, out_sems = rest[18:]
    right, send1, recv1, keep2 = (gw, gn), (s1w, s1n), (r1w, r1n), (k2w, k2n)
    send2, recv2, sendf, recvf = (s2w, s2n), (r2w, r2n), (sfw, sfn), (rfw, rfn)
    out_buf, cross_buf = (ow, on), (ct_w, ct_n)
    chip = lax.axis_index("dp")
    core = lax.axis_index("tensor")
    bit = {mask: lax.rem(chip // mask, 2) for mask in (1, 2, 4, 8)}
    to = {mask: (chip + mask * (1 - 2 * bit[mask]), core) for mask in (1, 2, 4, 8)}
    near = (chip, 1 - core)
    tokens = first_ref.shape[0]
    half1, half2 = bit[GATHER_1], bit[GATHER_2]

    barrier = pltpu.get_barrier_semaphore()
    for target in (*to.values(), near):
        pl.semaphore_signal(barrier, inc=1, device_id=target, device_id_type=MESH)
    pl.semaphore_wait(barrier, 5)

    def remote(source, target, sems, index, device):
        return pltpu.make_async_remote_copy(
            src_ref=source, dst_ref=target, send_sem=sems.at[(0, *index)],
            recv_sem=sems.at[(1, *index)], device_id=device, device_id_type=MESH,
        )

    def left_rows(a, piece):
        start = pl.multiple_of((2 * piece + core) * tokens, tokens)
        return left.at[a, pl.ds(start, tokens), :]

    def left_copy(a, name):
        place = {"one": 0, "two": 1, "far": 2}
        if name == "one":
            return remote(own.at[a, 1 - half1], left_rows(a, 1), left_sems, (a, 0), to[GATHER_1])
        if name == "two":
            return remote(own.at[a, half1], left_rows(a, 2), left_sems, (a, 1), to[GATHER_2])
        if name == "far":
            return remote(left_rows(a, 1), left_rows(a, 3), left_sems, (a, 2), to[GATHER_2])
        piece = int(name)
        return remote(left_rows(a, piece), left_rows(a, piece), left_sems, (a, 3 + piece), near)

    def left_start(a):
        natural = (cot_ref, second_ref, state_ref, first_ref)[a]
        for block in range(CHIPS):
            half, place = block_place(block)
            own[a, half, :, place * HEAD : (place + 1) * HEAD] = natural[
                :, block * HEAD : (block + 1) * HEAD
            ]
        left_copy(a, "one").start()
        left_copy(a, "two").start()
        left[a, pl.ds(pl.multiple_of(core * tokens, tokens), tokens), :] = own[a, half1]
        left_copy(a, "0").start()

    def left_middle(a):
        left_copy(a, "one").wait_recv()
        left_copy(a, "far").start()
        left_copy(a, "1").start()
        left_copy(a, "two").wait_recv()
        left_copy(a, "2").start()

    def left_end(a):
        left_copy(a, "far").wait_recv()
        left_copy(a, "3").start()
        for piece in range(4):
            left_copy(a, str(piece)).wait_recv()

    def left_sent(a):
        for name in ("one", "two", "far", "0", "1", "2", "3"):
            left_copy(a, name).wait_send()

    def source(kind, half):
        group, place, _ = KINDS[kind]
        if group == 0:
            return wide_ref.at[half, place]
        return mixed_ref.at[half] if place == 0 else low_ref.at[half, place - 1]

    def right_rows(kind, piece):
        group, place, _ = KINDS[kind]
        return right[group].at[place, 2 * piece * tokens : 2 * (piece + 1) * tokens, :]

    def right_copy(kind, name):
        if name == "one":
            return remote(
                source(kind, half2), right_rows(kind, 1), right_sems, (kind, 0), to[GATHER_1]
            )
        if name == "two":
            return remote(
                source(kind, 1 - half2), right_rows(kind, 2), right_sems, (kind, 1), to[GATHER_2]
            )
        return remote(
            right_rows(kind, 2), right_rows(kind, 3), right_sems, (kind, 2), to[GATHER_1]
        )

    def own_copy(kind):
        return pltpu.make_async_copy(source(kind, half2), right_rows(kind, 0), own_sems.at[kind])

    def right_start(kind):
        right_copy(kind, "two").start()
        right_copy(kind, "one").start()
        own_copy(kind).start()

    def right_middle(kind):
        right_copy(kind, "two").wait_recv()
        right_copy(kind, "far").start()

    def right_end(kind):
        right_copy(kind, "one").wait_recv()
        right_copy(kind, "far").wait_recv()
        own_copy(kind).wait()

    def product(kind, start):
        group, place, a = KINDS[kind]
        columns = pl.ds(pl.multiple_of(start, 2 * HEAD), 2 * HEAD)
        return dot(left[a, :, columns], right[group][place], TN)

    def sum_copy(kind, stage):
        group, place, _ = KINDS[kind]
        slot = kind % 2
        source_ref = (send1, send2, sendf)[stage][group].at[slot]
        target_ref = (recv1, recv2, recvf)[stage][group].at[place]
        device = to[(REDUCE_1, REDUCE_2, GATHER_2)[stage]]
        return remote(source_ref, target_ref, sum_sems, (kind, stage), device)

    last, stored = {}, {}

    def slot_free(kind, stage):
        key = (KINDS[kind][0], kind % 2, stage)
        if key in last:
            sum_copy(last[key], stage).wait_send()
        last[key] = kind

    mine1, mine2 = bit[REDUCE_1], bit[REDUCE_2]
    quarter = 2 * HEAD

    def first_sums(kind):
        group = KINDS[kind][0]
        slot_free(kind, 0)

        @pl.loop(0, 2)
        def _(index):
            rows = pl.ds(pl.multiple_of(index * quarter, quarter), quarter)
            send1[group][kind % 2, rows, :] = product(
                kind, (1 - mine1) * 2 * quarter + index * quarter
            ).astype(BF16)

        sum_copy(kind, 0).start()

    def second_sums(kind):
        group, place, _ = KINDS[kind]
        slot_free(kind, 1)
        sum_copy(kind, 0).wait_recv()

        def total(which):
            rows = pl.ds(pl.multiple_of(which * quarter, quarter), quarter)
            return product(kind, mine1 * 2 * quarter + which * quarter) + recv1[group][
                place, rows, :
            ].astype(F32)

        send2[group][kind % 2] = total(1 - mine2).astype(BF16)
        sum_copy(kind, 1).start()
        keep2[group][kind % 2] = total(mine2)

    def out_copy(kind):
        group = KINDS[kind][0]
        buffer = (cross_buf if kind in CROSSED else out_buf)[group]
        return pltpu.make_async_copy(buffer.at[kind % 2], outs[kind], out_sems.at[kind])

    def store(kind, half, value):
        group = KINDS[kind][0]
        width = value.shape[1]
        start = pl.multiple_of(half * width, HEAD)
        if kind in CROSSED:
            cross_buf[group][kind % 2, pl.ds(start, width), :] = value.T
        else:
            out_buf[group][kind % 2, :, pl.ds(start, width)] = value

    def third_sums(kind):
        group, place, _ = KINDS[kind]
        slot_free(kind, 2)
        sum_copy(kind, 1).wait_recv()

        def total(which):
            rows = pl.ds(pl.multiple_of(which * HEAD, HEAD), HEAD)
            return keep2[group][kind % 2, rows, :] + recv2[group][place, rows, :].astype(F32)

        sendf[group][kind % 2] = total(1 - half2).astype(BF16)
        sum_copy(kind, 2).start()
        key = (group, kind % 2, kind in CROSSED)
        if key in stored:
            out_copy(stored[key]).wait()
        stored[key] = kind
        store(kind, half2, total(half2))

    def finish(kind):
        group, place, _ = KINDS[kind]
        sum_copy(kind, 2).wait_recv()
        store(kind, 1 - half2, recvf[group][place].astype(F32))
        out_copy(kind).start()

    count = len(KINDS)
    started, middled, ended = [], [], []

    def once(done, a, action):
        if a not in done:
            done.append(a)
            action(a)

    def start(kind):
        once(started, KINDS[kind][2], left_start)
        right_start(kind)

    def middle(kind):
        once(middled, KINDS[kind][2], left_middle)
        right_middle(kind)

    def end(kind):
        once(ended, KINDS[kind][2], left_end)
        right_end(kind)

    start(0)
    start(1)
    middle(0)
    for step in range(count + 3):
        if step < count:
            end(step)
        if step + 2 < count:
            start(step + 2)
        if step < count:
            first_sums(step)
        if step + 1 < count:
            middle(step + 1)
        if 0 <= step - 1 < count:
            second_sums(step - 1)
        if 0 <= step - 2 < count:
            third_sums(step - 2)
        if 0 <= step - 3 < count:
            finish(step - 3)
    for a in range(4):
        left_sent(a)
    for kind in range(count):
        for name in ("one", "two", "far"):
            right_copy(kind, name).wait_send()
    for key, kind in last.items():
        sum_copy(kind, key[2]).wait_send()
    for kind in stored.values():
        out_copy(kind).wait()


def call_grads(cot, second, state, first, wide, mixed, low):
    tokens, width = first.shape
    rows = 2 * tokens
    wide_cols, cols = wide.shape[-1], low.shape[-1]
    vmem = pl.BlockSpec(memory_space=pltpu.VMEM)
    anywhere = pl.BlockSpec(memory_space=pl.ANY)
    shape = lambda kind: (
        ((2 * (wide_cols, cols)[KINDS[kind][0]], HEAD)) if kind in CROSSED
        else (HEAD, 2 * (wide_cols, cols)[KINDS[kind][0]])
    )
    half = width // 2
    both = lambda count, height, dtype: [
        pltpu.VMEM((count[0], height, wide_cols), dtype), pltpu.VMEM((count[1], height, cols), dtype)
    ]
    dedicated, slots = (3, 5), (2, 2)
    return pl.pallas_call(
        grads_kernel,
        in_specs=[vmem, vmem, vmem, vmem, anywhere, anywhere, anywhere],
        out_specs=[anywhere] * 8,
        out_shape=[jax.ShapeDtypeStruct(shape(kind), F32) for kind in range(8)],
        scratch_shapes=[
            pltpu.VMEM((4, 2, tokens, half), BF16), pltpu.VMEM((4, 8 * tokens, half), BF16),
            *both(dedicated, 4 * rows, BF16),
            *both(slots, half // 2, BF16), *both(dedicated, half // 2, BF16),
            *both(slots, half // 4, F32), *both(slots, half // 4, BF16),
            *both(dedicated, half // 4, BF16), *both(slots, half // 8, BF16),
            *both(dedicated, half // 8, BF16),
            pltpu.VMEM((2, HEAD, 2 * wide_cols), F32), pltpu.VMEM((2, HEAD, 2 * cols), F32),
            pltpu.VMEM((2, 2 * wide_cols, HEAD), F32), pltpu.VMEM((2, 2 * cols, HEAD), F32),
            pltpu.SemaphoreType.DMA((2, 4, 7)), pltpu.SemaphoreType.DMA((2, 8, 3)),
            pltpu.SemaphoreType.DMA((8,)), pltpu.SemaphoreType.DMA((2, 8, 3)),
            pltpu.SemaphoreType.DMA((8,)),
        ],
        compiler_params=pltpu.CompilerParams(
            vmem_limit_bytes=60 * 1024 * 1024, collective_id=1, has_side_effects=True
        ),
        cost_estimate=pl.CostEstimate(
            flops=2 * rows * width * 2 * (3 * wide_cols + 5 * cols), bytes_accessed=10**8,
            transcendentals=0,
        ),
        name="weight_grads",
    )(cot, second, state, first, wide, mixed, low)


def local(
    tokens, norm1_gain, w_query, w_key, w_value, w_beta, w_gate_out, conv_weights, head_gain,
    w_out, norm2_gain, w_gate, w_up, w_down, cotangent, cubic,
):
    core = lax.axis_index("tensor")
    inputs = tokens.astype(F32)
    first_scale = lax.rsqrt(jnp.mean(inputs * inputs, -1, keepdims=True) + norm_eps)
    first_own = (inputs * first_scale * norm1_gain).astype(BF16)
    first_normed = both_rows(first_own, sibling(first_own), core)
    out_grad = both_rows(cotangent, sibling(cotangent), core)
    gain_row = head_gain.reshape(1, HEAD)
    mixed, out_part, *saved = call_mixer_forward(
        first_normed, w_query, w_key, w_value, w_gate_out, w_beta, conv_weights, gain_row, w_out
    )
    hidden_state = inputs + swap_sum(out_part, core)
    second_scale = lax.rsqrt(jnp.mean(hidden_state * hidden_state, -1, keepdims=True) + norm_eps)
    second_own = (hidden_state * second_scale * norm2_gain).astype(BF16)
    second_normed = both_rows(second_own, sibling(second_own), core)

    wide, down_part, back_part = call_mlp(second_normed, out_grad, w_gate, w_up, w_down)
    block_out = hidden_state + swap_sum(down_part, core)
    second_grad = swap_sum(back_part, core)
    norm2_part = jnp.sum(second_grad * hidden_state * second_scale, 0)
    state_grad = cotangent.astype(F32) + norm_back(
        second_grad, hidden_state, second_scale, norm2_gain
    )
    state_own = state_grad.astype(BF16)
    state_rows = both_rows(state_own, sibling(state_own), core)
    low, beta_low, first_part, conv_grad, head_part = (
        call_mixer_backward(
            state_rows, w_query, w_key, w_value, w_gate_out, w_beta, conv_weights, gain_row, w_out,
            *saved,
        )
    )
    first_grad = swap_sum(first_part, core)
    norm1_part = jnp.sum(first_grad * inputs * first_scale, 0)
    input_grad = state_grad + norm_back(first_grad, inputs, first_scale, norm1_gain)
    grad_beta = dot(first_normed, beta_low, TN)

    if cubic:
        grads = call_grads(cotangent, second_own, state_own, first_own, wide, mixed, low)
        grad_out, grad_down, grad_gate, grad_up = grads[:4]
        grad_query, grad_key, grad_value, grad_gate_out = grads[4:]
        small = jnp.concatenate(
            [
                item.reshape(-1, HEAD)
                for item in (conv_grad, grad_beta, norm1_part, norm2_part, head_part)
            ]
        )
        for bit in (1, 2, 4, 8):
            small = small + trade(small, bit)
        taps = conv_grad.size // HEAD
        beta_rows = grad_beta.size // HEAD
        conv_total = small[:taps].reshape(conv_grad.shape)
        beta_sum = lax.dynamic_slice_in_dim(
            small[taps : taps + beta_rows].reshape(grad_beta.shape),
            lax.axis_index("dp") * (grad_beta.shape[0] // 16), grad_beta.shape[0] // 16,
        )
        gains = small[taps + beta_rows :]
        gains = (gains + sibling(gains)).reshape(-1)
        width = norm1_part.size
        norm1_sum, norm2_sum, head_sum = gains[:width], gains[width : 2 * width], gains[2 * width :]
    else:
        scatter = lambda value, axis: lax.psum_scatter(
            value, "dp", scatter_dimension=axis, tiled=True
        )
        whole = lambda value: jnp.concatenate([value[0], value[1]], 1)
        product, gate_grad, up_grad = (whole(wide[:, kind]) for kind in range(3))
        mixed = whole(mixed)
        grad_down = scatter(dot(product, out_grad, TN), 1)
        grad_gate = scatter(dot(second_normed, gate_grad, TN), 0)
        grad_up = scatter(dot(second_normed, up_grad, TN), 0)
        grad_out = scatter(dot(mixed, state_rows, TN), 1)
        grad_query, grad_key, grad_value, grad_gate_out = (
            scatter(dot(first_normed, kind_low, TN), 0)
            for kind_low in (whole(low[:, kind]) for kind in range(4))
        )
        beta_sum = scatter(grad_beta, 0)
        conv_total = lax.psum(conv_grad, "dp")
        norm1_sum, norm2_sum, head_sum = lax.psum(
            (norm1_part, norm2_part, head_part.reshape(-1)), ("dp", "tensor")
        )
    return (
        block_out.astype(BF16), input_grad, norm1_sum, grad_query, grad_key, grad_value, beta_sum,
        grad_gate_out, conv_total, head_sum, grad_out, norm2_sum, grad_gate, grad_up, grad_down,
    )


def solution(mesh):
    rows = P(("dp", "tensor"), None)
    columns = P(None, "tensor")
    in_specs = (
        rows, P(), columns, columns, columns, columns, columns, P(None, None, "tensor"), P(),
        P("tensor", None), P(), columns, columns, P("tensor", None), rows,
    )
    scattered = P("dp", "tensor")
    crossed = P("tensor", "dp")
    out_specs = (
        rows, rows, P(), scattered, scattered, scattered, scattered, scattered,
        P(None, None, "tensor"), P(), crossed, P(), scattered, scattered, crossed,
    )
    cubic = mesh.shape["dp"] == 16
    return jax.shard_map(
        functools.partial(local, cubic=cubic), mesh=mesh, in_specs=in_specs, out_specs=out_specs,
        check_vma=False,
    )
```

```python
import functools
import typing

import jax
import jax.numpy as jnp
from jax import lax
from jax.experimental import pallas as pl
from jax.experimental.pallas import tpu as pltpu
from jax.sharding import PartitionSpec as P

HEAD = 128
CONV = 4
PAIR = 2 * HEAD
GROUP = 4 * HEAD
F32 = jnp.float32
BF16 = jnp.bfloat16
norm_eps = 1e-06
unit_eps = 1e-06
VMEM_LIMIT = 56 * 1024 * 1024

NN = (((1,), (0,)), ((), ()))
NT = (((1,), (1,)), ((), ()))
TN = (((0,), (0,)), ((), ()))


def dot(left, right, dims=NN):
    return lax.dot_general(left, right, dims, preferred_element_type=F32)


def halves(value):
    high = value.astype(BF16)
    return high, (value - high.astype(F32)).astype(BF16)


def dot3(left, right, dims=NN):
    left_high, left_low = halves(left)
    right_high, right_low = halves(right)
    return (
        dot(left_high, right_low, dims) + dot(left_low, right_high, dims)
    ) + dot(left_high, right_high, dims)


def rows_down(value, shift):
    if shift == 0:
        return value
    row = lax.broadcasted_iota(jnp.int32, value.shape, 0)
    return jnp.where(row >= shift, pltpu.roll(value, shift, 0), 0.0)


def rows_up(value, shift):
    if shift == 0:
        return value
    rows = value.shape[0]
    row = lax.broadcasted_iota(jnp.int32, value.shape, 0)
    return jnp.where(row < rows - shift, pltpu.roll(value, rows - shift, 0), 0.0)


def causal_conv(value, taps):
    total = value * taps[CONV - 1 : CONV]
    for offset in range(CONV - 1):
        total = total + rows_down(value, CONV - 1 - offset) * taps[offset : offset + 1]
    return total


def sigmoid(value):
    return 1.0 / (1.0 + jnp.exp(-value))


def tri_mask(rows, strict):
    row = lax.broadcasted_iota(jnp.int32, (rows, rows), 0)
    col = lax.broadcasted_iota(jnp.int32, (rows, rows), 1)
    return row > col if strict else row >= col


def unit_lower_inverses(lowers):
    size = lowers[0].shape[0]
    row = lax.broadcasted_iota(jnp.int32, (size, size), 0)
    col = lax.broadcasted_iota(jnp.int32, (size, size), 1)
    eye = jnp.where(row == col, 1.0, 0.0)
    lows = [lower.astype(BF16) for lower in lowers]
    level, inverses = 0, None
    while (1 << level) < size:
        mask = (
            ((row >> (level + 1)) == (col >> (level + 1)))
            & (((row >> level) & 1) == 1)
            & (((col >> level) & 1) == 0)
        )
        if inverses is None:
            inverses = [eye - jnp.where(mask, lower, 0.0) for lower in lowers]
        else:
            known = [inverse.astype(BF16) for inverse in inverses]
            parts = [jnp.where(mask, low, jnp.zeros_like(low)) for low in lows]
            inner = [dot(part, each).astype(BF16) for part, each in zip(parts, known)]
            inverses = [
                inverse - dot(each, right)
                for inverse, each, right in zip(inverses, known, inner)
            ]
        level += 1
    lefts = [
        (eye - inverse - dot3(lower, inverse)).astype(BF16)
        for lower, inverse in zip(lowers, inverses)
    ]
    return [
        inverse + dot(inverse.astype(BF16), left) for inverse, left in zip(inverses, lefts)
    ]


def head_column(values, head):
    lane = lax.broadcasted_iota(jnp.int32, values.shape, 1)
    return jnp.sum(jnp.where(lane == head, values, 0.0), -1, keepdims=True)


def forward_group(
    step, xn_ref, wq_ref, wk_ref, wv_ref, wg_ref, wb_ref, conv_ref, gain_ref, wo_ref,
    mixed_ref, resid_ref, beta_ref, inv_ref, total,
):
    xn = xn_ref[...]
    rows = xn.shape[0]
    half = rows // 2

    @pl.when(step == 0)
    def _():
        beta_ref[...] = dot(xn, wb_ref[...], NT)
        total[...] = jnp.zeros_like(total)

    query_in = dot(xn, wq_ref[...])
    key_in = dot(xn, wk_ref[...])
    value_in = dot(xn, wv_ref[...])
    gate_in = dot(xn, wg_ref[...])
    for place, value in enumerate((query_in, key_in, value_in, gate_in)):
        resid_ref[place] = value
    beta_all = sigmoid(beta_ref[...])
    conv_q = causal_conv(query_in, conv_ref[0])
    conv_k = causal_conv(key_in, conv_ref[1])
    conv_v = causal_conv(value_in, conv_ref[2])
    query_act = conv_q * sigmoid(conv_q)
    key_act = conv_k * sigmoid(conv_k)
    value_act = conv_v * sigmoid(conv_v)
    gate_act = gate_in * sigmoid(gate_in)
    strict = tri_mask(rows, True)
    causal = tri_mask(rows, False)
    heads = []
    for head in range(GROUP // HEAD):
        cols = slice(head * HEAD, (head + 1) * HEAD)
        queries = query_act[:, cols]
        queries = queries * lax.rsqrt(jnp.sum(queries * queries, -1, keepdims=True) + unit_eps)
        queries = queries * HEAD**-0.5
        keys = key_act[:, cols]
        keys = keys * lax.rsqrt(jnp.sum(keys * keys, -1, keepdims=True) + unit_eps)
        beta = head_column(beta_all, GROUP // HEAD * step + head)
        lower = jnp.where(strict, dot3(keys, keys, NT) * beta, 0.0)
        scores = jnp.where(causal, dot3(queries, keys, NT), 0.0)
        heads.append((cols, lower, scores, value_act[:, cols] * beta))
    inverses = unit_lower_inverses(
        [lower[part, part] for _, lower, _, _ in heads for part in (slice(0, half), slice(half, rows))]
    )
    for head, (cols, lower, scores, weighted) in enumerate(heads):
        first, second = inverses[2 * head : 2 * head + 2]
        inv_ref[head, 0] = first
        inv_ref[head, 1] = second
        upper_u = dot3(first, weighted[:half])
        lower_u = dot3(second, weighted[half:] - dot3(lower[half:, :half], upper_u))
        updates = jnp.concatenate([upper_u, lower_u], 0)
        resid_ref[4, :, cols] = updates
        output = dot3(scores, updates)
        resid_ref[5, :, cols] = output
        normed = output * lax.rsqrt(jnp.mean(output * output, -1, keepdims=True) + norm_eps)
        mixed_ref[0, :, cols] = (normed * gain_ref[...] * gate_act[:, cols]).astype(BF16)
    total[...] += dot(mixed_ref[0], wo_ref[...])


def mixer_forward(
    xn_ref, wq_ref, wk_ref, wv_ref, wg_ref, wb_ref, conv_ref, gain_ref, wo_ref,
    mixed_ref, part_ref, resid_ref, beta_ref, inv_ref, total,
):
    step = pl.program_id(0)
    forward_group(
        step, xn_ref, wq_ref, wk_ref, wv_ref, wg_ref, wb_ref, conv_ref, gain_ref, wo_ref,
        mixed_ref, resid_ref, beta_ref, inv_ref, total,
    )

    @pl.when(step == pl.num_programs(0) - 1)
    def _():
        part_ref[...] = total[...].astype(BF16)


def call_mixer_forward(xn, wq, wk, wv, wg, wb, conv, gain, wo):
    rows, width = xn.shape
    cols = wq.shape[1]
    groups = cols // GROUP
    heads = wb.shape[0]
    whole = lambda *shape: pl.BlockSpec(shape, lambda i: (0,) * len(shape))
    weight = pl.BlockSpec((width, GROUP), lambda i: (0, i))
    return pl.pallas_call(
        mixer_forward,
        grid=(groups,),
        in_specs=[
            whole(rows, width), weight, weight, weight, weight, whole(heads, width),
            pl.BlockSpec((3, CONV, GROUP), lambda i: (0, 0, i)), whole(1, HEAD),
            pl.BlockSpec((GROUP, width), lambda i: (i, 0)),
        ],
        out_specs=[
            pl.BlockSpec((1, rows, GROUP), lambda i: (i // (groups // 2), 0, i % (groups // 2))),
            whole(rows, width), pl.BlockSpec((6, rows, GROUP), lambda i: (0, 0, i)), whole(rows, heads),
            pl.BlockSpec((GROUP // HEAD, 2, rows // 2, rows // 2), lambda i: (i, 0, 0, 0)),
        ],
        out_shape=[
            jax.ShapeDtypeStruct((2, rows, cols // 2), BF16),
            jax.ShapeDtypeStruct((rows, width), BF16),
            jax.ShapeDtypeStruct((6, rows, cols), F32), jax.ShapeDtypeStruct((rows, heads), F32),
            jax.ShapeDtypeStruct((heads, 2, rows // 2, rows // 2), F32),
        ],
        scratch_shapes=[pltpu.VMEM((rows, width), F32)],
        compiler_params=pltpu.CompilerParams(vmem_limit_bytes=VMEM_LIMIT),
        cost_estimate=pl.CostEstimate(
            flops=2 * rows * width * cols * 5 + 10**10, bytes_accessed=5 * width * cols * 2 + 10**7,
            transcendentals=0,
        ),
        name="mixer_forward",
    )(xn, wq, wk, wv, wg, wb, conv, gain, wo)


def silu_slope(value, sig):
    return sig * (1.0 + value * (1.0 - sig))


def backward_pair(
    step, steps, dh_ref, wq_ref, wk_ref, wv_ref, wg_ref, wb_ref, conv_ref, gain_ref, wo_ref,
    resid_ref, beta_ref, inv_ref, low_ref, bl_ref, dconv_ref, dgain_ref, total, beta_total,
):
    rows = dh_ref.shape[0]
    half = rows // 2

    @pl.when(step == 0)
    def _():
        total[...] = jnp.zeros_like(total)
        beta_total[...] = jnp.zeros_like(beta_total)
        dgain_ref[...] = jnp.zeros_like(dgain_ref)

    mixed_grad = dot(dh_ref[...], wo_ref[...], NT)
    query_in, key_in, value_in, gate_in = (resid_ref[place] for place in range(4))
    beta_all = sigmoid(beta_ref[...])
    lane = lax.broadcasted_iota(jnp.int32, beta_all.shape, 1)
    conv_q = causal_conv(query_in, conv_ref[0])
    conv_k = causal_conv(key_in, conv_ref[1])
    conv_v = causal_conv(value_in, conv_ref[2])
    sig_q, sig_k, sig_v = sigmoid(conv_q), sigmoid(conv_k), sigmoid(conv_v)
    sig_g = sigmoid(gate_in)
    query_act = conv_q * sig_q
    key_act = conv_k * sig_k
    value_act = conv_v * sig_v
    gate_act = gate_in * sig_g
    strict = tri_mask(rows, True)
    causal = tri_mask(rows, False)
    grads_q, grads_k, grads_v, grads_g = [], [], [], []
    gain = gain_ref[...]
    for head in range(2):
        cols = slice(head * HEAD, (head + 1) * HEAD)
        raw_q, raw_k, values = query_act[:, cols], key_act[:, cols], value_act[:, cols]
        scale_q = lax.rsqrt(jnp.sum(raw_q * raw_q, -1, keepdims=True) + unit_eps)
        scale_k = lax.rsqrt(jnp.sum(raw_k * raw_k, -1, keepdims=True) + unit_eps)
        queries = raw_q * scale_q * HEAD**-0.5
        keys = raw_k * scale_k
        beta = head_column(beta_all, 2 * step + head)
        updates = resid_ref[4, :, cols]
        output = resid_ref[5, :, cols]
        upstream = mixed_grad[:, cols]
        scale_o = lax.rsqrt(jnp.mean(output * output, -1, keepdims=True) + norm_eps)
        unit_out = output * scale_o
        grads_g.append(upstream * (unit_out * gain))
        d_normed = upstream * gate_act[:, cols]
        dgain_ref[...] += jnp.sum(d_normed * unit_out, 0, keepdims=True)
        d_unit = d_normed * gain
        d_output = scale_o * (d_unit - unit_out * jnp.mean(d_unit * unit_out, -1, keepdims=True))
        inner = dot3(keys, keys, NT)
        lower_21 = inner[half:, :half] * beta[half:]
        scores = jnp.where(causal, dot3(queries, keys, NT), 0.0)
        d_scores = jnp.where(causal, dot3(d_output, updates, NT), 0.0)
        d_updates = dot3(scores, d_output, TN)
        d_right_2 = dot3(inv_ref[head, 1], d_updates[half:], TN)
        d_right_1 = dot3(
            inv_ref[head, 0], d_updates[:half] - dot3(lower_21, d_right_2, TN), TN
        )
        d_right = jnp.concatenate([d_right_1, d_right_2], 0)
        d_lower = jnp.where(strict, -dot3(d_right, updates, NT), 0.0)
        d_beta = jnp.sum(d_lower * inner, -1, keepdims=True) + jnp.sum(
            d_right * values, -1, keepdims=True
        )
        grads_v.append(d_right * beta)
        d_inner = d_lower * beta
        d_keys = dot3(d_scores, queries, TN) + dot3(d_inner, keys) + dot3(d_inner, keys, TN)
        d_queries = dot3(d_scores, keys) * HEAD**-0.5
        grads_q.append(
            scale_q
            * (d_queries - raw_q * (scale_q * scale_q) * jnp.sum(d_queries * raw_q, -1, keepdims=True))
        )
        grads_k.append(
            scale_k
            * (d_keys - raw_k * (scale_k * scale_k) * jnp.sum(d_keys * raw_k, -1, keepdims=True))
        )
        d_beta_in = d_beta * beta * (1.0 - beta)
        beta_total[...] += jnp.where(lane == 2 * step + head, d_beta_in, 0.0)
    for kind, (grads, pre, conv, sig) in enumerate(
        (
            (grads_q, query_in, conv_q, sig_q),
            (grads_k, key_in, conv_k, sig_k),
            (grads_v, value_in, conv_v, sig_v),
        )
    ):
        d_conv = jnp.concatenate(grads, 1) * silu_slope(conv, sig)
        taps = conv_ref[kind]
        d_pre = d_conv * taps[CONV - 1 : CONV]
        for offset in range(CONV):
            shift = CONV - 1 - offset
            dconv_ref[kind, offset : offset + 1, :] = jnp.sum(
                d_conv * rows_down(pre, shift), 0, keepdims=True
            )
            if shift:
                d_pre = d_pre + rows_up(d_conv, shift) * taps[offset : offset + 1]
        low_ref[0, kind] = d_pre.astype(BF16)
    low_ref[0, 3] = (jnp.concatenate(grads_g, 1) * silu_slope(gate_in, sig_g)).astype(BF16)
    total[...] += (
        dot(low_ref[0, 0], wq_ref[...], NT)
        + dot(low_ref[0, 1], wk_ref[...], NT)
        + dot(low_ref[0, 2], wv_ref[...], NT)
        + dot(low_ref[0, 3], wg_ref[...], NT)
    )

    @pl.when(step == steps - 1)
    def _():
        bl_ref[...] = beta_total[...].astype(BF16)
        total[...] += dot(bl_ref[...], wb_ref[...])


def mixer_backward(
    dh_ref, wq_ref, wk_ref, wv_ref, wg_ref, wb_ref, conv_ref, gain_ref, wo_ref,
    resid_ref, beta_ref, inv_ref, low_ref, bl_ref, part_ref, dconv_ref, dgain_ref,
    total, beta_total,
):
    step, steps = pl.program_id(0), pl.num_programs(0)
    backward_pair(
        step, steps, dh_ref, wq_ref, wk_ref, wv_ref, wg_ref, wb_ref, conv_ref, gain_ref, wo_ref,
        resid_ref, beta_ref, inv_ref, low_ref, bl_ref, dconv_ref, dgain_ref, total, beta_total,
    )

    @pl.when(step == steps - 1)
    def _():
        part_ref[...] = total[...].astype(BF16)


def call_mixer_backward(dh, wq, wk, wv, wg, wb, conv, gain, wo, resid, beta, inv):
    rows, width = dh.shape
    cols = wq.shape[1]
    pairs = cols // PAIR
    heads = wb.shape[0]
    whole = lambda *shape: pl.BlockSpec(shape, lambda i: (0,) * len(shape))
    weight = pl.BlockSpec((width, PAIR), lambda i: (0, i))
    taps = pl.BlockSpec((3, CONV, PAIR), lambda i: (0, 0, i))
    return pl.pallas_call(
        mixer_backward,
        grid=(pairs,),
        in_specs=[
            whole(rows, width), weight, weight, weight, weight, whole(heads, width), taps,
            whole(1, HEAD), pl.BlockSpec((PAIR, width), lambda i: (i, 0)),
            pl.BlockSpec((6, rows, PAIR), lambda i: (0, 0, i)), whole(rows, heads),
            pl.BlockSpec((2, 2, rows // 2, rows // 2), lambda i: (i, 0, 0, 0)),
        ],
        out_specs=[
            pl.BlockSpec((1, 4, rows, PAIR), lambda i: (i // (pairs // 2), 0, 0, i % (pairs // 2))),
            whole(rows, heads), whole(rows, width), taps, whole(1, HEAD),
        ],
        out_shape=[
            jax.ShapeDtypeStruct((2, 4, rows, cols // 2), BF16),
            jax.ShapeDtypeStruct((rows, heads), BF16),
            jax.ShapeDtypeStruct((rows, width), BF16), jax.ShapeDtypeStruct(conv.shape, F32),
            jax.ShapeDtypeStruct((1, HEAD), F32),
        ],
        scratch_shapes=[pltpu.VMEM((rows, width), F32), pltpu.VMEM((rows, heads), F32)],
        compiler_params=pltpu.CompilerParams(vmem_limit_bytes=VMEM_LIMIT),
        cost_estimate=pl.CostEstimate(
            flops=2 * rows * width * cols * 5 + 2 * 10**10,
            bytes_accessed=5 * width * cols * 2 + 10**7,
            transcendentals=0,
        ),
        name="mixer_backward",
    )(dh, wq, wk, wv, wg, wb, conv, gain, wo, resid, beta, inv)


def mlp_copies(index, slot, wg_ref, wu_ref, wd_ref, wg_buf, wu_buf, wd_buf, sems):
    hidden = wg_ref.shape[1] // 2
    for part in range(2):
        start = pl.multiple_of(part * hidden + index * HEAD, HEAD)
        lanes = pl.ds(part * HEAD, HEAD)
        yield pltpu.make_async_copy(
            wg_ref.at[:, pl.ds(start, HEAD)], wg_buf.at[slot, :, lanes], sems.at[slot, part]
        )
        yield pltpu.make_async_copy(
            wu_ref.at[:, pl.ds(start, HEAD)], wu_buf.at[slot, :, lanes], sems.at[slot, 2 + part]
        )
        yield pltpu.make_async_copy(
            wd_ref.at[pl.ds(start, HEAD), :], wd_buf.at[slot, lanes, :], sems.at[slot, 4 + part]
        )


def mlp_tile(step, steps, yn_ref, dy_ref, weights, low_store, down_total, back_total):
    wg_ref, wu_ref, wd_ref, wg_buf, wu_buf, wd_buf, sems = weights
    slot = lax.rem(step, 2)

    @pl.when(step == 0)
    def _():
        down_total[...] = jnp.zeros_like(down_total)
        back_total[...] = jnp.zeros_like(back_total)

    @pl.when(step + 1 < steps)
    def _():
        for copy in mlp_copies(step + 1, 1 - slot, *weights):
            copy.start()

    for copy in mlp_copies(step, slot, *weights):
        copy.wait()
    yn, dy = yn_ref[...], dy_ref[...]
    w_gate, w_up, w_down = wg_buf[slot], wu_buf[slot], wd_buf[slot]
    gate = dot(yn, w_gate)
    up = dot(yn, w_up)
    d_product = dot(dy, w_down, NT)
    sig = sigmoid(gate)
    act = gate * sig
    product = (act * up).astype(BF16)
    gate_grad = (d_product * up * silu_slope(gate, sig)).astype(BF16)
    up_grad = (d_product * act).astype(BF16)
    down_total[...] += dot(product, w_down)
    back_total[...] += dot(gate_grad, w_gate, NT) + dot(up_grad, w_up, NT)
    for kind, value in enumerate((product, gate_grad, up_grad)):
        low_store(0, kind, value[:, :HEAD])
        low_store(1, kind, value[:, HEAD:])


def mlp_kernel(
    yn_ref, dy_ref, wg_ref, wu_ref, wd_ref, low_ref, down_ref, back_ref,
    wg_buf, wu_buf, wd_buf, down_total, back_total, sems,
):
    step, steps = pl.program_id(0), pl.num_programs(0)
    weights = (wg_ref, wu_ref, wd_ref, wg_buf, wu_buf, wd_buf, sems)

    @pl.when(step == 0)
    def _():
        for copy in mlp_copies(0, 0, *weights):
            copy.start()

    def low_store(half, kind, value):
        low_ref[half, kind] = value

    mlp_tile(step, steps, yn_ref, dy_ref, weights, low_store, down_total, back_total)

    @pl.when(step == steps - 1)
    def _():
        down_ref[...] = down_total[...].astype(BF16)
        back_ref[...] = back_total[...].astype(BF16)


def call_mlp(yn, dy, w_gate, w_up, w_down):
    rows, width = yn.shape
    hidden = w_gate.shape[1] // 2
    whole = lambda *shape: pl.BlockSpec(shape, lambda i: (0,) * len(shape))
    anywhere = pl.BlockSpec(memory_space=pl.ANY)
    tile = pl.BlockSpec((2, 3, rows, HEAD), lambda i: (0, 0, 0, i))
    return pl.pallas_call(
        mlp_kernel,
        grid=(hidden // HEAD,),
        in_specs=[whole(rows, width), whole(rows, width), anywhere, anywhere, anywhere],
        out_specs=[tile, whole(rows, width), whole(rows, width)],
        out_shape=[
            jax.ShapeDtypeStruct((2, 3, rows, hidden), BF16),
            jax.ShapeDtypeStruct((rows, width), BF16),
            jax.ShapeDtypeStruct((rows, width), BF16),
        ],
        scratch_shapes=[
            pltpu.VMEM((2, width, PAIR), BF16), pltpu.VMEM((2, width, PAIR), BF16),
            pltpu.VMEM((2, PAIR, width), BF16), pltpu.VMEM((rows, width), F32),
            pltpu.VMEM((rows, width), F32), pltpu.SemaphoreType.DMA((2, 6)),
        ],
        compiler_params=pltpu.CompilerParams(vmem_limit_bytes=VMEM_LIMIT),
        cost_estimate=pl.CostEstimate(
            flops=12 * rows * width * w_gate.shape[1], bytes_accessed=6 * width * w_gate.shape[1],
            transcendentals=0,
        ),
        name="mlp",
    )(yn, dy, w_gate, w_up, w_down)


def norm_back(upstream, inputs, scale_rows, gain_row):
    scaled_grad = upstream * gain_row
    return scale_rows * (
        scaled_grad
        - inputs * scale_rows * scale_rows * jnp.mean(scaled_grad * inputs, -1, keepdims=True)
    )


def take(value, axis, index):
    return lax.dynamic_index_in_dim(value, index, axis, keepdims=False)


def sibling(value):
    return lax.ppermute(value, "tensor", [(0, 1), (1, 0)])


def both_rows(mine, other, core):
    axis = mine.ndim - 2
    return jnp.where(
        core == 0, jnp.concatenate([mine, other], axis), jnp.concatenate([other, mine], axis)
    )


def swap_sum(partial, core):
    parts = partial.reshape(2, -1, partial.shape[-1])
    received = sibling(take(parts, 0, 1 - core))
    return take(parts, 0, core).astype(F32) + received.astype(F32)


BIT_X, BIT_Y, BIT_ZA, BIT_ZB = 1, 2, 4, 8
GATHER_1, GATHER_2, REDUCE_1 = BIT_X, BIT_ZA, BIT_Y
BITS = (1, 2, 4, 8)
SMALL_BITS = (8, 4, 2, 1)
CHIPS = 16
MESH = pl.DeviceIdType.MESH
KINDS = ((0, 0, 0), (0, 1, 2), (0, 2, 2), (1, 0, 3), (1, 1, 1), (1, 2, 1), (1, 3, 1), (1, 4, 1))
COUNT = len(KINDS)
CROSSED = (0, 3)
LEFT_SLOT = (0, 0, 2, 1)
SMALL_ROWS = 24
SCHEDULE = (
    200, 121, 40,
    201, 230, 231, 140,
    50, 300, 210, 150,
    60, 211, 700, 160, 800,
    70, 301, 170, 701,
    330, 600, 730, 331,
    731, 601, 630, 220, 800,
    400, 631, 221, 310,
    430, 500, 530, 610,
    311, 710, 250, 251,
    611, 711, 320, 410,
    620, 321, 240, 720,
    621, 241, 350, 510, 800,
    721, 351, 270, 271,
    650, 651, 340, 420,
    640, 341, 260, 641,
    261, 750, 370, 751, 800,
    520, 371, 670, 740,
    450, 671, 360, 741, 800,
    660, 361, 550, 661,
    440, 770, 771, 540,
    470, 760, 570, 761,
    460, 560,
)


def block_place(block):
    bit = lambda mask: int((block & mask) != 0)
    return bit(GATHER_1), bit(REDUCE_1) * 4 + bit(BIT_ZB) * 2 + bit(GATHER_2)


class Place:
    def __init__(self, tokens):
        self.chip, self.core = lax.axis_index("dp"), lax.axis_index("tensor")
        self.bit = {mask: lax.rem(self.chip // mask, 2) for mask in BITS}
        step = {mask: mask * (1 - 2 * self.bit[mask]) for mask in BITS}
        self.to = {mask: (self.chip + step[mask], self.core) for mask in BITS}
        self.mirror = (self.chip + step[BIT_ZA] + step[BIT_ZB], self.core)
        self.near = (self.chip, 1 - self.core)
        self.own_rows = pl.ds(pl.multiple_of(self.core * tokens, tokens), tokens)
        self.other_rows = pl.ds(pl.multiple_of((1 - self.core) * tokens, tokens), tokens)
        self.tokens = tokens

    def greet(self, partners):
        barrier = pltpu.get_barrier_semaphore()
        for target in partners:
            pl.semaphore_signal(barrier, inc=1, device_id=target, device_id_type=MESH)
        pl.semaphore_wait(barrier, len(partners))


def remote_pair(source, target, send_sem, recv_sem, device):
    return pltpu.make_async_remote_copy(
        src_ref=source, dst_ref=target, send_sem=send_sem, recv_sem=recv_sem,
        device_id=device, device_id_type=MESH,
    )


def remote(source, target, sems, index, device):
    return remote_pair(source, target, sems.at[(0, *index)], sems.at[(1, *index)], device)


class Lefts:
    def __init__(self, place, own, landed, sems, local_sems):
        self.place, self.own, self.landed, self.sems, self.local = place, own, landed, sems, local_sems

    def rows(self, a, piece):
        tokens = self.place.tokens
        start = pl.multiple_of((2 * piece + self.place.core) * tokens, tokens)
        return self.landed.at[a, pl.ds(start, tokens), :]

    def copy(self, a, name):
        place, own, sems = self.place, self.own, self.sems
        half = place.bit[GATHER_1]
        if name == "one":
            return remote(own.at[a, 1 - half], self.rows(a, 1), sems, (a, 0), place.to[GATHER_1])
        if name == "two":
            return remote(own.at[a, half], self.rows(a, 2), sems, (a, 1), place.to[GATHER_2])
        if name == "far":
            return remote(self.rows(a, 1), self.rows(a, 3), sems, (a, 2), place.to[GATHER_2])
        if name == 0:
            return remote(own.at[a, half], self.rows(a, 0), sems, (a, 3), place.near)
        return remote(self.rows(a, name), self.rows(a, name), sems, (a, 3 + name), place.near)

    def own_copy(self, a):
        half = self.place.bit[GATHER_1]
        return pltpu.make_async_copy(self.own.at[a, half], self.rows(a, 0), self.local.at[a])

    def start(self, a, natural):
        for block in range(CHIPS):
            half, place = block_place(block)
            self.own[a, half, :, place * HEAD : (place + 1) * HEAD] = natural[
                :, block * HEAD : (block + 1) * HEAD
            ]
        for name in ("one", "two", 0):
            self.copy(a, name).start()
        self.own_copy(a).start()

    def middle(self, a):
        self.copy(a, "one").wait_recv()
        self.copy(a, "far").start()
        self.copy(a, 1).start()
        self.copy(a, "two").wait_recv()
        self.copy(a, 2).start()

    def far(self, a):
        self.copy(a, "far").wait_recv()
        self.copy(a, 3).start()

    def arrived(self, a):
        for piece in range(4):
            self.copy(a, piece).wait_recv()
        self.own_copy(a).wait()

    def sent(self, a):
        for name in ("one", "two", "far", 0, 1, 2, 3):
            self.copy(a, name).wait_send()


def front_kernel(
    tokens_ref, cot_ref, wq_ref, wk_ref, wv_ref, wg_ref, wb_ref, conv_ref, gain_ref, wo_ref,
    norm1_ref, norm2_ref,
    mixed_ref, resid_ref, beta_ref, inv_ref, hidden_ref, second_ref, xn_out, dy_out, yn_out,
    landed,
    total, xn, dy, yn, own, stage, part, lsem, qsem, csem,
):
    step, steps = pl.program_id(0), pl.num_programs(0)
    place = Place(tokens_ref.shape[0])
    own_rows, other_rows = place.own_rows, place.other_rows
    lefts = Lefts(place, own, landed, lsem, csem)

    def row_copy(index):
        source = stage if index == 2 else (xn, dy, None, yn)[index].at[own_rows, :]
        target = part if index == 2 else source
        return remote(source, target, qsem, (index,), place.near)

    def out_copy(index):
        source, target = ((xn, xn_out), (dy, dy_out), (yn, yn_out))[index]
        return pltpu.make_async_copy(source, target, csem.at[2 + index])

    @pl.when(step == 0)
    def _():
        place.greet((place.to[GATHER_1], place.to[GATHER_2], place.near))
        inputs = tokens_ref[...].astype(F32)
        scale = lax.rsqrt(jnp.mean(inputs * inputs, -1, keepdims=True) + norm_eps)
        xn[own_rows, :] = (inputs * scale * norm1_ref[...]).astype(BF16)
        row_copy(0).start()
        dy[own_rows, :] = cot_ref[...]
        row_copy(1).start()
        lefts.start(0, cot_ref)
        lefts.start(1, xn[own_rows, :])
        row_copy(0).wait()
        out_copy(0).start()

    forward_group(
        step, xn, wq_ref, wk_ref, wv_ref, wg_ref, wb_ref, conv_ref, gain_ref, wo_ref,
        mixed_ref, resid_ref, beta_ref, inv_ref, total,
    )

    @pl.when(step == 0)
    def _():
        row_copy(1).wait()
        out_copy(1).start()
        lefts.middle(0)
        lefts.middle(1)

    @pl.when(step == steps - 1)
    def _():
        stage[...] = total[other_rows, :].astype(BF16)
        row_copy(2).start()
        lefts.far(0)
        lefts.far(1)
        hidden = tokens_ref[...].astype(F32) + total[own_rows, :]
        row_copy(2).wait()
        hidden = hidden + part[...].astype(F32)
        hidden_ref[...] = hidden
        scale = lax.rsqrt(jnp.mean(hidden * hidden, -1, keepdims=True) + norm_eps)
        second = (hidden * scale * norm2_ref[...]).astype(BF16)
        yn[own_rows, :] = second
        row_copy(3).start()
        second_ref[...] = second
        for a in range(2):
            lefts.arrived(a)
            lefts.sent(a)
        row_copy(3).wait()
        out_copy(2).start()
        for index in range(3):
            out_copy(index).wait()


def call_front(tokens, cot, wq, wk, wv, wg, wb, conv, gain, wo, norm1, norm2):
    count, width = tokens.shape
    rows, cols, heads = 2 * count, wq.shape[1], wb.shape[0]
    groups = cols // GROUP
    sds = jax.ShapeDtypeStruct
    whole = lambda *shape: pl.BlockSpec(shape, lambda i: (0,) * len(shape))
    weight = pl.BlockSpec((width, GROUP), lambda i: (0, i))
    anywhere = pl.BlockSpec(memory_space=pl.ANY)
    sem = pltpu.SemaphoreType.DMA
    low = lambda *shape: pltpu.VMEM(shape, BF16)
    return pl.pallas_call(
        front_kernel,
        grid=(groups,),
        in_specs=[
            whole(count, width), whole(count, width), weight, weight, weight, weight,
            whole(heads, width), pl.BlockSpec((3, CONV, GROUP), lambda i: (0, 0, i)),
            whole(1, HEAD), pl.BlockSpec((GROUP, width), lambda i: (i, 0)), whole(1, width),
            whole(1, width),
        ],
        out_specs=[
            pl.BlockSpec((1, rows, GROUP), lambda i: (i // (groups // 2), 0, i % (groups // 2))),
            pl.BlockSpec((6, rows, GROUP), lambda i: (0, 0, i)), whole(rows, heads),
            pl.BlockSpec((GROUP // HEAD, 2, count, count), lambda i: (i, 0, 0, 0)),
            whole(count, width), whole(count, width), anywhere, anywhere, anywhere, anywhere,
        ],
        out_shape=[
            sds((2, rows, cols // 2), BF16), sds((6, rows, cols), F32), sds((rows, heads), F32),
            sds((heads, 2, count, count), F32), sds((count, width), F32),
            sds((count, width), BF16), sds((rows, width), BF16), sds((rows, width), BF16),
            sds((rows, width), BF16), sds((2, 8 * count, width // 2), BF16),
        ],
        scratch_shapes=[
            pltpu.VMEM((rows, width), F32), low(rows, width), low(rows, width), low(rows, width),
            low(2, 2, count, width // 2), low(count, width), low(count, width),
            sem((2, 2, 7)), sem((2, 4)), sem((5,)),
        ],
        compiler_params=pltpu.CompilerParams(
            vmem_limit_bytes=VMEM_LIMIT, collective_id=2, has_side_effects=True
        ),
        cost_estimate=pl.CostEstimate(flops=2 * 10**10, bytes_accessed=4 * 10**7, transcendentals=0),
        name="front",
    )(tokens, cot, wq, wk, wv, wg, wb, conv, gain, wo, norm1, norm2)


class Refs(typing.NamedTuple):
    hidden: typing.Any
    tokens: typing.Any
    cot: typing.Any
    second: typing.Any
    wb: typing.Any
    conv: typing.Any
    gain: typing.Any
    beta: typing.Any
    norm1: typing.Any
    norm2: typing.Any
    early: typing.Any
    yn: typing.Any
    dy: typing.Any
    xn: typing.Any
    wg: typing.Any
    wu: typing.Any
    wd: typing.Any
    wq: typing.Any
    wk: typing.Any
    wv: typing.Any
    wgo: typing.Any
    wo: typing.Any
    mixed: typing.Any
    resid: typing.Any
    inv: typing.Any
    out: typing.Any
    ingrad: typing.Any
    smalls: typing.Any
    lefts: typing.Any
    gws: typing.Any
    gns: typing.Any
    lows: typing.Any
    paw: typing.Any
    pan: typing.Any
    pbw: typing.Any
    pbn: typing.Any
    own: typing.Any
    wide: typing.Any
    r1w: typing.Any
    r1n: typing.Any
    r2w: typing.Any
    r2n: typing.Any
    rfw: typing.Any
    rfn: typing.Any
    rows: typing.Any
    dh: typing.Any
    state: typing.Any
    small: typing.Any
    smallr: typing.Any
    dconv: typing.Any
    dgain: typing.Any
    bl: typing.Any
    lsem: typing.Any
    rsem: typing.Any
    csem: typing.Any
    qsem: typing.Any
    ssem: typing.Any
    zsem: typing.Any
    fsem: typing.Any
    psem: typing.Any
    msem: typing.Any
    osem: typing.Any


def block_kernel(*refs):
    outs = refs[28 : 28 + COUNT]
    r = Refs(*refs[:28], *refs[28 + COUNT :])
    own, wide, dh, state, small = r.own, r.wide, r.dh, r.state, r.small
    recv1, recv2, recvf = (r.r1w, r.r1n), (r.r2w, r.r2n), (r.rfw, r.rfn)
    landed = (r.gws, r.gns)
    relay = ((r.paw, r.pan), (r.pbw, r.pbn))
    tokens, width = r.second.shape
    place = Place(tokens)
    bit, to, near = place.bit, place.to, place.near
    own_rows, other_rows = place.own_rows, place.other_rows
    quarter, eighth = width // 8, width // 16
    half1, half2 = bit[GATHER_1], bit[GATHER_2]
    mine1, mine2 = bit[REDUCE_1], bit[BIT_ZB]
    end = bit[BIT_ZA] == bit[BIT_ZB]
    inner = bit[BIT_ZA] != bit[BIT_ZB]
    place.greet((*to.values(), place.mirror, near))
    lefts = Lefts(place, own, r.lefts, r.lsem, r.csem)

    def source(kind, half):
        group, place, _ = KINDS[kind]
        if group == 0:
            return wide.at[half, place]
        return r.mixed.at[half] if place == 0 else r.lows.at[half, place - 1]

    def right_landed(kind, piece):
        group, place, _ = KINDS[kind]
        return landed[group].at[place, piece - 1]

    split = wide.shape[-1] // HEAD // 2 * HEAD + HEAD

    def parts(kind):
        return 2 if KINDS[kind][0] == 0 else 1

    def right_copy(kind, name, part):
        columns = slice(None)
        if parts(kind) == 2:
            columns = slice(0, split) if part == 0 else slice(split, wide.shape[-1])
        view = lambda ref: ref.at[:, columns]
        if name == "one":
            return remote(
                view(source(kind, half2)), view(right_landed(kind, 1)), r.rsem, (kind, 0, part),
                to[GATHER_1],
            )
        if name == "two":
            return remote(
                view(source(kind, 1 - half2)), view(right_landed(kind, 2)), r.rsem,
                (kind, 1, part), to[GATHER_2],
            )
        return remote(
            view(right_landed(kind, 2)), view(right_landed(kind, 3)), r.rsem, (kind, 2, part),
            to[GATHER_1],
        )

    def one(kind, part):
        right_copy(kind, "one", part).start()

    def two(kind, part):
        right_copy(kind, "two", part).start()

    def far(kind, part):
        right_copy(kind, "two", part).wait_recv()
        right_copy(kind, "far", part).start()

    def row_copy(index, source_ref):
        target = dh.at[own_rows, :] if index == 3 else r.rows.at[index]
        return remote(source_ref, target, r.qsem, (index,), near)

    def small_copy(stage):
        if stage == len(BITS):
            return remote(
                small.at[SMALL_ROWS - 8 :, :], r.smallr.at[stage, :8, :], r.psem, (stage,), near
            )
        return remote(small, r.smallr.at[stage], r.psem, (stage,), to[SMALL_BITS[stage]])

    def small_sum(stage):
        small_copy(stage).wait()
        if stage == len(BITS):
            small[SMALL_ROWS - 8 :, :] += r.smallr[stage, :8, :]
        else:
            small[...] += r.smallr[stage]

    steps = wide.shape[-1] // HEAD
    pairs = r.wq.shape[1] // PAIR

    def mixer_copies(pair, slot, wbuf, wobuf, resid_buf, inv_buf):
        columns = pl.ds(pl.multiple_of(pair * PAIR, PAIR), PAIR)
        sems = r.msem
        for index, weight in enumerate((r.wq, r.wk, r.wv, r.wgo)):
            yield pltpu.make_async_copy(
                weight.at[:, columns], wbuf.at[slot, index], sems.at[slot, index]
            )
        yield pltpu.make_async_copy(r.wo.at[columns, :], wobuf.at[slot], sems.at[slot, 4])
        yield pltpu.make_async_copy(
            r.resid.at[:, :, columns], resid_buf.at[slot], sems.at[slot, 5]
        )
        yield pltpu.make_async_copy(
            r.inv.at[pl.ds(2 * pair, 2)], inv_buf.at[slot], sems.at[slot, 6]
        )

    def mlp_phase(prefetch, yn, dy, wg_buf, wu_buf, wd_buf, down_total, back_total, stage):
        weights = (r.wg, r.wu, r.wd, wg_buf, wu_buf, wd_buf, r.msem)
        loads = [
            pltpu.make_async_copy(r.yn, yn, r.csem.at[4]),
            pltpu.make_async_copy(r.dy, dy, r.csem.at[5]),
        ]
        for copy in (*loads, *mlp_copies(0, 0, *weights)):
            copy.start()
        lefts.start(0, r.second)
        two(3, 0)
        one(3, 0)
        for copy in loads:
            copy.wait()

        def five():
            far(3, 0)
            two(0, 0)
            one(0, 0)

        events = {2: lambda: lefts.middle(0), split // HEAD - 1: five, 8: lambda: lefts.far(0)}

        @pl.loop(0, steps)
        def _(step):
            columns = pl.ds(pl.multiple_of(step * HEAD, HEAD), HEAD)

            def low_store(half, kind, value):
                wide[half, kind, :, columns] = value

            mlp_tile(step, steps, yn, dy, weights, low_store, down_total, back_total)
            for when, event in events.items():
                pl.when(step == when)(event)

        far(0, 0)
        for kind, part in ((0, 1), (1, 0), (1, 1), (2, 0), (2, 1)):
            two(kind, part)
        one(0, 1)
        prefetch()
        for index, total in enumerate((down_total, back_total)):
            stage[index] = total[other_rows, :].astype(BF16)
            row_copy(index, stage.at[index]).start()
        for index in range(2):
            row_copy(index, stage.at[index]).wait()
        hidden = r.hidden[...]
        r.out[...] = (hidden + down_total[own_rows, :] + r.rows[0].astype(F32)).astype(BF16)
        second_grad = back_total[own_rows, :] + r.rows[1].astype(F32)
        scale = lax.rsqrt(jnp.mean(hidden * hidden, -1, keepdims=True) + norm_eps)
        small[...] = jnp.zeros_like(small)
        small[17:18, :] = jnp.sum(second_grad * hidden * scale, 0, keepdims=True)
        grad = r.cot[...].astype(F32) + norm_back(second_grad, hidden, scale, r.norm2[...])
        state[...] = grad
        dh[own_rows, :] = grad.astype(BF16)
        row_copy(3, dh.at[own_rows, :]).start()
        lefts.start(1, dh[own_rows, :])
        row_copy(3, dh.at[own_rows, :]).wait()

    def mixer_phase(buffers, xn, total, beta_total, low_stage, stage):
        wbuf, wobuf, resid_buf, inv_buf = buffers
        load = pltpu.make_async_copy(r.xn, xn, r.csem.at[6])
        load.start()

        def low_copy(pair, slot):
            target = r.lows.at[
                pair // 2, :, :, pl.ds(pl.multiple_of(lax.rem(pair, 2) * PAIR, PAIR), PAIR)
            ]
            return pltpu.make_async_copy(low_stage.at[slot, 0], target, r.osem.at[slot])

        def event_0():
            far(0, 1)
            one(1, 0)

        def event_1():
            far(1, 0)
            one(1, 1)

        def event_2():
            lefts.middle(1)
            far(1, 1)
            one(2, 0)

        def event_3():
            far(2, 0)
            one(2, 1)
            lefts.far(1)

        @pl.loop(0, pairs)
        def _(pair):
            slot = lax.rem(pair, 2)

            @pl.when(pair + 1 < pairs)
            def _():
                for copy in mixer_copies(pair + 1, 1 - slot, *buffers):
                    copy.start()

            for copy in mixer_copies(pair, slot, *buffers):
                copy.wait()

            @pl.when(pair >= 2)
            def _():
                low_copy(pair - 2, slot).wait()

            lanes = pl.ds(pl.multiple_of(pair * PAIR, PAIR), PAIR)
            backward_pair(
                pair, pairs, dh, *(wbuf.at[slot, index] for index in range(4)), r.wb,
                r.conv.at[:, :, lanes], r.gain, wobuf.at[slot], resid_buf.at[slot],
                r.beta, inv_buf.at[slot], low_stage.at[slot], r.bl,
                r.dconv.at[:, :, lanes], r.dgain, total, beta_total,
            )
            low_copy(pair, slot).start()
            for when, event in enumerate((event_0, event_1, event_2, event_3)):
                pl.when(pair == when)(event)

        for pair in (pairs - 2, pairs - 1):
            low_copy(pair, pair % 2).wait()
        stage[...] = total[other_rows, :].astype(BF16)
        row_copy(2, stage).start()
        load.wait()
        small[0:8, :] = dot(r.bl[...], xn[...], TN)
        for kind in range(3):
            for offset in range(CONV):
                row = kind * CONV + offset
                lanes = slice(0, width // 2) if row < 8 else slice(width // 2, width)
                small[8 + row % 8 : 9 + row % 8, lanes] = r.dconv[kind, offset : offset + 1, :]
        small[18:19, :HEAD] = r.dgain[...]
        row_copy(2, stage).wait()
        first_grad = total[own_rows, :] + r.rows[2].astype(F32)
        inputs = r.tokens[...].astype(F32)
        scale = lax.rsqrt(jnp.mean(inputs * inputs, -1, keepdims=True) + norm_eps)
        small[16:17, :] = jnp.sum(first_grad * inputs * scale, 0, keepdims=True)
        small_copy(0).start()
        for kind in range(4, COUNT):
            two(kind, 0)
        state[...] += norm_back(first_grad, inputs, scale, r.norm1[...])
        pltpu.make_async_copy(state, r.ingrad, r.csem.at[7]).start()

    def scoped_mixer(wbuf, wobuf, resid_buf, inv_buf):
        buffers = (wbuf, wobuf, resid_buf, inv_buf)

        def prefetch():
            for copy in mixer_copies(0, 0, *buffers):
                copy.start()

        rows = 2 * tokens
        pl.run_scoped(
            functools.partial(mlp_phase, prefetch),
            pltpu.VMEM((rows, width), BF16), pltpu.VMEM((rows, width), BF16),
            pltpu.VMEM((2, width, PAIR), BF16), pltpu.VMEM((2, width, PAIR), BF16),
            pltpu.VMEM((2, PAIR, width), BF16), pltpu.VMEM((rows, width), F32),
            pltpu.VMEM((rows, width), F32), pltpu.VMEM((2, tokens, width), BF16),
        )
        pl.run_scoped(
            functools.partial(mixer_phase, buffers),
            pltpu.VMEM((rows, width), BF16), pltpu.VMEM((rows, width), F32),
            pltpu.VMEM(r.beta.shape, F32), pltpu.VMEM((2, 1, 4, rows, PAIR), BF16),
            pltpu.VMEM((tokens, width), BF16),
        )

    pl.run_scoped(
        scoped_mixer, pltpu.VMEM((2, 4, width, PAIR), BF16), pltpu.VMEM((2, PAIR, width), BF16),
        pltpu.VMEM((2, 6, 2 * tokens, PAIR), F32), pltpu.VMEM((2, 2, 2, tokens, tokens), F32),
    )

    def sums_phase(left, gw, gn, s1w, s1n, s2w, s2n, sfw, sfn, ow, on, cw, cn):
        right, send1 = (gw, gn), (s1w, s1n)
        send2, sendf, out_buf, cross_buf = (s2w, s2n), (sfw, sfn), (ow, on), (cw, cn)

        def left_load(a):
            from_ref = r.early.at[a] if a < 2 else r.lefts.at[a - 2]
            return pltpu.make_async_copy(
                from_ref, left.at[LEFT_SLOT[a]], r.csem.at[8 + LEFT_SLOT[a]]
            )

        def right_loads(kind):
            group = KINDS[kind][0]
            rows = 2 * tokens
            for piece in range(4):
                yield pltpu.make_async_copy(
                    right_landed(kind, piece) if piece else source(kind, half2),
                    right[group].at[kind % 2, piece * rows : (piece + 1) * rows, :],
                    r.csem.at[11 + piece],
                )

        in_slot, right_slot = {}, {}

        def load(kind):
            group, _, a = KINDS[kind]
            right_slot[group, kind % 2] = kind
            fresh = in_slot.get(LEFT_SLOT[a]) != a
            if fresh:
                in_slot[LEFT_SLOT[a]] = a
                if a >= 2:
                    lefts.arrived(a - 2)
                left_load(a).start()
            for part in range(parts(kind)):
                right_copy(kind, "one", part).wait_recv()
                right_copy(kind, "far", part).wait_recv()
            for copy in right_loads(kind):
                copy.start()
            if fresh:
                left_load(a).wait()
            for copy in right_loads(kind):
                copy.wait()

        def product(kind, start):
            group, _, a = KINDS[kind]
            assert in_slot[LEFT_SLOT[a]] == a and right_slot[group, kind % 2] == kind
            lanes = pl.ds(pl.multiple_of(start, quarter), quarter)
            return dot(left[LEFT_SLOT[a], :, lanes], right[group][kind % 2], TN)

        def rows_of(which):
            return pl.ds(pl.multiple_of(which * quarter, quarter), quarter)

        last, stored = {}, {}

        def slot_free(kind, stage, wait):
            key = (KINDS[kind][0], kind % 2, stage)
            if key in last:
                wait(last[key])
            last[key] = kind

        def first_copy(kind, part):
            group, at, _ = KINDS[kind]
            rows = rows_of(1 - mine2 if part == 0 else mine2)
            return remote(
                send1[group].at[kind % 2, rows, :], recv1[group].at[at, rows, :], r.ssem,
                (kind, part), to[REDUCE_1],
            )

        def first_sent(kind):
            for part in range(2):
                first_copy(kind, part).wait_send()

        def first_sums(kind, part):
            if part == 0:
                load(kind)
                slot_free(kind, 0, first_sent)
            group = KINDS[kind][0]
            which = 1 - mine2 if part == 0 else mine2
            send1[group][kind % 2, rows_of(which), :] = product(
                kind, (1 - mine1) * 2 * quarter + which * quarter
            ).astype(BF16)
            first_copy(kind, part).start()

        def second_copy(kind, part, from_end):
            group, at, _ = KINDS[kind]
            rows = slice(part * eighth, (part + 1) * eighth)
            return remote_pair(
                send2[group].at[kind % 2, rows, :],
                relay[0 if from_end else 1][group].at[at, rows, :],
                r.zsem.at[0, kind, part], r.zsem.at[1 if from_end else 2, kind, part],
                to[BIT_ZA] if from_end else place.mirror,
            )

        def second_sent(kind):
            for part in range(2):
                second_copy(kind, part, True).wait_send()

        def pass_copy(kind, part, which):
            group, at, _ = KINDS[kind]
            rows = slice(part * eighth, (part + 1) * eighth)
            return remote_pair(
                relay[which][group].at[at, rows, :], recv2[group].at[at, rows, :],
                r.fsem.at[which, kind, part], r.fsem.at[2, kind, part],
                place.mirror if which == 0 else to[BIT_ZA],
            )

        def pass_on(kind, part, which):
            @pl.when(inner)
            def _():
                second_copy(kind, part, which == 0).wait_recv()
                pass_copy(kind, part, which).start()

        def second_sums(kind, part):
            group, at, _ = KINDS[kind]
            which = mine2 if part else 1 - mine2
            first_copy(kind, part).wait_recv()
            total = product(kind, mine1 * 2 * quarter + which * quarter) + recv1[group][
                at, rows_of(which), :
            ].astype(F32)
            if part:
                recv1[group][at, rows_of(which), :] = total.astype(BF16)
                return
            slot_free(kind, 1, second_sent)
            send2[group][kind % 2] = total.astype(BF16)
            for from_end, here in ((True, end), (False, inner)):

                @pl.when(here)
                def _():
                    for index in range(2):
                        second_copy(kind, index, from_end).start()

        def last_copy(kind):
            group, at, _ = KINDS[kind]
            return remote(
                sendf[group].at[kind % 2], recvf[group].at[at], r.ssem, (kind, 2), to[GATHER_2]
            )

        def last_sent(kind):
            last_copy(kind).wait_send()

        def out_copy(kind):
            group = KINDS[kind][0]
            buffer = cross_buf[group] if kind in CROSSED else out_buf[group].at[kind % 2]
            return pltpu.make_async_copy(buffer, outs[kind], r.osem.at[2 + kind])

        def store(kind, half, value):
            group = KINDS[kind][0]
            count = value.shape[1]
            start = pl.multiple_of(half * count, HEAD)
            if kind in CROSSED:
                cross_buf[group][pl.ds(start, count), :] = value.T
            else:
                out_buf[group][kind % 2, :, pl.ds(start, count)] = value

        finished = []

        def third_sums(kind):
            group, at, _ = KINDS[kind]
            slot_free(kind, 2, last_sent)
            for part in range(2):
                pass_copy(kind, part, 0).wait_recv()

            def total(which):
                rows = pl.ds(pl.multiple_of(which * eighth, eighth), eighth)
                kept = pl.ds(pl.multiple_of(mine2 * quarter + which * eighth, eighth), eighth)
                return recv1[group][at, kept, :].astype(F32) + recv2[group][at, rows, :].astype(F32)

            sendf[group][kind % 2] = total(1 - half2).astype(BF16)
            last_copy(kind).start()
            key = (group, kind % 2, kind in CROSSED)
            if key in stored:
                assert stored[key] in finished
                out_copy(stored[key]).wait()
            stored[key] = kind
            store(kind, half2, total(half2))

        def finish(kind):
            group, at, _ = KINDS[kind]
            last_copy(kind).wait_recv()
            store(kind, 1 - half2, recvf[group][at].astype(F32))
            out_copy(kind).start()
            finished.append(kind)

        actions = (
            one, far, first_sums, second_sums, lambda kind, part: third_sums(kind),
            lambda kind, part: finish(kind), lambda kind, part: pass_on(kind, part, 0),
            lambda kind, part: pass_on(kind, part, 1),
        )
        stage = 0
        for item in SCHEDULE:
            if item == 800:
                small_sum(stage)
                stage += 1
                if stage <= len(BITS):
                    small_copy(stage).start()
            else:
                actions[item // 100](item // 10 % 10, item % 10)
        r.smalls[...] = small[...]
        for (_, _, stage), kind in last.items():
            (first_sent, second_sent, last_sent)[stage](kind)

        @pl.when(inner)
        def _():
            for kind in range(COUNT):
                for part in range(2):
                    for which in range(2):
                        pass_copy(kind, part, which).wait_send()

        for kind in stored.values():
            out_copy(kind).wait()

    wide_cols, cols = wide.shape[-1], r.mixed.shape[-1]
    each = lambda count, height, dtype: [
        pltpu.VMEM((*count, height, wide_cols), dtype), pltpu.VMEM((*count, height, cols), dtype)
    ]
    pl.run_scoped(
        sums_phase, pltpu.VMEM((3, 8 * tokens, width // 2), BF16),
        *each((2,), 8 * tokens, BF16), *each((2,), 2 * quarter, BF16),
        *each((2,), quarter, BF16), *each((2,), eighth, BF16),
        pltpu.VMEM((2, HEAD, 2 * wide_cols), F32), pltpu.VMEM((2, HEAD, 2 * cols), F32),
        pltpu.VMEM((2 * wide_cols, HEAD), F32), pltpu.VMEM((2 * cols, HEAD), F32),
    )
    for a in range(2):
        lefts.sent(a)
    for kind in range(COUNT):
        for name in ("one", "two", "far"):
            for part in range(parts(kind)):
                right_copy(kind, name, part).wait_send()
    pltpu.make_async_copy(state, r.ingrad, r.csem.at[7]).wait()


def call_block(
    hidden, tokens, cot, second, wb, conv, gain, beta, norm1, norm2, early,
    yn, dy, xn, wg, wu, wd, wq, wk, wv, wgo, wo, mixed, resid, inv,
):
    count, width = second.shape
    rows, hidden_cols, cols = 2 * count, wg.shape[1] // 2, wq.shape[1] // 2
    vmem = pl.BlockSpec(memory_space=pltpu.VMEM)
    anywhere = pl.BlockSpec(memory_space=pl.ANY)
    columns = lambda kind: 2 * (hidden_cols, cols)[KINDS[kind][0]]
    shape = lambda kind: (columns(kind), HEAD) if kind in CROSSED else (HEAD, columns(kind))
    sds = jax.ShapeDtypeStruct
    each = lambda height: [
        pltpu.VMEM((3, height, hidden_cols), BF16), pltpu.VMEM((5, height, cols), BF16)
    ]
    sem = pltpu.SemaphoreType.DMA
    half = width // 2
    relay = [sds((3, half // 4, hidden_cols), BF16), sds((5, half // 4, cols), BF16)]
    return pl.pallas_call(
        block_kernel,
        in_specs=[vmem] * 10 + [anywhere] * 15,
        out_specs=[vmem, anywhere, vmem] + [anywhere] * 16,
        out_shape=[
            sds((count, width), BF16), sds((count, width), F32), sds((SMALL_ROWS, width), F32),
            *(sds(shape(kind), F32) for kind in range(COUNT)),
            sds((2, 8 * count, half), BF16), sds((3, 3, rows, hidden_cols), BF16),
            sds((5, 3, rows, cols), BF16), sds((2, 4, rows, cols), BF16), *relay, *relay,
        ],
        scratch_shapes=[
            pltpu.VMEM((2, 2, count, half), BF16), pltpu.VMEM((2, 3, rows, hidden_cols), BF16),
            *each(half // 2), *each(half // 4), *each(half // 8),
            pltpu.VMEM((3, count, width), BF16), pltpu.VMEM((rows, width), BF16),
            pltpu.VMEM((count, width), F32), pltpu.VMEM((SMALL_ROWS, width), F32),
            pltpu.VMEM((len(BITS) + 1, SMALL_ROWS, width), F32), pltpu.VMEM(conv.shape, F32),
            pltpu.VMEM((1, HEAD), F32), pltpu.VMEM(beta.shape, BF16),
            sem((2, 2, 7)), sem((2, COUNT, 3, 2)), sem((15,)), sem((2, 4)), sem((2, COUNT, 3)),
            sem((3, COUNT, 2)), sem((3, COUNT, 2)), sem((2, len(BITS) + 1)), sem((2, 7)),
            sem((2 + COUNT,)),
        ],
        compiler_params=pltpu.CompilerParams(
            vmem_limit_bytes=62 * 1024 * 1024, collective_id=1, has_side_effects=True
        ),
        cost_estimate=pl.CostEstimate(flops=5 * 10**10, bytes_accessed=2 * 10**8, transcendentals=0),
        name="block",
    )(
        hidden, tokens, cot, second, wb, conv, gain, beta, norm1, norm2, early,
        yn, dy, xn, wg, wu, wd, wq, wk, wv, wgo, wo, mixed, resid, inv,
    )


def finish_kernel(*refs):
    count = (len(refs) - 7) // 3
    small, sources = refs[0], refs[1 : 1 + count]
    n1, n2, conv, head, beta = refs[1 + count : 6 + count]
    targets, held, sems = refs[6 + count : 6 + 2 * count], refs[6 + 2 * count : -1], refs[-1]
    loads, stores = (
        [
            pltpu.make_async_copy(source, target, sems.at[way, index])
            for index, (source, target) in enumerate(zip(*pair, strict=True))
        ]
        for way, pair in enumerate(((sources, held), (held, targets)))
    )
    for load in loads:
        load.start()
    n1[...] = small[16:17, :]
    n2[...] = small[17:18, :]
    head[...] = small[18:19, :HEAD]
    cols = conv.shape[-1]
    for kind in range(3):
        for offset in range(CONV):
            row = kind * CONV + offset
            lanes = slice(0, cols) if row < 8 else slice(cols, 2 * cols)
            conv[kind, offset : offset + 1, :] = small[8 + row % 8 : 9 + row % 8, lanes]
    start = pl.multiple_of(lax.axis_index("dp") * HEAD, HEAD)
    beta[...] = small[0:8, pl.ds(start, HEAD)]
    for load, store in zip(loads, stores):
        load.wait()
        store.start()
    for store in stores:
        store.wait()


def call_finish(small, conv, arrays):
    width = small.shape[1]
    vmem = pl.BlockSpec(memory_space=pltpu.VMEM)
    anywhere = pl.BlockSpec(memory_space=pl.ANY)
    sds = jax.ShapeDtypeStruct
    return pl.pallas_call(
        finish_kernel,
        in_specs=[vmem] + [anywhere] * len(arrays),
        out_specs=[vmem] * 5 + [anywhere] * len(arrays),
        out_shape=[
            sds((1, width), F32), sds((1, width), F32), sds(conv.shape, F32), sds((1, HEAD), F32),
            sds((8, HEAD), F32), *(sds(each.shape, each.dtype) for each in arrays),
        ],
        scratch_shapes=[
            *(pltpu.VMEM(each.shape, each.dtype) for each in arrays),
            pltpu.SemaphoreType.DMA((2, len(arrays))),
        ],
        compiler_params=pltpu.CompilerParams(vmem_limit_bytes=VMEM_LIMIT),
        name="finish",
    )(small, *arrays)


def local(
    tokens, norm1_gain, w_query, w_key, w_value, w_beta, w_gate_out, conv_weights, head_gain,
    w_out, norm2_gain, w_gate, w_up, w_down, cotangent, cubic,
):
    gain_row = head_gain.reshape(1, HEAD)
    beta_rows = w_beta.T
    if cubic:
        norm1_row, norm2_row = norm1_gain.reshape(1, -1), norm2_gain.reshape(1, -1)
        mixed, resid, beta, inverses, hidden_state, second_own, xn, dy, yn, early = call_front(
            tokens, cotangent, w_query, w_key, w_value, w_gate_out, beta_rows, conv_weights,
            gain_row, w_out, norm1_row, norm2_row,
        )
        block_out, input_grad, small, *grads = call_block(
            hidden_state, tokens, cotangent, second_own, beta_rows, conv_weights, gain_row, beta,
            norm1_row, norm2_row, early, yn, dy, xn, w_gate, w_up, w_down, w_query, w_key, w_value,
            w_gate_out, w_out, mixed, resid, inverses,
        )
        norm1_sum, norm2_sum, conv_total, head_sum, beta_sum, block_out, input_grad, *grads = (
            call_finish(small, conv_weights, [block_out, input_grad, *grads[:COUNT]])
        )
        grad_down, grad_gate, grad_up, grad_out = grads[:4]
        grad_query, grad_key, grad_value, grad_gate_out = grads[4:]
        return (
            block_out, input_grad, norm1_sum[0], grad_query, grad_key, grad_value, beta_sum.T,
            grad_gate_out, conv_total, head_sum[0], grad_out, norm2_sum[0], grad_gate, grad_up,
            grad_down,
        )

    core = lax.axis_index("tensor")
    inputs = tokens.astype(F32)
    first_scale = lax.rsqrt(jnp.mean(inputs * inputs, -1, keepdims=True) + norm_eps)
    first_own = (inputs * first_scale * norm1_gain).astype(BF16)
    first_normed = both_rows(first_own, sibling(first_own), core)
    out_grad = both_rows(cotangent, sibling(cotangent), core)
    mixed, out_part, resid, beta, inverses = call_mixer_forward(
        first_normed, w_query, w_key, w_value, w_gate_out, beta_rows, conv_weights, gain_row, w_out
    )
    hidden_state = inputs + swap_sum(out_part, core)
    second_scale = lax.rsqrt(jnp.mean(hidden_state * hidden_state, -1, keepdims=True) + norm_eps)
    second_own = (hidden_state * second_scale * norm2_gain).astype(BF16)
    second_normed = both_rows(second_own, sibling(second_own), core)
    wide, down_part, back_part = call_mlp(second_normed, out_grad, w_gate, w_up, w_down)
    block_out = hidden_state + swap_sum(down_part, core)
    second_grad = swap_sum(back_part, core)
    norm2_part = jnp.sum(second_grad * hidden_state * second_scale, 0)
    state_grad = cotangent.astype(F32) + norm_back(
        second_grad, hidden_state, second_scale, norm2_gain
    )
    state_own = state_grad.astype(BF16)
    state_rows = both_rows(state_own, sibling(state_own), core)
    low, beta_low, first_part, conv_grad, head_part = call_mixer_backward(
        state_rows, w_query, w_key, w_value, w_gate_out, beta_rows, conv_weights, gain_row, w_out,
        resid, beta, inverses,
    )
    first_grad = swap_sum(first_part, core)
    norm1_part = jnp.sum(first_grad * inputs * first_scale, 0)
    input_grad = state_grad + norm_back(first_grad, inputs, first_scale, norm1_gain)
    scatter = lambda value, axis: lax.psum_scatter(value, "dp", scatter_dimension=axis, tiled=True)
    whole = lambda value: jnp.concatenate([value[0], value[1]], 1)
    product, gate_grad, up_grad = (whole(wide[:, kind]) for kind in range(3))
    grad_down = scatter(dot(product, out_grad, TN), 1)
    grad_gate = scatter(dot(second_normed, gate_grad, TN), 0)
    grad_up = scatter(dot(second_normed, up_grad, TN), 0)
    grad_out = scatter(dot(whole(mixed), state_rows, TN), 1)
    grad_query, grad_key, grad_value, grad_gate_out = (
        scatter(dot(first_normed, whole(low[:, kind]), TN), 0) for kind in range(4)
    )
    beta_sum = scatter(dot(first_normed, beta_low, TN), 0)
    conv_total = lax.psum(conv_grad, "dp")
    norm1_sum, norm2_sum, head_sum = lax.psum(
        (norm1_part, norm2_part, head_part.reshape(-1)), ("dp", "tensor")
    )
    return (
        block_out.astype(BF16), input_grad, norm1_sum, grad_query, grad_key, grad_value, beta_sum,
        grad_gate_out, conv_total, head_sum, grad_out, norm2_sum, grad_gate, grad_up, grad_down,
    )


def solution(mesh):
    rows = P(("dp", "tensor"), None)
    columns = P(None, "tensor")
    in_specs = (
        rows, P(), columns, columns, columns, columns, columns, P(None, None, "tensor"), P(),
        P("tensor", None), P(), columns, columns, P("tensor", None), rows,
    )
    scattered = P("dp", "tensor")
    crossed = P("tensor", "dp")
    out_specs = (
        rows, rows, P(), scattered, scattered, scattered, scattered, scattered,
        P(None, None, "tensor"), P(), crossed, P(), scattered, scattered, crossed,
    )
    cubic = mesh.shape["dp"] == 16
    return jax.shard_map(
        functools.partial(local, cubic=cubic), mesh=mesh, in_specs=in_specs, out_specs=out_specs,
        check_vma=False,
    )
```

```python
import functools
import typing

import jax
import jax.numpy as jnp
from jax import lax
from jax.experimental import pallas as pl
from jax.experimental.pallas import tpu as pltpu
from jax.sharding import PartitionSpec as P

HEAD = 128
CONV = 4
PAIR = 2 * HEAD
GROUP = 4 * HEAD
F32 = jnp.float32
BF16 = jnp.bfloat16
norm_eps = 1e-06
unit_eps = 1e-06
VMEM_LIMIT = 56 * 1024 * 1024

NN = (((1,), (0,)), ((), ()))
NT = (((1,), (1,)), ((), ()))
TN = (((0,), (0,)), ((), ()))


def dot(left, right, dims=NN):
    return lax.dot_general(left, right, dims, preferred_element_type=F32)


def halves(value):
    high = value.astype(BF16)
    return high, (value - high.astype(F32)).astype(BF16)


def dot3(left, right, dims=NN):
    left_high, left_low = halves(left)
    right_high, right_low = halves(right)
    return (
        dot(left_high, right_low, dims) + dot(left_low, right_high, dims)
    ) + dot(left_high, right_high, dims)


def rows_down(value, shift):
    if shift == 0:
        return value
    row = lax.broadcasted_iota(jnp.int32, value.shape, 0)
    return jnp.where(row >= shift, pltpu.roll(value, shift, 0), 0.0)


def rows_up(value, shift):
    if shift == 0:
        return value
    rows = value.shape[0]
    row = lax.broadcasted_iota(jnp.int32, value.shape, 0)
    return jnp.where(row < rows - shift, pltpu.roll(value, rows - shift, 0), 0.0)


def causal_conv(value, taps):
    total = value * taps[CONV - 1 : CONV]
    for offset in range(CONV - 1):
        total = total + rows_down(value, CONV - 1 - offset) * taps[offset : offset + 1]
    return total


def sigmoid(value):
    return 1.0 / (1.0 + jnp.exp(-value))


def tri_mask(rows, strict):
    row = lax.broadcasted_iota(jnp.int32, (rows, rows), 0)
    col = lax.broadcasted_iota(jnp.int32, (rows, rows), 1)
    return row > col if strict else row >= col


def unit_lower_inverses(lowers):
    size = lowers[0].shape[0]
    row = lax.broadcasted_iota(jnp.int32, (size, size), 0)
    col = lax.broadcasted_iota(jnp.int32, (size, size), 1)
    eye = jnp.where(row == col, 1.0, 0.0)
    lows = [lower.astype(BF16) for lower in lowers]
    level, inverses = 0, None
    while (1 << level) < size:
        mask = (
            ((row >> (level + 1)) == (col >> (level + 1)))
            & (((row >> level) & 1) == 1)
            & (((col >> level) & 1) == 0)
        )
        if inverses is None:
            inverses = [eye - jnp.where(mask, lower, 0.0) for lower in lowers]
        else:
            known = [inverse.astype(BF16) for inverse in inverses]
            parts = [jnp.where(mask, low, jnp.zeros_like(low)) for low in lows]
            inner = [dot(part, each).astype(BF16) for part, each in zip(parts, known)]
            inverses = [
                inverse - dot(each, right)
                for inverse, each, right in zip(inverses, known, inner)
            ]
        level += 1
    lefts = [
        (eye - inverse - dot3(lower, inverse)).astype(BF16)
        for lower, inverse in zip(lowers, inverses)
    ]
    return [
        inverse + dot(inverse.astype(BF16), left) for inverse, left in zip(inverses, lefts)
    ]


def head_column(values, head):
    lane = lax.broadcasted_iota(jnp.int32, values.shape, 1)
    return jnp.sum(jnp.where(lane == head, values, 0.0), -1, keepdims=True)


def forward_group(
    step, xn_ref, wq_ref, wk_ref, wv_ref, wg_ref, wb_ref, conv_ref, gain_ref, wo_ref,
    mixed_ref, resid_ref, beta_ref, inv_ref, total,
):
    xn = xn_ref[...]
    rows = xn.shape[0]
    half = rows // 2

    @pl.when(step == 0)
    def _():
        beta_ref[...] = dot(xn, wb_ref[...], NT)
        total[...] = jnp.zeros_like(total)

    query_in = dot(xn, wq_ref[...])
    key_in = dot(xn, wk_ref[...])
    value_in = dot(xn, wv_ref[...])
    gate_in = dot(xn, wg_ref[...])
    for place, value in enumerate((query_in, key_in, value_in, gate_in)):
        resid_ref[place] = value
    beta_all = sigmoid(beta_ref[...])
    conv_q = causal_conv(query_in, conv_ref[0])
    conv_k = causal_conv(key_in, conv_ref[1])
    conv_v = causal_conv(value_in, conv_ref[2])
    query_act = conv_q * sigmoid(conv_q)
    key_act = conv_k * sigmoid(conv_k)
    value_act = conv_v * sigmoid(conv_v)
    gate_act = gate_in * sigmoid(gate_in)
    strict = tri_mask(rows, True)
    causal = tri_mask(rows, False)
    heads = []
    for head in range(GROUP // HEAD):
        cols = slice(head * HEAD, (head + 1) * HEAD)
        queries = query_act[:, cols]
        queries = queries * lax.rsqrt(jnp.sum(queries * queries, -1, keepdims=True) + unit_eps)
        queries = queries * HEAD**-0.5
        keys = key_act[:, cols]
        keys = keys * lax.rsqrt(jnp.sum(keys * keys, -1, keepdims=True) + unit_eps)
        beta = head_column(beta_all, GROUP // HEAD * step + head)
        lower = jnp.where(strict, dot3(keys, keys, NT) * beta, 0.0)
        scores = jnp.where(causal, dot3(queries, keys, NT), 0.0)
        heads.append((cols, lower, scores, value_act[:, cols] * beta))
    inverses = unit_lower_inverses(
        [lower[part, part] for _, lower, _, _ in heads for part in (slice(0, half), slice(half, rows))]
    )
    for head, (cols, lower, scores, weighted) in enumerate(heads):
        first, second = inverses[2 * head : 2 * head + 2]
        inv_ref[head, 0] = first
        inv_ref[head, 1] = second
        upper_u = dot3(first, weighted[:half])
        lower_u = dot3(second, weighted[half:] - dot3(lower[half:, :half], upper_u))
        updates = jnp.concatenate([upper_u, lower_u], 0)
        resid_ref[4, :, cols] = updates
        output = dot3(scores, updates)
        resid_ref[5, :, cols] = output
        normed = output * lax.rsqrt(jnp.mean(output * output, -1, keepdims=True) + norm_eps)
        mixed_ref[0, :, cols] = (normed * gain_ref[...] * gate_act[:, cols]).astype(BF16)
    total[...] += dot(mixed_ref[0], wo_ref[...])


def mixer_forward(
    xn_ref, wq_ref, wk_ref, wv_ref, wg_ref, wb_ref, conv_ref, gain_ref, wo_ref,
    mixed_ref, part_ref, resid_ref, beta_ref, inv_ref, total,
):
    step = pl.program_id(0)
    forward_group(
        step, xn_ref, wq_ref, wk_ref, wv_ref, wg_ref, wb_ref, conv_ref, gain_ref, wo_ref,
        mixed_ref, resid_ref, beta_ref, inv_ref, total,
    )

    @pl.when(step == pl.num_programs(0) - 1)
    def _():
        part_ref[...] = total[...].astype(BF16)


def call_mixer_forward(xn, wq, wk, wv, wg, wb, conv, gain, wo):
    rows, width = xn.shape
    cols = wq.shape[1]
    groups = cols // GROUP
    heads = wb.shape[0]
    whole = lambda *shape: pl.BlockSpec(shape, lambda i: (0,) * len(shape))
    weight = pl.BlockSpec((width, GROUP), lambda i: (0, i))
    return pl.pallas_call(
        mixer_forward,
        grid=(groups,),
        in_specs=[
            whole(rows, width), weight, weight, weight, weight, whole(heads, width),
            pl.BlockSpec((3, CONV, GROUP), lambda i: (0, 0, i)), whole(1, HEAD),
            pl.BlockSpec((GROUP, width), lambda i: (i, 0)),
        ],
        out_specs=[
            pl.BlockSpec((1, rows, GROUP), lambda i: (i // (groups // 2), 0, i % (groups // 2))),
            whole(rows, width), pl.BlockSpec((6, rows, GROUP), lambda i: (0, 0, i)), whole(rows, heads),
            pl.BlockSpec((GROUP // HEAD, 2, rows // 2, rows // 2), lambda i: (i, 0, 0, 0)),
        ],
        out_shape=[
            jax.ShapeDtypeStruct((2, rows, cols // 2), BF16),
            jax.ShapeDtypeStruct((rows, width), BF16),
            jax.ShapeDtypeStruct((6, rows, cols), F32), jax.ShapeDtypeStruct((rows, heads), F32),
            jax.ShapeDtypeStruct((heads, 2, rows // 2, rows // 2), F32),
        ],
        scratch_shapes=[pltpu.VMEM((rows, width), F32)],
        compiler_params=pltpu.CompilerParams(vmem_limit_bytes=VMEM_LIMIT),
        cost_estimate=pl.CostEstimate(
            flops=2 * rows * width * cols * 5 + 10**10, bytes_accessed=5 * width * cols * 2 + 10**7,
            transcendentals=0,
        ),
        name="mixer_forward",
    )(xn, wq, wk, wv, wg, wb, conv, gain, wo)


def silu_slope(value, sig):
    return sig * (1.0 + value * (1.0 - sig))


def backward_pair(
    step, steps, dh_ref, wq_ref, wk_ref, wv_ref, wg_ref, wb_ref, conv_ref, gain_ref, wo_ref,
    resid_ref, beta_ref, inv_ref, low_ref, bl_ref, dconv_ref, dgain_ref, total, beta_total,
):
    rows = dh_ref.shape[0]
    half = rows // 2

    @pl.when(step == 0)
    def _():
        total[...] = jnp.zeros_like(total)
        beta_total[...] = jnp.zeros_like(beta_total)
        dgain_ref[...] = jnp.zeros_like(dgain_ref)

    mixed_grad = dot(dh_ref[...], wo_ref[...], NT)
    query_in, key_in, value_in, gate_in = (resid_ref[place] for place in range(4))
    beta_all = sigmoid(beta_ref[...])
    lane = lax.broadcasted_iota(jnp.int32, beta_all.shape, 1)
    conv_q = causal_conv(query_in, conv_ref[0])
    conv_k = causal_conv(key_in, conv_ref[1])
    conv_v = causal_conv(value_in, conv_ref[2])
    sig_q, sig_k, sig_v = sigmoid(conv_q), sigmoid(conv_k), sigmoid(conv_v)
    sig_g = sigmoid(gate_in)
    query_act = conv_q * sig_q
    key_act = conv_k * sig_k
    value_act = conv_v * sig_v
    gate_act = gate_in * sig_g
    strict = tri_mask(rows, True)
    causal = tri_mask(rows, False)
    grads_q, grads_k, grads_v, grads_g = [], [], [], []
    gain = gain_ref[...]
    for head in range(2):
        cols = slice(head * HEAD, (head + 1) * HEAD)
        raw_q, raw_k, values = query_act[:, cols], key_act[:, cols], value_act[:, cols]
        scale_q = lax.rsqrt(jnp.sum(raw_q * raw_q, -1, keepdims=True) + unit_eps)
        scale_k = lax.rsqrt(jnp.sum(raw_k * raw_k, -1, keepdims=True) + unit_eps)
        queries = raw_q * scale_q * HEAD**-0.5
        keys = raw_k * scale_k
        beta = head_column(beta_all, 2 * step + head)
        updates = resid_ref[4, :, cols]
        output = resid_ref[5, :, cols]
        upstream = mixed_grad[:, cols]
        scale_o = lax.rsqrt(jnp.mean(output * output, -1, keepdims=True) + norm_eps)
        unit_out = output * scale_o
        grads_g.append(upstream * (unit_out * gain))
        d_normed = upstream * gate_act[:, cols]
        dgain_ref[...] += jnp.sum(d_normed * unit_out, 0, keepdims=True)
        d_unit = d_normed * gain
        d_output = scale_o * (d_unit - unit_out * jnp.mean(d_unit * unit_out, -1, keepdims=True))
        inner = dot3(keys, keys, NT)
        lower_21 = inner[half:, :half] * beta[half:]
        scores = jnp.where(causal, dot3(queries, keys, NT), 0.0)
        d_scores = jnp.where(causal, dot3(d_output, updates, NT), 0.0)
        d_updates = dot3(scores, d_output, TN)
        d_right_2 = dot3(inv_ref[head, 1], d_updates[half:], TN)
        d_right_1 = dot3(
            inv_ref[head, 0], d_updates[:half] - dot3(lower_21, d_right_2, TN), TN
        )
        d_right = jnp.concatenate([d_right_1, d_right_2], 0)
        d_lower = jnp.where(strict, -dot3(d_right, updates, NT), 0.0)
        d_beta = jnp.sum(d_lower * inner, -1, keepdims=True) + jnp.sum(
            d_right * values, -1, keepdims=True
        )
        grads_v.append(d_right * beta)
        d_inner = d_lower * beta
        d_keys = dot3(d_scores, queries, TN) + dot3(d_inner, keys) + dot3(d_inner, keys, TN)
        d_queries = dot3(d_scores, keys) * HEAD**-0.5
        grads_q.append(
            scale_q
            * (d_queries - raw_q * (scale_q * scale_q) * jnp.sum(d_queries * raw_q, -1, keepdims=True))
        )
        grads_k.append(
            scale_k
            * (d_keys - raw_k * (scale_k * scale_k) * jnp.sum(d_keys * raw_k, -1, keepdims=True))
        )
        d_beta_in = d_beta * beta * (1.0 - beta)
        beta_total[...] += jnp.where(lane == 2 * step + head, d_beta_in, 0.0)
    for kind, (grads, pre, conv, sig) in enumerate(
        (
            (grads_q, query_in, conv_q, sig_q),
            (grads_k, key_in, conv_k, sig_k),
            (grads_v, value_in, conv_v, sig_v),
        )
    ):
        d_conv = jnp.concatenate(grads, 1) * silu_slope(conv, sig)
        taps = conv_ref[kind]
        d_pre = d_conv * taps[CONV - 1 : CONV]
        for offset in range(CONV):
            shift = CONV - 1 - offset
            dconv_ref[kind, offset : offset + 1, :] = jnp.sum(
                d_conv * rows_down(pre, shift), 0, keepdims=True
            )
            if shift:
                d_pre = d_pre + rows_up(d_conv, shift) * taps[offset : offset + 1]
        low_ref[0, kind] = d_pre.astype(BF16)
    low_ref[0, 3] = (jnp.concatenate(grads_g, 1) * silu_slope(gate_in, sig_g)).astype(BF16)
    total[...] += (
        dot(low_ref[0, 0], wq_ref[...], NT)
        + dot(low_ref[0, 1], wk_ref[...], NT)
        + dot(low_ref[0, 2], wv_ref[...], NT)
        + dot(low_ref[0, 3], wg_ref[...], NT)
    )

    @pl.when(step == steps - 1)
    def _():
        bl_ref[...] = beta_total[...].astype(BF16)
        total[...] += dot(bl_ref[...], wb_ref[...])


def mixer_backward(
    dh_ref, wq_ref, wk_ref, wv_ref, wg_ref, wb_ref, conv_ref, gain_ref, wo_ref,
    resid_ref, beta_ref, inv_ref, low_ref, bl_ref, part_ref, dconv_ref, dgain_ref,
    total, beta_total,
):
    step, steps = pl.program_id(0), pl.num_programs(0)
    backward_pair(
        step, steps, dh_ref, wq_ref, wk_ref, wv_ref, wg_ref, wb_ref, conv_ref, gain_ref, wo_ref,
        resid_ref, beta_ref, inv_ref, low_ref, bl_ref, dconv_ref, dgain_ref, total, beta_total,
    )

    @pl.when(step == steps - 1)
    def _():
        part_ref[...] = total[...].astype(BF16)


def call_mixer_backward(dh, wq, wk, wv, wg, wb, conv, gain, wo, resid, beta, inv):
    rows, width = dh.shape
    cols = wq.shape[1]
    pairs = cols // PAIR
    heads = wb.shape[0]
    whole = lambda *shape: pl.BlockSpec(shape, lambda i: (0,) * len(shape))
    weight = pl.BlockSpec((width, PAIR), lambda i: (0, i))
    taps = pl.BlockSpec((3, CONV, PAIR), lambda i: (0, 0, i))
    return pl.pallas_call(
        mixer_backward,
        grid=(pairs,),
        in_specs=[
            whole(rows, width), weight, weight, weight, weight, whole(heads, width), taps,
            whole(1, HEAD), pl.BlockSpec((PAIR, width), lambda i: (i, 0)),
            pl.BlockSpec((6, rows, PAIR), lambda i: (0, 0, i)), whole(rows, heads),
            pl.BlockSpec((2, 2, rows // 2, rows // 2), lambda i: (i, 0, 0, 0)),
        ],
        out_specs=[
            pl.BlockSpec((1, 4, rows, PAIR), lambda i: (i // (pairs // 2), 0, 0, i % (pairs // 2))),
            whole(rows, heads), whole(rows, width), taps, whole(1, HEAD),
        ],
        out_shape=[
            jax.ShapeDtypeStruct((2, 4, rows, cols // 2), BF16),
            jax.ShapeDtypeStruct((rows, heads), BF16),
            jax.ShapeDtypeStruct((rows, width), BF16), jax.ShapeDtypeStruct(conv.shape, F32),
            jax.ShapeDtypeStruct((1, HEAD), F32),
        ],
        scratch_shapes=[pltpu.VMEM((rows, width), F32), pltpu.VMEM((rows, heads), F32)],
        compiler_params=pltpu.CompilerParams(vmem_limit_bytes=VMEM_LIMIT),
        cost_estimate=pl.CostEstimate(
            flops=2 * rows * width * cols * 5 + 2 * 10**10,
            bytes_accessed=5 * width * cols * 2 + 10**7,
            transcendentals=0,
        ),
        name="mixer_backward",
    )(dh, wq, wk, wv, wg, wb, conv, gain, wo, resid, beta, inv)


def mlp_copies(index, slot, wg_ref, wu_ref, wd_ref, wg_buf, wu_buf, wd_buf, sems):
    hidden = wg_ref.shape[1] // 2
    for part in range(2):
        start = pl.multiple_of(part * hidden + index * HEAD, HEAD)
        lanes = pl.ds(part * HEAD, HEAD)
        yield pltpu.make_async_copy(
            wg_ref.at[:, pl.ds(start, HEAD)], wg_buf.at[slot, :, lanes], sems.at[slot, part]
        )
        yield pltpu.make_async_copy(
            wu_ref.at[:, pl.ds(start, HEAD)], wu_buf.at[slot, :, lanes], sems.at[slot, 2 + part]
        )
        yield pltpu.make_async_copy(
            wd_ref.at[pl.ds(start, HEAD), :], wd_buf.at[slot, lanes, :], sems.at[slot, 4 + part]
        )


def mlp_tile(step, steps, yn_ref, dy_ref, weights, low_store, down_total, back_total):
    wg_ref, wu_ref, wd_ref, wg_buf, wu_buf, wd_buf, sems = weights
    slot = lax.rem(step, 2)

    @pl.when(step == 0)
    def _():
        down_total[...] = jnp.zeros_like(down_total)
        back_total[...] = jnp.zeros_like(back_total)

    @pl.when(step + 1 < steps)
    def _():
        for copy in mlp_copies(step + 1, 1 - slot, *weights):
            copy.start()

    for copy in mlp_copies(step, slot, *weights):
        copy.wait()
    yn, dy = yn_ref[...], dy_ref[...]
    w_gate, w_up, w_down = wg_buf[slot], wu_buf[slot], wd_buf[slot]
    gate = dot(yn, w_gate)
    up = dot(yn, w_up)
    d_product = dot(dy, w_down, NT)
    sig = sigmoid(gate)
    act = gate * sig
    product = (act * up).astype(BF16)
    gate_grad = (d_product * up * silu_slope(gate, sig)).astype(BF16)
    up_grad = (d_product * act).astype(BF16)
    down_total[...] += dot(product, w_down)
    back_total[...] += dot(gate_grad, w_gate, NT) + dot(up_grad, w_up, NT)
    for kind, value in enumerate((product, gate_grad, up_grad)):
        low_store(0, kind, value[:, :HEAD])
        low_store(1, kind, value[:, HEAD:])


def mlp_kernel(
    yn_ref, dy_ref, wg_ref, wu_ref, wd_ref, low_ref, down_ref, back_ref,
    wg_buf, wu_buf, wd_buf, down_total, back_total, sems,
):
    step, steps = pl.program_id(0), pl.num_programs(0)
    weights = (wg_ref, wu_ref, wd_ref, wg_buf, wu_buf, wd_buf, sems)

    @pl.when(step == 0)
    def _():
        for copy in mlp_copies(0, 0, *weights):
            copy.start()

    def low_store(half, kind, value):
        low_ref[half, kind] = value

    mlp_tile(step, steps, yn_ref, dy_ref, weights, low_store, down_total, back_total)

    @pl.when(step == steps - 1)
    def _():
        down_ref[...] = down_total[...].astype(BF16)
        back_ref[...] = back_total[...].astype(BF16)


def call_mlp(yn, dy, w_gate, w_up, w_down):
    rows, width = yn.shape
    hidden = w_gate.shape[1] // 2
    whole = lambda *shape: pl.BlockSpec(shape, lambda i: (0,) * len(shape))
    anywhere = pl.BlockSpec(memory_space=pl.ANY)
    tile = pl.BlockSpec((2, 3, rows, HEAD), lambda i: (0, 0, 0, i))
    return pl.pallas_call(
        mlp_kernel,
        grid=(hidden // HEAD,),
        in_specs=[whole(rows, width), whole(rows, width), anywhere, anywhere, anywhere],
        out_specs=[tile, whole(rows, width), whole(rows, width)],
        out_shape=[
            jax.ShapeDtypeStruct((2, 3, rows, hidden), BF16),
            jax.ShapeDtypeStruct((rows, width), BF16),
            jax.ShapeDtypeStruct((rows, width), BF16),
        ],
        scratch_shapes=[
            pltpu.VMEM((2, width, PAIR), BF16), pltpu.VMEM((2, width, PAIR), BF16),
            pltpu.VMEM((2, PAIR, width), BF16), pltpu.VMEM((rows, width), F32),
            pltpu.VMEM((rows, width), F32), pltpu.SemaphoreType.DMA((2, 6)),
        ],
        compiler_params=pltpu.CompilerParams(vmem_limit_bytes=VMEM_LIMIT),
        cost_estimate=pl.CostEstimate(
            flops=12 * rows * width * w_gate.shape[1], bytes_accessed=6 * width * w_gate.shape[1],
            transcendentals=0,
        ),
        name="mlp",
    )(yn, dy, w_gate, w_up, w_down)


def norm_back(upstream, inputs, scale_rows, gain_row):
    scaled_grad = upstream * gain_row
    return scale_rows * (
        scaled_grad
        - inputs * scale_rows * scale_rows * jnp.mean(scaled_grad * inputs, -1, keepdims=True)
    )


def take(value, axis, index):
    return lax.dynamic_index_in_dim(value, index, axis, keepdims=False)


def sibling(value):
    return lax.ppermute(value, "tensor", [(0, 1), (1, 0)])


def both_rows(mine, other, core):
    axis = mine.ndim - 2
    return jnp.where(
        core == 0, jnp.concatenate([mine, other], axis), jnp.concatenate([other, mine], axis)
    )


def swap_sum(partial, core):
    parts = partial.reshape(2, -1, partial.shape[-1])
    received = sibling(take(parts, 0, 1 - core))
    return take(parts, 0, core).astype(F32) + received.astype(F32)


BIT_X, BIT_Y, BIT_ZA, BIT_ZB = 1, 2, 4, 8
GATHER_2 = BIT_ZA
BITS = (1, 2, 4, 8)
SMALL_BITS = (8, 4, 2, 1)
CHIPS = 16
MESH = pl.DeviceIdType.MESH
KINDS = ((0, 0, 0), (0, 1, 2), (0, 2, 2), (1, 0, 3), (1, 1, 1), (1, 2, 1), (1, 3, 1), (1, 4, 1))
COUNT = len(KINDS)
CROSSED = (0, 3)
GATHER_1 = (BIT_Y, BIT_Y, BIT_X, BIT_X)
REDUCE_1 = tuple(BIT_X + BIT_Y - bit for bit in GATHER_1)
LEFT_SLOT = (0, 0, 2, 1)
SMALL_ROWS = 24
FIRST_STEPS = (
    830,
)
TILE_STEPS = {5: (10, 800, 30,), 8: (810,)}
LAST_TILE_STEPS = (
    1, 801, 21, 110, 0, 1100, 11,
)
PAIR_STEPS = {0: (811, 101,), 1: (1200, 130, 1101, 100, 821,), 2: (111, 1201,)}
SCHEDULE = (
    840, 850, 230, 200, 231, 50, 901, 330, 210, 630, 631, 820,
    140, 201, 300, 121, 20, 870, 700, 731, 900, 600, 860, 40,
    150, 301, 211, 310, 240, 241, 701, 340, 740, 120, 601, 900,
    160, 730, 610, 331, 741, 250, 711, 251, 60, 641, 640, 311,
    710, 220, 430, 221, 341, 611, 400, 350, 351, 410, 70, 900,
    320, 260, 261, 321, 750, 720, 620, 440, 170, 360, 270, 271,
    721, 621, 751, 651, 761, 760, 900, 540, 361, 650, 500, 900,
    661, 370, 420, 371, 530, 671, 770, 450, 660, 771, 670, 460,
    550, 470, 560, 520, 510, 570,
)


def block_place(block, left):
    bit = lambda mask: int((block & mask) != 0)
    return bit(GATHER_1[left]), bit(REDUCE_1[left]) * 4 + bit(BIT_ZB) * 2 + bit(GATHER_2)


class Place:
    def __init__(self, tokens):
        self.chip, self.core = lax.axis_index("dp"), lax.axis_index("tensor")
        self.bit = {mask: lax.rem(self.chip // mask, 2) for mask in BITS}
        step = {mask: mask * (1 - 2 * self.bit[mask]) for mask in BITS}
        self.to = {mask: (self.chip + step[mask], self.core) for mask in BITS}
        self.mirror = (self.chip + step[BIT_ZA] + step[BIT_ZB], self.core)
        self.near = (self.chip, 1 - self.core)
        self.own_rows = pl.ds(pl.multiple_of(self.core * tokens, tokens), tokens)
        self.other_rows = pl.ds(pl.multiple_of((1 - self.core) * tokens, tokens), tokens)
        self.tokens = tokens

    def greet(self, partners):
        barrier = pltpu.get_barrier_semaphore()
        for target in partners:
            pl.semaphore_signal(barrier, inc=1, device_id=target, device_id_type=MESH)
        pl.semaphore_wait(barrier, len(partners))


def remote_pair(source, target, send_sem, recv_sem, device):
    return pltpu.make_async_remote_copy(
        src_ref=source, dst_ref=target, send_sem=send_sem, recv_sem=recv_sem,
        device_id=device, device_id_type=MESH,
    )


def remote(source, target, sems, index, device):
    return remote_pair(source, target, sems.at[(0, *index)], sems.at[(1, *index)], device)


class Lefts:
    def __init__(self, lefts, place, own, landed, sems, local_sems):
        self.place, self.own, self.landed, self.sems, self.local = place, own, landed, sems, local_sems
        self.lefts = lefts

    def rows(self, a, piece):
        tokens = self.place.tokens
        start = pl.multiple_of((2 * piece + self.place.core) * tokens, tokens)
        return self.landed.at[a, pl.ds(start, tokens), :]

    def copy(self, a, name):
        place, own, sems = self.place, self.own, self.sems
        first = GATHER_1[self.lefts[a]]
        half = place.bit[first]
        if name == "one":
            return remote(own.at[a, 1 - half], self.rows(a, 1), sems, (a, 0), place.to[first])
        if name == "two":
            return remote(own.at[a, half], self.rows(a, 2), sems, (a, 1), place.to[GATHER_2])
        if name == "far":
            return remote(self.rows(a, 1), self.rows(a, 3), sems, (a, 2), place.to[GATHER_2])
        if name == 0:
            return remote(own.at[a, half], self.rows(a, 0), sems, (a, 3), place.near)
        return remote(self.rows(a, name), self.rows(a, name), sems, (a, 3 + name), place.near)

    def own_copy(self, a):
        half = self.place.bit[GATHER_1[self.lefts[a]]]
        return pltpu.make_async_copy(self.own.at[a, half], self.rows(a, 0), self.local.at[a])

    def start(self, a, natural):
        for block in range(CHIPS):
            half, place = block_place(block, self.lefts[a])
            self.own[a, half, :, place * HEAD : (place + 1) * HEAD] = natural[
                :, block * HEAD : (block + 1) * HEAD
            ]
        for name in ("one", "two", 0):
            self.copy(a, name).start()
        self.own_copy(a).start()

    def middle(self, a):
        self.copy(a, "one").wait_recv()
        self.copy(a, "far").start()
        self.copy(a, 1).start()
        self.copy(a, "two").wait_recv()
        self.copy(a, 2).start()

    def far(self, a):
        self.copy(a, "far").wait_recv()
        self.copy(a, 3).start()

    def arrived(self, a):
        for piece in range(4):
            self.copy(a, piece).wait_recv()
        self.own_copy(a).wait()

    def sent(self, a):
        for name in ("one", "two", "far", 0, 1, 2, 3):
            self.copy(a, name).wait_send()


def front_kernel(
    tokens_ref, cot_ref, wq_ref, wk_ref, wv_ref, wg_ref, wb_ref, conv_ref, gain_ref, wo_ref,
    norm1_ref, norm2_ref,
    mixed_ref, resid_ref, beta_ref, inv_ref, hidden_ref, second_ref, xn_out, dy_out, yn_out,
    landed,
    total, xn, dy, yn, own, stage, part, wbuf, wobuf, lsem, qsem, csem, wsem,
):
    step, steps = pl.program_id(0), pl.num_programs(0)
    place = Place(tokens_ref.shape[0])
    own_rows, other_rows = place.own_rows, place.other_rows
    lefts = Lefts((0, 1), place, own, landed, lsem, csem)

    def row_copy(index):
        source = stage if index == 2 else (xn, dy, None, yn)[index].at[own_rows, :]
        target = part if index == 2 else source
        return remote(source, target, qsem, (index,), place.near)

    def out_copy(index):
        source, target = ((xn, xn_out), (dy, dy_out), (yn, yn_out))[index]
        return pltpu.make_async_copy(source, target, csem.at[2 + index])

    def weight_copies(group):
        columns = pl.ds(pl.multiple_of(group * GROUP, GROUP), GROUP)
        for index, weight in enumerate((wq_ref, wk_ref, wv_ref, wg_ref)):
            yield pltpu.make_async_copy(
                weight.at[:, columns], wbuf.at[group, index], wsem.at[group, index]
            )
        yield pltpu.make_async_copy(wo_ref.at[columns, :], wobuf.at[group], wsem.at[group, 4])

    @pl.when(step == 0)
    def _():
        for group in range(wbuf.shape[0]):
            for copy in weight_copies(group):
                copy.start()
        place.greet((place.to[BIT_X], place.to[BIT_Y], place.to[GATHER_2], place.near))
        inputs = tokens_ref[...].astype(F32)
        scale = lax.rsqrt(jnp.mean(inputs * inputs, -1, keepdims=True) + norm_eps)
        xn[own_rows, :] = (inputs * scale * norm1_ref[...]).astype(BF16)
        row_copy(0).start()
        dy[own_rows, :] = cot_ref[...]
        row_copy(1).start()
        lefts.start(0, cot_ref)
        lefts.start(1, xn[own_rows, :])
        row_copy(0).wait()
        out_copy(0).start()

    for copy in weight_copies(step):
        copy.wait()
    forward_group(
        step, xn, *(wbuf.at[step, index] for index in range(4)), wb_ref, conv_ref, gain_ref,
        wobuf.at[step], mixed_ref, resid_ref, beta_ref, inv_ref, total,
    )

    @pl.when(step == 0)
    def _():
        row_copy(1).wait()
        out_copy(1).start()
        lefts.middle(0)
        lefts.middle(1)

    @pl.when(step == steps - 1)
    def _():
        stage[...] = total[other_rows, :].astype(BF16)
        row_copy(2).start()
        lefts.far(0)
        lefts.far(1)
        hidden = tokens_ref[...].astype(F32) + total[own_rows, :]
        row_copy(2).wait()
        hidden = hidden + part[...].astype(F32)
        hidden_ref[...] = hidden
        scale = lax.rsqrt(jnp.mean(hidden * hidden, -1, keepdims=True) + norm_eps)
        second = (hidden * scale * norm2_ref[...]).astype(BF16)
        yn[own_rows, :] = second
        row_copy(3).start()
        second_ref[...] = second
        for a in range(2):
            lefts.arrived(a)
            lefts.sent(a)
        row_copy(3).wait()
        out_copy(2).start()
        for index in range(3):
            out_copy(index).wait()


def call_front(tokens, cot, wq, wk, wv, wg, wb, conv, gain, wo, norm1, norm2):
    count, width = tokens.shape
    rows, cols, heads = 2 * count, wq.shape[1], wb.shape[0]
    groups = cols // GROUP
    sds = jax.ShapeDtypeStruct
    whole = lambda *shape: pl.BlockSpec(shape, lambda i: (0,) * len(shape))
    anywhere = pl.BlockSpec(memory_space=pl.ANY)
    sem = pltpu.SemaphoreType.DMA
    low = lambda *shape: pltpu.VMEM(shape, BF16)
    return pl.pallas_call(
        front_kernel,
        grid=(groups,),
        in_specs=[
            whole(count, width), whole(count, width), anywhere, anywhere, anywhere, anywhere,
            whole(heads, width), pl.BlockSpec((3, CONV, GROUP), lambda i: (0, 0, i)),
            whole(1, HEAD), anywhere, whole(1, width), whole(1, width),
        ],
        out_specs=[
            pl.BlockSpec((1, rows, GROUP), lambda i: (i // (groups // 2), 0, i % (groups // 2))),
            pl.BlockSpec((6, rows, GROUP), lambda i: (0, 0, i)), whole(rows, heads),
            pl.BlockSpec((GROUP // HEAD, 2, count, count), lambda i: (i, 0, 0, 0)),
            whole(count, width), whole(count, width), anywhere, anywhere, anywhere, anywhere,
        ],
        out_shape=[
            sds((2, rows, cols // 2), BF16), sds((6, rows, cols), F32), sds((rows, heads), F32),
            sds((heads, 2, count, count), F32), sds((count, width), F32),
            sds((count, width), BF16), sds((rows, width), BF16), sds((rows, width), BF16),
            sds((rows, width), BF16), sds((2, 8 * count, width // 2), BF16),
        ],
        scratch_shapes=[
            pltpu.VMEM((rows, width), F32), low(rows, width), low(rows, width), low(rows, width),
            low(2, 2, count, width // 2), low(count, width), low(count, width),
            low(groups, 4, width, GROUP), low(groups, GROUP, width),
            sem((2, 2, 7)), sem((2, 4)), sem((5,)), sem((groups, 5)),
        ],
        compiler_params=pltpu.CompilerParams(
            vmem_limit_bytes=VMEM_LIMIT, collective_id=2, has_side_effects=True
        ),
        cost_estimate=pl.CostEstimate(flops=2 * 10**10, bytes_accessed=4 * 10**7, transcendentals=0),
        name="front",
    )(tokens, cot, wq, wk, wv, wg, wb, conv, gain, wo, norm1, norm2)


class Refs(typing.NamedTuple):
    hidden: typing.Any
    tokens: typing.Any
    cot: typing.Any
    second: typing.Any
    wb: typing.Any
    conv: typing.Any
    gain: typing.Any
    beta: typing.Any
    norm1: typing.Any
    norm2: typing.Any
    early: typing.Any
    yn: typing.Any
    dy: typing.Any
    xn: typing.Any
    wg: typing.Any
    wu: typing.Any
    wd: typing.Any
    wq: typing.Any
    wk: typing.Any
    wv: typing.Any
    wgo: typing.Any
    wo: typing.Any
    mixed: typing.Any
    resid: typing.Any
    inv: typing.Any
    out: typing.Any
    ingrad: typing.Any
    smalls: typing.Any
    lefts: typing.Any
    gws: typing.Any
    gns: typing.Any
    lows: typing.Any
    paw: typing.Any
    pan: typing.Any
    pbw: typing.Any
    pbn: typing.Any
    own: typing.Any
    wide: typing.Any
    r1w: typing.Any
    r1n: typing.Any
    r2w: typing.Any
    r2n: typing.Any
    rfw: typing.Any
    rfn: typing.Any
    rows: typing.Any
    dh: typing.Any
    state: typing.Any
    small: typing.Any
    first: typing.Any
    smallr: typing.Any
    dconv: typing.Any
    dgain: typing.Any
    bl: typing.Any
    lsem: typing.Any
    rsem: typing.Any
    csem: typing.Any
    qsem: typing.Any
    ssem: typing.Any
    zsem: typing.Any
    fsem: typing.Any
    psem: typing.Any
    msem: typing.Any
    osem: typing.Any


def block_kernel(*refs):
    outs = refs[28 : 28 + COUNT]
    r = Refs(*refs[:28], *refs[28 + COUNT :])
    own, wide, dh, state, small = r.own, r.wide, r.dh, r.state, r.small
    recv1, recv2, recvf = (r.r1w, r.r1n), (r.r2w, r.r2n), (r.rfw, r.rfn)
    landed = (r.gws, r.gns)
    relay = ((r.paw, r.pan), (r.pbw, r.pbn))
    tokens, width = r.second.shape
    place = Place(tokens)
    bit, to, near = place.bit, place.to, place.near
    own_rows, other_rows = place.own_rows, place.other_rows
    quarter, eighth = width // 8, width // 16
    half2, mine2 = bit[GATHER_2], bit[BIT_ZB]
    end = bit[BIT_ZA] == bit[BIT_ZB]
    inner = bit[BIT_ZA] != bit[BIT_ZB]
    place.greet((*to.values(), place.mirror, near))
    lefts = Lefts((2, 3), place, own, r.lefts, r.lsem, r.csem)

    def source(kind, half):
        group, place, _ = KINDS[kind]
        if group == 0:
            return wide.at[half, place]
        return r.mixed.at[half] if place == 0 else r.lows.at[half, place - 1]

    def right_landed(kind, piece):
        group, place, _ = KINDS[kind]
        return landed[group].at[place, piece - 1]

    split = wide.shape[-1] // HEAD // 2 * HEAD + HEAD

    def parts(kind):
        return 2 if KINDS[kind][0] == 0 else 1

    def right_copy(kind, name, part):
        columns = slice(None)
        if parts(kind) == 2:
            columns = slice(0, split) if part == 0 else slice(split, wide.shape[-1])
        view = lambda ref: ref.at[:, columns]
        if name == "one":
            return remote(
                view(source(kind, half2)), view(right_landed(kind, 1)), r.rsem, (kind, 0, part),
                to[GATHER_1[KINDS[kind][2]]],
            )
        if name == "two":
            return remote(
                view(source(kind, 1 - half2)), view(right_landed(kind, 2)), r.rsem,
                (kind, 1, part), to[GATHER_2],
            )
        return remote(
            view(right_landed(kind, 2)), view(right_landed(kind, 3)), r.rsem, (kind, 2, part),
            to[GATHER_1[KINDS[kind][2]]],
        )

    def one(kind, part):
        right_copy(kind, "one", part).start()

    def two(kind, part):
        right_copy(kind, "two", part).start()

    def far(kind, part):
        right_copy(kind, "two", part).wait_recv()
        right_copy(kind, "far", part).start()

    def run(items, actions):
        for item in items:
            digits = (item % 10,) if item >= 1000 else (item // 10 % 10, item % 10)
            actions[item // 100](*digits)

    copy_actions = {0: one, 1: far, 8: two, 11: lefts.middle, 12: lefts.far}

    def run_at(step, table):
        for when, items in table.items():

            @pl.when(step == when)
            def _(items=items):
                run(items, copy_actions)

    def row_copy(index, source_ref):
        target = dh.at[own_rows, :] if index == 3 else r.rows.at[index]
        return remote(source_ref, target, r.qsem, (index,), near)

    def small_copy(stage):
        if stage == len(BITS):
            return remote(
                small.at[SMALL_ROWS - 8 :, :], r.smallr.at[stage, :8, :], r.psem, (stage,), near
            )
        return remote(small, r.smallr.at[stage], r.psem, (stage,), to[SMALL_BITS[stage]])

    def small_sum(stage):
        small_copy(stage).wait()
        if stage == len(BITS):
            small[SMALL_ROWS - 8 :, :] += r.smallr[stage, :8, :]
        else:
            small[...] += r.smallr[stage]

    steps = wide.shape[-1] // HEAD
    pairs = r.wq.shape[1] // PAIR

    def mixer_copies(pair, slot, wbuf, wobuf, resid_buf, inv_buf):
        columns = pl.ds(pl.multiple_of(pair * PAIR, PAIR), PAIR)
        sems = r.msem
        for index, weight in enumerate((r.wq, r.wk, r.wv, r.wgo)):
            yield pltpu.make_async_copy(
                weight.at[:, columns], wbuf.at[slot, index], sems.at[slot, index]
            )
        yield pltpu.make_async_copy(r.wo.at[columns, :], wobuf.at[slot], sems.at[slot, 4])
        yield pltpu.make_async_copy(
            r.resid.at[:, :, columns], resid_buf.at[slot], sems.at[slot, 5]
        )
        yield pltpu.make_async_copy(
            r.inv.at[pl.ds(2 * pair, 2)], inv_buf.at[slot], sems.at[slot, 6]
        )

    def mlp_phase(prefetch, yn, dy, wg_buf, wu_buf, wd_buf, down_total, back_total, stage):
        weights = (r.wg, r.wu, r.wd, wg_buf, wu_buf, wd_buf, r.msem)
        loads = [
            pltpu.make_async_copy(r.yn, yn, r.csem.at[4]),
            pltpu.make_async_copy(r.dy, dy, r.csem.at[5]),
        ]
        for copy in (*loads, *mlp_copies(0, 0, *weights)):
            copy.start()
        lefts.start(0, r.second)
        run(FIRST_STEPS, copy_actions)
        for copy in loads:
            copy.wait()

        @pl.loop(0, steps)
        def _(step):
            columns = pl.ds(pl.multiple_of(step * HEAD, HEAD), HEAD)

            def low_store(half, kind, value):
                wide[half, kind, :, columns] = value

            mlp_tile(step, steps, yn, dy, weights, low_store, down_total, back_total)
            run_at(step, TILE_STEPS)

        run(LAST_TILE_STEPS, copy_actions)
        prefetch()
        for index, total in enumerate((down_total, back_total)):
            stage[index] = total[other_rows, :].astype(BF16)
            row_copy(index, stage.at[index]).start()
        for index in range(2):
            row_copy(index, stage.at[index]).wait()
        hidden = r.hidden[...]
        r.out[...] = (hidden + down_total[own_rows, :] + r.rows[0].astype(F32)).astype(BF16)
        second_grad = back_total[own_rows, :] + r.rows[1].astype(F32)
        scale = lax.rsqrt(jnp.mean(hidden * hidden, -1, keepdims=True) + norm_eps)
        small[...] = jnp.zeros_like(small)
        small[17:18, :] = jnp.sum(second_grad * hidden * scale, 0, keepdims=True)
        grad = r.cot[...].astype(F32) + norm_back(second_grad, hidden, scale, r.norm2[...])
        state[...] = grad
        dh[own_rows, :] = grad.astype(BF16)
        row_copy(3, dh.at[own_rows, :]).start()
        lefts.start(1, dh[own_rows, :])
        row_copy(3, dh.at[own_rows, :]).wait()

    def mixer_phase(buffers, xn, total, beta_total, low_stage):
        wbuf, wobuf, resid_buf, inv_buf = buffers
        load = pltpu.make_async_copy(r.xn, xn, r.csem.at[6])
        load.start()

        def low_copy(pair, slot):
            target = r.lows.at[
                pair // 2, :, :, pl.ds(pl.multiple_of(lax.rem(pair, 2) * PAIR, PAIR), PAIR)
            ]
            return pltpu.make_async_copy(low_stage.at[slot, 0], target, r.osem.at[slot])

        @pl.loop(0, pairs)
        def _(pair):
            slot = lax.rem(pair, 2)

            @pl.when(pair + 1 < pairs)
            def _():
                for copy in mixer_copies(pair + 1, 1 - slot, *buffers):
                    copy.start()

            for copy in mixer_copies(pair, slot, *buffers):
                copy.wait()

            @pl.when(pair >= 2)
            def _():
                low_copy(pair - 2, slot).wait()

            lanes = pl.ds(pl.multiple_of(pair * PAIR, PAIR), PAIR)
            backward_pair(
                pair, pairs, dh, *(wbuf.at[slot, index] for index in range(4)), r.wb,
                r.conv.at[:, :, lanes], r.gain, wobuf.at[slot], resid_buf.at[slot],
                r.beta, inv_buf.at[slot], low_stage.at[slot], r.bl,
                r.dconv.at[:, :, lanes], r.dgain, total, beta_total,
            )
            low_copy(pair, slot).start()
            run_at(pair, PAIR_STEPS)

        for pair in (pairs - 2, pairs - 1):
            low_copy(pair, pair % 2).wait()
        r.rows[0] = total[other_rows, :].astype(BF16)
        row_copy(2, r.rows.at[0]).start()
        r.first[...] = total[own_rows, :]
        load.wait()
        small[0:8, :] = dot(r.bl[...], xn[...], TN)

    def first_norm_back():
        for kind in range(3):
            for offset in range(CONV):
                row = kind * CONV + offset
                lanes = slice(0, width // 2) if row < 8 else slice(width // 2, width)
                small[8 + row % 8 : 9 + row % 8, lanes] = r.dconv[kind, offset : offset + 1, :]
        small[18:19, :HEAD] = r.dgain[...]
        row_copy(2, r.rows.at[0]).wait()
        first_grad = r.first[...] + r.rows[2].astype(F32)
        inputs = r.tokens[...].astype(F32)
        scale = lax.rsqrt(jnp.mean(inputs * inputs, -1, keepdims=True) + norm_eps)
        small[16:17, :] = jnp.sum(first_grad * inputs * scale, 0, keepdims=True)
        small_copy(0).start()
        state[...] += norm_back(first_grad, inputs, scale, r.norm1[...])
        pltpu.make_async_copy(state, r.ingrad, r.csem.at[7]).start()

    def scoped_mixer(wbuf, wobuf, resid_buf, inv_buf):
        buffers = (wbuf, wobuf, resid_buf, inv_buf)

        def prefetch():
            for copy in mixer_copies(0, 0, *buffers):
                copy.start()

        rows = 2 * tokens
        pl.run_scoped(
            functools.partial(mlp_phase, prefetch),
            pltpu.VMEM((rows, width), BF16), pltpu.VMEM((rows, width), BF16),
            pltpu.VMEM((2, width, PAIR), BF16), pltpu.VMEM((2, width, PAIR), BF16),
            pltpu.VMEM((2, PAIR, width), BF16), pltpu.VMEM((rows, width), F32),
            pltpu.VMEM((rows, width), F32), pltpu.VMEM((2, tokens, width), BF16),
        )
        pl.run_scoped(
            functools.partial(mixer_phase, buffers),
            pltpu.VMEM((rows, width), BF16), pltpu.VMEM((rows, width), F32),
            pltpu.VMEM(r.beta.shape, F32), pltpu.VMEM((2, 1, 4, rows, PAIR), BF16),
        )

    pl.run_scoped(
        scoped_mixer, pltpu.VMEM((2, 4, width, PAIR), BF16), pltpu.VMEM((2, PAIR, width), BF16),
        pltpu.VMEM((2, 6, 2 * tokens, PAIR), F32), pltpu.VMEM((2, 2, 2, tokens, tokens), F32),
    )

    def sums_phase(left, gw, gn, s1w, s1n, s2w, s2n, sfw, sfn, ow, on, cw, cn):
        right, send1 = (gw, gn), (s1w, s1n)
        send2, sendf, out_buf, cross_buf = (s2w, s2n), (sfw, sfn), (ow, on), (cw, cn)

        def left_load(a):
            from_ref = r.early.at[a] if a < 2 else r.lefts.at[a - 2]
            return pltpu.make_async_copy(
                from_ref, left.at[LEFT_SLOT[a]], r.csem.at[8 + LEFT_SLOT[a]]
            )

        def right_loads(kind):
            group = KINDS[kind][0]
            rows = 2 * tokens
            for piece in range(4):
                yield pltpu.make_async_copy(
                    right_landed(kind, piece) if piece else source(kind, half2),
                    right[group].at[kind % 2, piece * rows : (piece + 1) * rows, :],
                    r.csem.at[11 + piece],
                )

        in_slot, right_slot = {}, {}

        def load(kind):
            group, _, a = KINDS[kind]
            right_slot[group, kind % 2] = kind
            fresh = in_slot.get(LEFT_SLOT[a]) != a
            if fresh:
                in_slot[LEFT_SLOT[a]] = a
                if a >= 2:
                    lefts.arrived(a - 2)
                left_load(a).start()
            for part in range(parts(kind)):
                right_copy(kind, "one", part).wait_recv()
                right_copy(kind, "far", part).wait_recv()
            for copy in right_loads(kind):
                copy.start()
            if fresh:
                left_load(a).wait()
            for copy in right_loads(kind):
                copy.wait()

        def product(kind, start):
            group, _, a = KINDS[kind]
            assert in_slot[LEFT_SLOT[a]] == a and right_slot[group, kind % 2] == kind
            lanes = pl.ds(pl.multiple_of(start, quarter), quarter)
            return dot(left[LEFT_SLOT[a], :, lanes], right[group][kind % 2], TN)

        def mine1(kind):
            return bit[REDUCE_1[KINDS[kind][2]]]

        def rows_of(which):
            return pl.ds(pl.multiple_of(which * quarter, quarter), quarter)

        last, stored = {}, {}

        def slot_free(kind, stage, wait):
            key = (KINDS[kind][0], kind % 2, stage)
            if key in last:
                wait(last[key])
            last[key] = kind

        def first_copy(kind, part):
            group, at, _ = KINDS[kind]
            rows = rows_of(1 - mine2 if part == 0 else mine2)
            return remote(
                send1[group].at[kind % 2, rows, :], recv1[group].at[at, rows, :], r.ssem,
                (kind, part), to[REDUCE_1[KINDS[kind][2]]],
            )

        def first_sent(kind):
            for part in range(2):
                first_copy(kind, part).wait_send()

        def first_sums(kind, part):
            if part == 0:
                load(kind)
                slot_free(kind, 0, first_sent)
            group = KINDS[kind][0]
            which = 1 - mine2 if part == 0 else mine2
            send1[group][kind % 2, rows_of(which), :] = product(
                kind, (1 - mine1(kind)) * 2 * quarter + which * quarter
            ).astype(BF16)
            first_copy(kind, part).start()

        def second_copy(kind, part, from_end):
            group, at, _ = KINDS[kind]
            rows = slice(part * eighth, (part + 1) * eighth)
            return remote_pair(
                send2[group].at[kind % 2, rows, :],
                relay[0 if from_end else 1][group].at[at, rows, :],
                r.zsem.at[0, kind, part], r.zsem.at[1 if from_end else 2, kind, part],
                to[BIT_ZA] if from_end else place.mirror,
            )

        def second_sent(kind):
            for part in range(2):
                second_copy(kind, part, True).wait_send()

        def pass_copy(kind, part, which):
            group, at, _ = KINDS[kind]
            rows = slice(part * eighth, (part + 1) * eighth)
            return remote_pair(
                relay[which][group].at[at, rows, :], recv2[group].at[at, rows, :],
                r.fsem.at[which, kind, part], r.fsem.at[2, kind, part],
                place.mirror if which == 0 else to[BIT_ZA],
            )

        def pass_on(kind, part, which):
            @pl.when(inner)
            def _():
                second_copy(kind, part, which == 0).wait_recv()
                pass_copy(kind, part, which).start()

        def second_sums(kind, part):
            group, at, _ = KINDS[kind]
            which = mine2 if part else 1 - mine2
            first_copy(kind, part).wait_recv()
            total = product(kind, mine1(kind) * 2 * quarter + which * quarter) + recv1[group][
                at, rows_of(which), :
            ].astype(F32)
            if part:
                recv1[group][at, rows_of(which), :] = total.astype(BF16)
                return
            slot_free(kind, 1, second_sent)
            send2[group][kind % 2] = total.astype(BF16)
            for from_end, here in ((True, end), (False, inner)):

                @pl.when(here)
                def _():
                    for index in range(2):
                        second_copy(kind, index, from_end).start()

        def last_copy(kind):
            group, at, _ = KINDS[kind]
            return remote(
                sendf[group].at[kind % 2], recvf[group].at[at], r.ssem, (kind, 2), to[GATHER_2]
            )

        def last_sent(kind):
            last_copy(kind).wait_send()

        def out_copy(kind):
            group = KINDS[kind][0]
            buffer = cross_buf[group] if kind in CROSSED else out_buf[group].at[kind % 2]
            return pltpu.make_async_copy(buffer, outs[kind], r.osem.at[2 + kind])

        def store(kind, half, value):
            group = KINDS[kind][0]
            count = value.shape[1]
            start = pl.multiple_of(half * count, HEAD)
            if kind in CROSSED:
                cross_buf[group][pl.ds(start, count), :] = value.T
            else:
                out_buf[group][kind % 2, :, pl.ds(start, count)] = value

        finished = []

        def third_sums(kind):
            group, at, _ = KINDS[kind]
            slot_free(kind, 2, last_sent)
            for part in range(2):
                pass_copy(kind, part, 0).wait_recv()

            def total(which):
                rows = pl.ds(pl.multiple_of(which * eighth, eighth), eighth)
                kept = pl.ds(pl.multiple_of(mine2 * quarter + which * eighth, eighth), eighth)
                return recv1[group][at, kept, :].astype(F32) + recv2[group][at, rows, :].astype(F32)

            sendf[group][kind % 2] = total(1 - half2).astype(BF16)
            last_copy(kind).start()
            key = (group, kind % 2, kind in CROSSED)
            if key in stored:
                assert stored[key] in finished
                out_copy(stored[key]).wait()
            stored[key] = kind
            store(kind, half2, total(half2))

        def finish(kind):
            group, at, _ = KINDS[kind]
            last_copy(kind).wait_recv()
            store(kind, 1 - half2, recvf[group][at].astype(F32))
            out_copy(kind).start()
            finished.append(kind)

        stage = 0

        def small_step(kind, part):
            nonlocal stage
            if part == 1:
                first_norm_back()
                return
            small_sum(stage)
            stage += 1
            if stage <= len(BITS):
                small_copy(stage).start()

        actions = {
            **copy_actions, 2: first_sums, 3: second_sums, 4: lambda kind, part: third_sums(kind),
            5: lambda kind, part: finish(kind), 6: lambda kind, part: pass_on(kind, part, 0),
            7: lambda kind, part: pass_on(kind, part, 1), 9: small_step,
        }
        run(SCHEDULE, actions)
        r.smalls[...] = small[...]
        for (_, _, stage), kind in last.items():
            (first_sent, second_sent, last_sent)[stage](kind)

        @pl.when(inner)
        def _():
            for kind in range(COUNT):
                for part in range(2):
                    for which in range(2):
                        pass_copy(kind, part, which).wait_send()

        for kind in stored.values():
            out_copy(kind).wait()

    wide_cols, cols = wide.shape[-1], r.mixed.shape[-1]
    each = lambda count, height, dtype: [
        pltpu.VMEM((*count, height, wide_cols), dtype), pltpu.VMEM((*count, height, cols), dtype)
    ]
    pl.run_scoped(
        sums_phase, pltpu.VMEM((3, 8 * tokens, width // 2), BF16),
        *each((2,), 8 * tokens, BF16), *each((2,), 2 * quarter, BF16),
        *each((2,), quarter, BF16), *each((2,), eighth, BF16),
        pltpu.VMEM((2, HEAD, 2 * wide_cols), F32), pltpu.VMEM((2, HEAD, 2 * cols), F32),
        pltpu.VMEM((2 * wide_cols, HEAD), F32), pltpu.VMEM((2 * cols, HEAD), F32),
    )
    for a in range(2):
        lefts.sent(a)
    for kind in range(COUNT):
        for name in ("one", "two", "far"):
            for part in range(parts(kind)):
                right_copy(kind, name, part).wait_send()
    pltpu.make_async_copy(state, r.ingrad, r.csem.at[7]).wait()


def call_block(
    hidden, tokens, cot, second, wb, conv, gain, beta, norm1, norm2, early,
    yn, dy, xn, wg, wu, wd, wq, wk, wv, wgo, wo, mixed, resid, inv,
):
    count, width = second.shape
    rows, hidden_cols, cols = 2 * count, wg.shape[1] // 2, wq.shape[1] // 2
    vmem = pl.BlockSpec(memory_space=pltpu.VMEM)
    anywhere = pl.BlockSpec(memory_space=pl.ANY)
    columns = lambda kind: 2 * (hidden_cols, cols)[KINDS[kind][0]]
    shape = lambda kind: (columns(kind), HEAD) if kind in CROSSED else (HEAD, columns(kind))
    sds = jax.ShapeDtypeStruct
    each = lambda height: [
        pltpu.VMEM((3, height, hidden_cols), BF16), pltpu.VMEM((5, height, cols), BF16)
    ]
    sem = pltpu.SemaphoreType.DMA
    half = width // 2
    relay = [sds((3, half // 4, hidden_cols), BF16), sds((5, half // 4, cols), BF16)]
    return pl.pallas_call(
        block_kernel,
        in_specs=[vmem] * 10 + [anywhere] * 15,
        out_specs=[vmem, anywhere, vmem] + [anywhere] * 16,
        out_shape=[
            sds((count, width), BF16), sds((count, width), F32), sds((SMALL_ROWS, width), F32),
            *(sds(shape(kind), F32) for kind in range(COUNT)),
            sds((2, 8 * count, half), BF16), sds((3, 3, rows, hidden_cols), BF16),
            sds((5, 3, rows, cols), BF16), sds((2, 4, rows, cols), BF16), *relay, *relay,
        ],
        scratch_shapes=[
            pltpu.VMEM((2, 2, count, half), BF16), pltpu.VMEM((2, 3, rows, hidden_cols), BF16),
            *each(half // 2), *each(half // 4), *each(half // 8),
            pltpu.VMEM((3, count, width), BF16), pltpu.VMEM((rows, width), BF16),
            pltpu.VMEM((count, width), F32), pltpu.VMEM((SMALL_ROWS, width), F32),
            pltpu.VMEM((count, width), F32),
            pltpu.VMEM((len(BITS) + 1, SMALL_ROWS, width), F32), pltpu.VMEM(conv.shape, F32),
            pltpu.VMEM((1, HEAD), F32), pltpu.VMEM(beta.shape, BF16),
            sem((2, 2, 7)), sem((2, COUNT, 3, 2)), sem((15,)), sem((2, 4)), sem((2, COUNT, 3)),
            sem((3, COUNT, 2)), sem((3, COUNT, 2)), sem((2, len(BITS) + 1)), sem((2, 7)),
            sem((2 + COUNT,)),
        ],
        compiler_params=pltpu.CompilerParams(
            vmem_limit_bytes=62 * 1024 * 1024, collective_id=1, has_side_effects=True
        ),
        cost_estimate=pl.CostEstimate(flops=5 * 10**10, bytes_accessed=2 * 10**8, transcendentals=0),
        name="block",
    )(
        hidden, tokens, cot, second, wb, conv, gain, beta, norm1, norm2, early,
        yn, dy, xn, wg, wu, wd, wq, wk, wv, wgo, wo, mixed, resid, inv,
    )


def finish_kernel(*refs):
    count = (len(refs) - 7) // 3
    small, sources = refs[0], refs[1 : 1 + count]
    n1, n2, conv, head, beta = refs[1 + count : 6 + count]
    targets, held, sems = refs[6 + count : 6 + 2 * count], refs[6 + 2 * count : -1], refs[-1]
    loads, stores = (
        [
            pltpu.make_async_copy(source, target, sems.at[way, index])
            for index, (source, target) in enumerate(zip(*pair, strict=True))
        ]
        for way, pair in enumerate(((sources, held), (held, targets)))
    )
    for load in loads:
        load.start()
    n1[...] = small[16:17, :]
    n2[...] = small[17:18, :]
    head[...] = small[18:19, :HEAD]
    cols = conv.shape[-1]
    for kind in range(3):
        for offset in range(CONV):
            row = kind * CONV + offset
            lanes = slice(0, cols) if row < 8 else slice(cols, 2 * cols)
            conv[kind, offset : offset + 1, :] = small[8 + row % 8 : 9 + row % 8, lanes]
    start = pl.multiple_of(lax.axis_index("dp") * HEAD, HEAD)
    beta[...] = small[0:8, pl.ds(start, HEAD)]
    for load, store in zip(loads, stores):
        load.wait()
        store.start()
    for store in stores:
        store.wait()


def call_finish(small, conv, arrays):
    width = small.shape[1]
    vmem = pl.BlockSpec(memory_space=pltpu.VMEM)
    anywhere = pl.BlockSpec(memory_space=pl.ANY)
    sds = jax.ShapeDtypeStruct
    return pl.pallas_call(
        finish_kernel,
        in_specs=[vmem] + [anywhere] * len(arrays),
        out_specs=[vmem] * 5 + [anywhere] * len(arrays),
        out_shape=[
            sds((1, width), F32), sds((1, width), F32), sds(conv.shape, F32), sds((1, HEAD), F32),
            sds((8, HEAD), F32), *(sds(each.shape, each.dtype) for each in arrays),
        ],
        scratch_shapes=[
            *(pltpu.VMEM(each.shape, each.dtype) for each in arrays),
            pltpu.SemaphoreType.DMA((2, len(arrays))),
        ],
        compiler_params=pltpu.CompilerParams(vmem_limit_bytes=VMEM_LIMIT),
        name="finish",
    )(small, *arrays)


def local(
    tokens, norm1_gain, w_query, w_key, w_value, w_beta, w_gate_out, conv_weights, head_gain,
    w_out, norm2_gain, w_gate, w_up, w_down, cotangent, cubic,
):
    gain_row = head_gain.reshape(1, HEAD)
    beta_rows = w_beta.T
    if cubic:
        norm1_row, norm2_row = norm1_gain.reshape(1, -1), norm2_gain.reshape(1, -1)
        mixed, resid, beta, inverses, hidden_state, second_own, xn, dy, yn, early = call_front(
            tokens, cotangent, w_query, w_key, w_value, w_gate_out, beta_rows, conv_weights,
            gain_row, w_out, norm1_row, norm2_row,
        )
        block_out, input_grad, small, *grads = call_block(
            hidden_state, tokens, cotangent, second_own, beta_rows, conv_weights, gain_row, beta,
            norm1_row, norm2_row, early, yn, dy, xn, w_gate, w_up, w_down, w_query, w_key, w_value,
            w_gate_out, w_out, mixed, resid, inverses,
        )
        norm1_sum, norm2_sum, conv_total, head_sum, beta_sum, block_out, input_grad, *grads = (
            call_finish(small, conv_weights, [block_out, input_grad, *grads[:COUNT]])
        )
        grad_down, grad_gate, grad_up, grad_out = grads[:4]
        grad_query, grad_key, grad_value, grad_gate_out = grads[4:]
        return (
            block_out, input_grad, norm1_sum[0], grad_query, grad_key, grad_value, beta_sum.T,
            grad_gate_out, conv_total, head_sum[0], grad_out, norm2_sum[0], grad_gate, grad_up,
            grad_down,
        )

    core = lax.axis_index("tensor")
    inputs = tokens.astype(F32)
    first_scale = lax.rsqrt(jnp.mean(inputs * inputs, -1, keepdims=True) + norm_eps)
    first_own = (inputs * first_scale * norm1_gain).astype(BF16)
    first_normed = both_rows(first_own, sibling(first_own), core)
    out_grad = both_rows(cotangent, sibling(cotangent), core)
    mixed, out_part, resid, beta, inverses = call_mixer_forward(
        first_normed, w_query, w_key, w_value, w_gate_out, beta_rows, conv_weights, gain_row, w_out
    )
    hidden_state = inputs + swap_sum(out_part, core)
    second_scale = lax.rsqrt(jnp.mean(hidden_state * hidden_state, -1, keepdims=True) + norm_eps)
    second_own = (hidden_state * second_scale * norm2_gain).astype(BF16)
    second_normed = both_rows(second_own, sibling(second_own), core)
    wide, down_part, back_part = call_mlp(second_normed, out_grad, w_gate, w_up, w_down)
    block_out = hidden_state + swap_sum(down_part, core)
    second_grad = swap_sum(back_part, core)
    norm2_part = jnp.sum(second_grad * hidden_state * second_scale, 0)
    state_grad = cotangent.astype(F32) + norm_back(
        second_grad, hidden_state, second_scale, norm2_gain
    )
    state_own = state_grad.astype(BF16)
    state_rows = both_rows(state_own, sibling(state_own), core)
    low, beta_low, first_part, conv_grad, head_part = call_mixer_backward(
        state_rows, w_query, w_key, w_value, w_gate_out, beta_rows, conv_weights, gain_row, w_out,
        resid, beta, inverses,
    )
    first_grad = swap_sum(first_part, core)
    norm1_part = jnp.sum(first_grad * inputs * first_scale, 0)
    input_grad = state_grad + norm_back(first_grad, inputs, first_scale, norm1_gain)
    scatter = lambda value, axis: lax.psum_scatter(value, "dp", scatter_dimension=axis, tiled=True)
    whole = lambda value: jnp.concatenate([value[0], value[1]], 1)
    product, gate_grad, up_grad = (whole(wide[:, kind]) for kind in range(3))
    grad_down = scatter(dot(product, out_grad, TN), 1)
    grad_gate = scatter(dot(second_normed, gate_grad, TN), 0)
    grad_up = scatter(dot(second_normed, up_grad, TN), 0)
    grad_out = scatter(dot(whole(mixed), state_rows, TN), 1)
    grad_query, grad_key, grad_value, grad_gate_out = (
        scatter(dot(first_normed, whole(low[:, kind]), TN), 0) for kind in range(4)
    )
    beta_sum = scatter(dot(first_normed, beta_low, TN), 0)
    conv_total = lax.psum(conv_grad, "dp")
    norm1_sum, norm2_sum, head_sum = lax.psum(
        (norm1_part, norm2_part, head_part.reshape(-1)), ("dp", "tensor")
    )
    return (
        block_out.astype(BF16), input_grad, norm1_sum, grad_query, grad_key, grad_value, beta_sum,
        grad_gate_out, conv_total, head_sum, grad_out, norm2_sum, grad_gate, grad_up, grad_down,
    )


def solution(mesh):
    rows = P(("dp", "tensor"), None)
    columns = P(None, "tensor")
    in_specs = (
        rows, P(), columns, columns, columns, columns, columns, P(None, None, "tensor"), P(),
        P("tensor", None), P(), columns, columns, P("tensor", None), rows,
    )
    scattered = P("dp", "tensor")
    crossed = P("tensor", "dp")
    out_specs = (
        rows, rows, P(), scattered, scattered, scattered, scattered, scattered,
        P(None, None, "tensor"), P(), crossed, P(), scattered, scattered, crossed,
    )
    cubic = mesh.shape["dp"] == 16
    return jax.shard_map(
        functools.partial(local, cubic=cubic), mesh=mesh, in_specs=in_specs, out_specs=out_specs,
        check_vma=False,
    )
```

```python
import functools
import typing

import jax
import jax.numpy as jnp
from jax import lax
from jax.experimental import pallas as pl
from jax.experimental.pallas import tpu as pltpu
from jax.sharding import PartitionSpec as P

HEAD = 128
CONV = 4
PAIR = 2 * HEAD
GROUP = 4 * HEAD
F32 = jnp.float32
BF16 = jnp.bfloat16
norm_eps = 1e-06
unit_eps = 1e-06
VMEM_LIMIT = 56 * 1024 * 1024

NN = (((1,), (0,)), ((), ()))
NT = (((1,), (1,)), ((), ()))
TN = (((0,), (0,)), ((), ()))


def dot(left, right, dims=NN):
    return lax.dot_general(left, right, dims, preferred_element_type=F32)


def halves(value):
    high = value.astype(BF16)
    return high, (value - high.astype(F32)).astype(BF16)


def dot3(left, right, dims=NN):
    left_high, left_low = halves(left)
    right_high, right_low = halves(right)
    return (
        dot(left_high, right_low, dims) + dot(left_low, right_high, dims)
    ) + dot(left_high, right_high, dims)


def rows_down(value, shift):
    if shift == 0:
        return value
    row = lax.broadcasted_iota(jnp.int32, value.shape, 0)
    return jnp.where(row >= shift, pltpu.roll(value, shift, 0), 0.0)


def rows_up(value, shift):
    if shift == 0:
        return value
    rows = value.shape[0]
    row = lax.broadcasted_iota(jnp.int32, value.shape, 0)
    return jnp.where(row < rows - shift, pltpu.roll(value, rows - shift, 0), 0.0)


def causal_conv(value, taps):
    total = value * taps[CONV - 1 : CONV]
    for offset in range(CONV - 1):
        total = total + rows_down(value, CONV - 1 - offset) * taps[offset : offset + 1]
    return total


def sigmoid(value):
    return 1.0 / (1.0 + jnp.exp(-value))


def tri_mask(rows, strict):
    row = lax.broadcasted_iota(jnp.int32, (rows, rows), 0)
    col = lax.broadcasted_iota(jnp.int32, (rows, rows), 1)
    return row > col if strict else row >= col


def unit_lower_inverses(lowers):
    size = lowers[0].shape[0]
    row = lax.broadcasted_iota(jnp.int32, (size, size), 0)
    col = lax.broadcasted_iota(jnp.int32, (size, size), 1)
    eye = jnp.where(row == col, 1.0, 0.0)
    lows = [lower.astype(BF16) for lower in lowers]
    level, inverses = 0, None
    while (1 << level) < size:
        mask = (
            ((row >> (level + 1)) == (col >> (level + 1)))
            & (((row >> level) & 1) == 1)
            & (((col >> level) & 1) == 0)
        )
        if inverses is None:
            inverses = [eye - jnp.where(mask, lower, 0.0) for lower in lowers]
        else:
            known = [inverse.astype(BF16) for inverse in inverses]
            parts = [jnp.where(mask, low, jnp.zeros_like(low)) for low in lows]
            inner = [dot(part, each).astype(BF16) for part, each in zip(parts, known)]
            inverses = [
                inverse - dot(each, right)
                for inverse, each, right in zip(inverses, known, inner)
            ]
        level += 1
    lefts = [
        (eye - inverse - dot3(lower, inverse)).astype(BF16)
        for lower, inverse in zip(lowers, inverses)
    ]
    return [
        inverse + dot(inverse.astype(BF16), left) for inverse, left in zip(inverses, lefts)
    ]


def head_column(values, head):
    lane = lax.broadcasted_iota(jnp.int32, values.shape, 1)
    return jnp.sum(jnp.where(lane == head, values, 0.0), -1, keepdims=True)


def forward_group(
    step, xn_ref, wq_ref, wk_ref, wv_ref, wg_ref, wb_ref, conv_ref, gain_ref, wo_ref,
    mixed_ref, resid_ref, beta_ref, inv_ref, total,
):
    xn = xn_ref[...]
    rows = xn.shape[0]
    half = rows // 2

    @pl.when(step == 0)
    def _():
        beta_ref[...] = dot(xn, wb_ref[...], NT)
        total[...] = jnp.zeros_like(total)

    query_in = dot(xn, wq_ref[...])
    key_in = dot(xn, wk_ref[...])
    value_in = dot(xn, wv_ref[...])
    gate_in = dot(xn, wg_ref[...])
    for place, value in enumerate((query_in, key_in, value_in, gate_in)):
        resid_ref[place] = value
    beta_all = sigmoid(beta_ref[...])
    conv_q = causal_conv(query_in, conv_ref[0])
    conv_k = causal_conv(key_in, conv_ref[1])
    conv_v = causal_conv(value_in, conv_ref[2])
    query_act = conv_q * sigmoid(conv_q)
    key_act = conv_k * sigmoid(conv_k)
    value_act = conv_v * sigmoid(conv_v)
    gate_act = gate_in * sigmoid(gate_in)
    strict = tri_mask(rows, True)
    causal = tri_mask(rows, False)
    heads = []
    for head in range(GROUP // HEAD):
        cols = slice(head * HEAD, (head + 1) * HEAD)
        queries = query_act[:, cols]
        queries = queries * lax.rsqrt(jnp.sum(queries * queries, -1, keepdims=True) + unit_eps)
        queries = queries * HEAD**-0.5
        keys = key_act[:, cols]
        keys = keys * lax.rsqrt(jnp.sum(keys * keys, -1, keepdims=True) + unit_eps)
        beta = head_column(beta_all, GROUP // HEAD * step + head)
        lower = jnp.where(strict, dot3(keys, keys, NT) * beta, 0.0)
        scores = jnp.where(causal, dot3(queries, keys, NT), 0.0)
        heads.append((cols, lower, scores, value_act[:, cols] * beta))
    inverses = unit_lower_inverses(
        [lower[part, part] for _, lower, _, _ in heads for part in (slice(0, half), slice(half, rows))]
    )
    upper_u = [dot3(inverses[2 * n], weighted[:half]) for n, (_, _, _, weighted) in enumerate(heads)]
    rest = [
        weighted[half:] - dot3(lower[half:, :half], upper)
        for (_, lower, _, weighted), upper in zip(heads, upper_u)
    ]
    lower_u = [dot3(inverses[2 * n + 1], right) for n, right in enumerate(rest)]
    updates = [jnp.concatenate(pair, 0) for pair in zip(upper_u, lower_u)]
    outputs = [dot3(scores, update) for (_, _, scores, _), update in zip(heads, updates)]
    for head, (cols, _, _, _) in enumerate(heads):
        inv_ref[head, 0] = inverses[2 * head]
        inv_ref[head, 1] = inverses[2 * head + 1]
        resid_ref[4, :, cols] = updates[head]
        output = outputs[head]
        resid_ref[5, :, cols] = output
        normed = output * lax.rsqrt(jnp.mean(output * output, -1, keepdims=True) + norm_eps)
        mixed_ref[0, :, cols] = (normed * gain_ref[...] * gate_act[:, cols]).astype(BF16)
    total[...] += dot(mixed_ref[0], wo_ref[...])


def mixer_forward(
    xn_ref, wq_ref, wk_ref, wv_ref, wg_ref, wb_ref, conv_ref, gain_ref, wo_ref,
    mixed_ref, part_ref, resid_ref, beta_ref, inv_ref, total,
):
    step = pl.program_id(0)
    forward_group(
        step, xn_ref, wq_ref, wk_ref, wv_ref, wg_ref, wb_ref, conv_ref, gain_ref, wo_ref,
        mixed_ref, resid_ref, beta_ref, inv_ref, total,
    )

    @pl.when(step == pl.num_programs(0) - 1)
    def _():
        part_ref[...] = total[...].astype(BF16)


def call_mixer_forward(xn, wq, wk, wv, wg, wb, conv, gain, wo):
    rows, width = xn.shape
    cols = wq.shape[1]
    groups = cols // GROUP
    heads = wb.shape[0]
    whole = lambda *shape: pl.BlockSpec(shape, lambda i: (0,) * len(shape))
    weight = pl.BlockSpec((width, GROUP), lambda i: (0, i))
    return pl.pallas_call(
        mixer_forward,
        grid=(groups,),
        in_specs=[
            whole(rows, width), weight, weight, weight, weight, whole(heads, width),
            pl.BlockSpec((3, CONV, GROUP), lambda i: (0, 0, i)), whole(1, HEAD),
            pl.BlockSpec((GROUP, width), lambda i: (i, 0)),
        ],
        out_specs=[
            pl.BlockSpec((1, rows, GROUP), lambda i: (i // (groups // 2), 0, i % (groups // 2))),
            whole(rows, width), pl.BlockSpec((6, rows, GROUP), lambda i: (0, 0, i)), whole(rows, heads),
            pl.BlockSpec((GROUP // HEAD, 2, rows // 2, rows // 2), lambda i: (i, 0, 0, 0)),
        ],
        out_shape=[
            jax.ShapeDtypeStruct((2, rows, cols // 2), BF16),
            jax.ShapeDtypeStruct((rows, width), BF16),
            jax.ShapeDtypeStruct((6, rows, cols), F32), jax.ShapeDtypeStruct((rows, heads), F32),
            jax.ShapeDtypeStruct((heads, 2, rows // 2, rows // 2), F32),
        ],
        scratch_shapes=[pltpu.VMEM((rows, width), F32)],
        compiler_params=pltpu.CompilerParams(vmem_limit_bytes=VMEM_LIMIT),
        cost_estimate=pl.CostEstimate(
            flops=2 * rows * width * cols * 5 + 10**10, bytes_accessed=5 * width * cols * 2 + 10**7,
            transcendentals=0,
        ),
        name="mixer_forward",
    )(xn, wq, wk, wv, wg, wb, conv, gain, wo)


def silu_slope(value, sig):
    return sig * (1.0 + value * (1.0 - sig))


def backward_pair(
    step, steps, dh_ref, wq_ref, wk_ref, wv_ref, wg_ref, wb_ref, conv_ref, gain_ref, wo_ref,
    resid_ref, beta_ref, inv_ref, low_ref, bl_ref, dconv_ref, dgain_ref, total, beta_total,
):
    rows = dh_ref.shape[0]
    half = rows // 2

    @pl.when(step == 0)
    def _():
        total[...] = jnp.zeros_like(total)
        beta_total[...] = jnp.zeros_like(beta_total)
        dgain_ref[...] = jnp.zeros_like(dgain_ref)

    mixed_grad = dot(dh_ref[...], wo_ref[...], NT)
    query_in, key_in, value_in, gate_in = (resid_ref[place] for place in range(4))
    beta_all = sigmoid(beta_ref[...])
    lane = lax.broadcasted_iota(jnp.int32, beta_all.shape, 1)
    conv_q = causal_conv(query_in, conv_ref[0])
    conv_k = causal_conv(key_in, conv_ref[1])
    conv_v = causal_conv(value_in, conv_ref[2])
    sig_q, sig_k, sig_v = sigmoid(conv_q), sigmoid(conv_k), sigmoid(conv_v)
    sig_g = sigmoid(gate_in)
    query_act = conv_q * sig_q
    key_act = conv_k * sig_k
    value_act = conv_v * sig_v
    gate_act = gate_in * sig_g
    strict = tri_mask(rows, True)
    causal = tri_mask(rows, False)
    gain = gain_ref[...]
    both = range(2)
    cols = [slice(head * HEAD, (head + 1) * HEAD) for head in both]
    raw_q = [query_act[:, each] for each in cols]
    raw_k = [key_act[:, each] for each in cols]
    values = [value_act[:, each] for each in cols]
    scale_q = [lax.rsqrt(jnp.sum(each * each, -1, keepdims=True) + unit_eps) for each in raw_q]
    scale_k = [lax.rsqrt(jnp.sum(each * each, -1, keepdims=True) + unit_eps) for each in raw_k]
    queries = [raw_q[head] * scale_q[head] * HEAD**-0.5 for head in both]
    keys = [raw_k[head] * scale_k[head] for head in both]
    beta = [head_column(beta_all, 2 * step + head) for head in both]
    updates = [resid_ref[4, :, each] for each in cols]
    output = [resid_ref[5, :, each] for each in cols]
    upstream = [mixed_grad[:, each] for each in cols]
    scale_o = [lax.rsqrt(jnp.mean(each * each, -1, keepdims=True) + norm_eps) for each in output]
    unit_out = [output[head] * scale_o[head] for head in both]
    grads_g = [upstream[head] * (unit_out[head] * gain) for head in both]
    d_normed = [upstream[head] * gate_act[:, cols[head]] for head in both]
    for head in both:
        dgain_ref[...] += jnp.sum(d_normed[head] * unit_out[head], 0, keepdims=True)
    d_unit = [each * gain for each in d_normed]
    d_output = [
        scale_o[head]
        * (
            d_unit[head]
            - unit_out[head] * jnp.mean(d_unit[head] * unit_out[head], -1, keepdims=True)
        )
        for head in both
    ]
    inner = [dot3(each, each, NT) for each in keys]
    lower_21 = [inner[head][half:, :half] * beta[head][half:] for head in both]
    scores = [jnp.where(causal, dot3(queries[head], keys[head], NT), 0.0) for head in both]
    d_updates = [dot3(scores[head], d_output[head], TN) for head in both]
    d_right_2 = [dot3(inv_ref[head, 1], d_updates[head][half:], TN) for head in both]
    d_upper = [
        d_updates[head][:half] - dot3(lower_21[head], d_right_2[head], TN) for head in both
    ]
    d_right_1 = [dot3(inv_ref[head, 0], d_upper[head], TN) for head in both]
    d_right = [jnp.concatenate([d_right_1[head], d_right_2[head]], 0) for head in both]
    d_scores = [jnp.where(causal, dot3(d_output[head], updates[head], NT), 0.0) for head in both]
    d_lower = [jnp.where(strict, -dot3(d_right[head], updates[head], NT), 0.0) for head in both]
    d_inner = [d_lower[head] * beta[head] for head in both]
    d_queries = [dot3(d_scores[head], keys[head]) * HEAD**-0.5 for head in both]
    d_keys = [
        dot3(d_scores[head], queries[head], TN)
        + dot3(d_inner[head], keys[head])
        + dot3(d_inner[head], keys[head], TN)
        for head in both
    ]
    grads_v = [d_right[head] * beta[head] for head in both]
    unit_back = lambda grad, raw, scale: scale * (
        grad - raw * (scale * scale) * jnp.sum(grad * raw, -1, keepdims=True)
    )
    grads_q = [unit_back(d_queries[head], raw_q[head], scale_q[head]) for head in both]
    grads_k = [unit_back(d_keys[head], raw_k[head], scale_k[head]) for head in both]
    for head in both:
        d_beta = jnp.sum(d_lower[head] * inner[head], -1, keepdims=True) + jnp.sum(
            d_right[head] * values[head], -1, keepdims=True
        )
        d_beta_in = d_beta * beta[head] * (1.0 - beta[head])
        beta_total[...] += jnp.where(lane == 2 * step + head, d_beta_in, 0.0)
    for kind, (grads, pre, conv, sig) in enumerate(
        (
            (grads_q, query_in, conv_q, sig_q),
            (grads_k, key_in, conv_k, sig_k),
            (grads_v, value_in, conv_v, sig_v),
        )
    ):
        d_conv = jnp.concatenate(grads, 1) * silu_slope(conv, sig)
        taps = conv_ref[kind]
        d_pre = d_conv * taps[CONV - 1 : CONV]
        for offset in range(CONV):
            shift = CONV - 1 - offset
            dconv_ref[kind, offset : offset + 1, :] = jnp.sum(
                d_conv * rows_down(pre, shift), 0, keepdims=True
            )
            if shift:
                d_pre = d_pre + rows_up(d_conv, shift) * taps[offset : offset + 1]
        low_ref[0, kind] = d_pre.astype(BF16)
    low_ref[0, 3] = (jnp.concatenate(grads_g, 1) * silu_slope(gate_in, sig_g)).astype(BF16)
    total[...] += (
        dot(low_ref[0, 0], wq_ref[...], NT)
        + dot(low_ref[0, 1], wk_ref[...], NT)
        + dot(low_ref[0, 2], wv_ref[...], NT)
        + dot(low_ref[0, 3], wg_ref[...], NT)
    )

    @pl.when(step == steps - 1)
    def _():
        bl_ref[...] = beta_total[...].astype(BF16)
        total[...] += dot(bl_ref[...], wb_ref[...])


def mixer_backward(
    dh_ref, wq_ref, wk_ref, wv_ref, wg_ref, wb_ref, conv_ref, gain_ref, wo_ref,
    resid_ref, beta_ref, inv_ref, low_ref, bl_ref, part_ref, dconv_ref, dgain_ref,
    total, beta_total,
):
    step, steps = pl.program_id(0), pl.num_programs(0)
    backward_pair(
        step, steps, dh_ref, wq_ref, wk_ref, wv_ref, wg_ref, wb_ref, conv_ref, gain_ref, wo_ref,
        resid_ref, beta_ref, inv_ref, low_ref, bl_ref, dconv_ref, dgain_ref, total, beta_total,
    )

    @pl.when(step == steps - 1)
    def _():
        part_ref[...] = total[...].astype(BF16)


def call_mixer_backward(dh, wq, wk, wv, wg, wb, conv, gain, wo, resid, beta, inv):
    rows, width = dh.shape
    cols = wq.shape[1]
    pairs = cols // PAIR
    heads = wb.shape[0]
    whole = lambda *shape: pl.BlockSpec(shape, lambda i: (0,) * len(shape))
    weight = pl.BlockSpec((width, PAIR), lambda i: (0, i))
    taps = pl.BlockSpec((3, CONV, PAIR), lambda i: (0, 0, i))
    return pl.pallas_call(
        mixer_backward,
        grid=(pairs,),
        in_specs=[
            whole(rows, width), weight, weight, weight, weight, whole(heads, width), taps,
            whole(1, HEAD), pl.BlockSpec((PAIR, width), lambda i: (i, 0)),
            pl.BlockSpec((6, rows, PAIR), lambda i: (0, 0, i)), whole(rows, heads),
            pl.BlockSpec((2, 2, rows // 2, rows // 2), lambda i: (i, 0, 0, 0)),
        ],
        out_specs=[
            pl.BlockSpec((1, 4, rows, PAIR), lambda i: (i // (pairs // 2), 0, 0, i % (pairs // 2))),
            whole(rows, heads), whole(rows, width), taps, whole(1, HEAD),
        ],
        out_shape=[
            jax.ShapeDtypeStruct((2, 4, rows, cols // 2), BF16),
            jax.ShapeDtypeStruct((rows, heads), BF16),
            jax.ShapeDtypeStruct((rows, width), BF16), jax.ShapeDtypeStruct(conv.shape, F32),
            jax.ShapeDtypeStruct((1, HEAD), F32),
        ],
        scratch_shapes=[pltpu.VMEM((rows, width), F32), pltpu.VMEM((rows, heads), F32)],
        compiler_params=pltpu.CompilerParams(vmem_limit_bytes=VMEM_LIMIT),
        cost_estimate=pl.CostEstimate(
            flops=2 * rows * width * cols * 5 + 2 * 10**10,
            bytes_accessed=5 * width * cols * 2 + 10**7,
            transcendentals=0,
        ),
        name="mixer_backward",
    )(dh, wq, wk, wv, wg, wb, conv, gain, wo, resid, beta, inv)


def mlp_copies(index, slot, wg_ref, wu_ref, wd_ref, wg_buf, wu_buf, wd_buf, sems):
    hidden = wg_ref.shape[1] // 2
    for part in range(2):
        start = pl.multiple_of(part * hidden + index * HEAD, HEAD)
        lanes = pl.ds(part * HEAD, HEAD)
        yield pltpu.make_async_copy(
            wg_ref.at[:, pl.ds(start, HEAD)], wg_buf.at[slot, :, lanes], sems.at[slot, part]
        )
        yield pltpu.make_async_copy(
            wu_ref.at[:, pl.ds(start, HEAD)], wu_buf.at[slot, :, lanes], sems.at[slot, 2 + part]
        )
        yield pltpu.make_async_copy(
            wd_ref.at[pl.ds(start, HEAD), :], wd_buf.at[slot, lanes, :], sems.at[slot, 4 + part]
        )


def mlp_tile(step, steps, yn_ref, dy_ref, weights, low_store, down_total, back_total):
    wg_ref, wu_ref, wd_ref, wg_buf, wu_buf, wd_buf, sems = weights
    slot = lax.rem(step, 2)

    @pl.when(step == 0)
    def _():
        down_total[...] = jnp.zeros_like(down_total)
        back_total[...] = jnp.zeros_like(back_total)

    @pl.when(step + 1 < steps)
    def _():
        for copy in mlp_copies(step + 1, 1 - slot, *weights):
            copy.start()

    for copy in mlp_copies(step, slot, *weights):
        copy.wait()
    yn, dy = yn_ref[...], dy_ref[...]
    w_gate, w_up, w_down = wg_buf[slot], wu_buf[slot], wd_buf[slot]
    gate = dot(yn, w_gate)
    up = dot(yn, w_up)
    d_product = dot(dy, w_down, NT)
    sig = sigmoid(gate)
    act = gate * sig
    product = (act * up).astype(BF16)
    gate_grad = (d_product * up * silu_slope(gate, sig)).astype(BF16)
    up_grad = (d_product * act).astype(BF16)
    down_total[...] += dot(product, w_down)
    back_total[...] += dot(gate_grad, w_gate, NT) + dot(up_grad, w_up, NT)
    for kind, value in enumerate((product, gate_grad, up_grad)):
        low_store(0, kind, value[:, :HEAD])
        low_store(1, kind, value[:, HEAD:])


def mlp_kernel(
    yn_ref, dy_ref, wg_ref, wu_ref, wd_ref, low_ref, down_ref, back_ref,
    wg_buf, wu_buf, wd_buf, down_total, back_total, sems,
):
    step, steps = pl.program_id(0), pl.num_programs(0)
    weights = (wg_ref, wu_ref, wd_ref, wg_buf, wu_buf, wd_buf, sems)

    @pl.when(step == 0)
    def _():
        for copy in mlp_copies(0, 0, *weights):
            copy.start()

    def low_store(half, kind, value):
        low_ref[half, kind] = value

    mlp_tile(step, steps, yn_ref, dy_ref, weights, low_store, down_total, back_total)

    @pl.when(step == steps - 1)
    def _():
        down_ref[...] = down_total[...].astype(BF16)
        back_ref[...] = back_total[...].astype(BF16)


def call_mlp(yn, dy, w_gate, w_up, w_down):
    rows, width = yn.shape
    hidden = w_gate.shape[1] // 2
    whole = lambda *shape: pl.BlockSpec(shape, lambda i: (0,) * len(shape))
    anywhere = pl.BlockSpec(memory_space=pl.ANY)
    tile = pl.BlockSpec((2, 3, rows, HEAD), lambda i: (0, 0, 0, i))
    return pl.pallas_call(
        mlp_kernel,
        grid=(hidden // HEAD,),
        in_specs=[whole(rows, width), whole(rows, width), anywhere, anywhere, anywhere],
        out_specs=[tile, whole(rows, width), whole(rows, width)],
        out_shape=[
            jax.ShapeDtypeStruct((2, 3, rows, hidden), BF16),
            jax.ShapeDtypeStruct((rows, width), BF16),
            jax.ShapeDtypeStruct((rows, width), BF16),
        ],
        scratch_shapes=[
            pltpu.VMEM((2, width, PAIR), BF16), pltpu.VMEM((2, width, PAIR), BF16),
            pltpu.VMEM((2, PAIR, width), BF16), pltpu.VMEM((rows, width), F32),
            pltpu.VMEM((rows, width), F32), pltpu.SemaphoreType.DMA((2, 6)),
        ],
        compiler_params=pltpu.CompilerParams(vmem_limit_bytes=VMEM_LIMIT),
        cost_estimate=pl.CostEstimate(
            flops=12 * rows * width * w_gate.shape[1], bytes_accessed=6 * width * w_gate.shape[1],
            transcendentals=0,
        ),
        name="mlp",
    )(yn, dy, w_gate, w_up, w_down)


def norm_back(upstream, inputs, scale_rows, gain_row):
    scaled_grad = upstream * gain_row
    return scale_rows * (
        scaled_grad
        - inputs * scale_rows * scale_rows * jnp.mean(scaled_grad * inputs, -1, keepdims=True)
    )


def take(value, axis, index):
    return lax.dynamic_index_in_dim(value, index, axis, keepdims=False)


def sibling(value):
    return lax.ppermute(value, "tensor", [(0, 1), (1, 0)])


def both_rows(mine, other, core):
    axis = mine.ndim - 2
    return jnp.where(
        core == 0, jnp.concatenate([mine, other], axis), jnp.concatenate([other, mine], axis)
    )


def swap_sum(partial, core):
    parts = partial.reshape(2, -1, partial.shape[-1])
    received = sibling(take(parts, 0, 1 - core))
    return take(parts, 0, core).astype(F32) + received.astype(F32)


BIT_X, BIT_Y, BIT_ZA, BIT_ZB = 1, 2, 4, 8
GATHER_2 = BIT_ZA
BITS = (1, 2, 4, 8)
SMALL_STAGES = ((1, 1, True), (2, 1, True), (4, 4, True), (8, 4, True), (1, 4, False), (2, 2, False))
CHIPS = 16
MESH = pl.DeviceIdType.MESH
KINDS = ((0, 0, 0), (0, 1, 2), (0, 2, 2), (1, 0, 3), (1, 1, 1), (1, 2, 1), (1, 3, 1), (1, 4, 1))
COUNT = len(KINDS)
CROSSED = (0, 3)
GATHER_1 = (BIT_Y, BIT_Y, BIT_X, BIT_Y)
REDUCE_1 = tuple(BIT_X + BIT_Y - bit for bit in GATHER_1)
LEFT_SLOT = (0, 0, 2, 1)
SMALL_ROWS = 24
FIRST_STEPS = (
    830,
)
TILE_STEPS = {2: (1100,), 3: (130,), 5: (10, 20, 810, 0,), 8: (800,)}
LAST_TILE_STEPS = (
    811, 1, 21, 11, 801, 30,
)
PAIR_STEPS = {0: (110,), 1: (1200, 1101, 101, 821, 100, 820,), 2: (111, 1201,)}
SCHEDULE = (
    230, 40, 850, 50, 200, 60, 901, 231, 330, 201, 840, 630,
    210, 211, 631, 870, 300, 140, 860, 310, 600, 120, 701, 121,
    900, 150, 601, 301, 331, 731, 70, 730, 430, 220, 700, 170,
    250, 610, 240, 900, 400, 711, 611, 221, 241, 340, 160, 710,
    251, 350, 351, 640, 270, 900, 271, 341, 320, 641, 311, 410,
    720, 721, 620, 900, 621, 510, 321, 751, 651, 750, 530, 650,
    370, 260, 741, 261, 670, 900, 360, 660, 740, 420, 770, 450,
    520, 771, 671, 900, 550, 661, 440, 760, 761, 900, 371, 470,
    500, 540, 361, 460, 570, 560,
)


def block_place(block, left):
    bit = lambda mask: int((block & mask) != 0)
    return bit(GATHER_1[left]), bit(REDUCE_1[left]) * 4 + bit(BIT_ZB) * 2 + bit(GATHER_2)


class Place:
    def __init__(self, tokens):
        self.chip, self.core = lax.axis_index("dp"), lax.axis_index("tensor")
        self.bit = {mask: lax.rem(self.chip // mask, 2) for mask in BITS}
        step = {mask: mask * (1 - 2 * self.bit[mask]) for mask in BITS}
        self.to = {mask: (self.chip + step[mask], self.core) for mask in BITS}
        self.mirror = (self.chip + step[BIT_ZA] + step[BIT_ZB], self.core)
        self.near = (self.chip, 1 - self.core)
        self.own_rows = pl.ds(pl.multiple_of(self.core * tokens, tokens), tokens)
        self.other_rows = pl.ds(pl.multiple_of((1 - self.core) * tokens, tokens), tokens)
        self.tokens = tokens

    def greet(self, partners):
        barrier = pltpu.get_barrier_semaphore()
        for target in partners:
            pl.semaphore_signal(barrier, inc=1, device_id=target, device_id_type=MESH)
        pl.semaphore_wait(barrier, len(partners))


def remote_pair(source, target, send_sem, recv_sem, device):
    return pltpu.make_async_remote_copy(
        src_ref=source, dst_ref=target, send_sem=send_sem, recv_sem=recv_sem,
        device_id=device, device_id_type=MESH,
    )


def remote(source, target, sems, index, device):
    return remote_pair(source, target, sems.at[(0, *index)], sems.at[(1, *index)], device)


class Lefts:
    def __init__(self, lefts, place, own, landed, sems, local_sems):
        self.place, self.own, self.landed, self.sems, self.local = place, own, landed, sems, local_sems
        self.lefts = lefts

    def rows(self, a, piece):
        tokens = self.place.tokens
        start = pl.multiple_of((2 * piece + self.place.core) * tokens, tokens)
        return self.landed.at[a, pl.ds(start, tokens), :]

    def copy(self, a, name):
        place, own, sems = self.place, self.own, self.sems
        first = GATHER_1[self.lefts[a]]
        half = place.bit[first]
        if name == "one":
            return remote(own.at[a, 1 - half], self.rows(a, 1), sems, (a, 0), place.to[first])
        if name == "two":
            return remote(own.at[a, half], self.rows(a, 2), sems, (a, 1), place.to[GATHER_2])
        if name == "far":
            return remote(self.rows(a, 1), self.rows(a, 3), sems, (a, 2), place.to[GATHER_2])
        if name == 0:
            return remote(own.at[a, half], self.rows(a, 0), sems, (a, 3), place.near)
        return remote(self.rows(a, name), self.rows(a, name), sems, (a, 3 + name), place.near)

    def own_copy(self, a):
        half = self.place.bit[GATHER_1[self.lefts[a]]]
        return pltpu.make_async_copy(self.own.at[a, half], self.rows(a, 0), self.local.at[a])

    def start(self, a, natural):
        for block in range(CHIPS):
            half, place = block_place(block, self.lefts[a])
            self.own[a, half, :, place * HEAD : (place + 1) * HEAD] = natural[
                :, block * HEAD : (block + 1) * HEAD
            ]
        for name in ("one", "two", 0):
            self.copy(a, name).start()
        self.own_copy(a).start()

    def middle(self, a):
        self.copy(a, "one").wait_recv()
        self.copy(a, "far").start()
        self.copy(a, 1).start()
        self.copy(a, "two").wait_recv()
        self.copy(a, 2).start()

    def far(self, a):
        self.copy(a, "far").wait_recv()
        self.copy(a, 3).start()

    def arrived(self, a):
        for piece in range(4):
            self.copy(a, piece).wait_recv()
        self.own_copy(a).wait()

    def sent(self, a):
        for name in ("one", "two", "far", 0, 1, 2, 3):
            self.copy(a, name).wait_send()


def front_kernel(
    tokens_ref, cot_ref, wq_ref, wk_ref, wv_ref, wg_ref, wb_ref, conv_ref, gain_ref, wo_ref,
    norm1_ref, norm2_ref,
    mixed_ref, resid_ref, beta_ref, inv_ref, hidden_ref, second_ref, xn_out, dy_out, yn_out,
    landed,
    total, xn, dy, yn, own, stage, part, wbuf, wobuf, lsem, qsem, csem, wsem,
):
    step, steps = pl.program_id(0), pl.num_programs(0)
    place = Place(tokens_ref.shape[0])
    own_rows, other_rows = place.own_rows, place.other_rows
    lefts = Lefts((0, 1), place, own, landed, lsem, csem)

    def row_copy(index):
        source = stage if index == 2 else (xn, dy, None, yn)[index].at[own_rows, :]
        target = part if index == 2 else source
        return remote(source, target, qsem, (index,), place.near)

    def out_copy(index):
        source, target = ((xn, xn_out), (dy, dy_out), (yn, yn_out))[index]
        return pltpu.make_async_copy(source, target, csem.at[2 + index])

    def weight_copies(group):
        columns = pl.ds(pl.multiple_of(group * GROUP, GROUP), GROUP)
        for index, weight in enumerate((wq_ref, wk_ref, wv_ref, wg_ref)):
            yield pltpu.make_async_copy(
                weight.at[:, columns], wbuf.at[group, index], wsem.at[group, index]
            )
        yield pltpu.make_async_copy(wo_ref.at[columns, :], wobuf.at[group], wsem.at[group, 4])

    @pl.when(step == 0)
    def _():
        for group in range(wbuf.shape[0]):
            for copy in weight_copies(group):
                copy.start()
        place.greet((place.to[BIT_X], place.to[BIT_Y], place.to[GATHER_2], place.near))
        inputs = tokens_ref[...].astype(F32)
        scale = lax.rsqrt(jnp.mean(inputs * inputs, -1, keepdims=True) + norm_eps)
        xn[own_rows, :] = (inputs * scale * norm1_ref[...]).astype(BF16)
        row_copy(0).start()
        dy[own_rows, :] = cot_ref[...]
        row_copy(1).start()
        lefts.start(0, cot_ref)
        lefts.start(1, xn[own_rows, :])
        row_copy(0).wait()
        out_copy(0).start()

    for copy in weight_copies(step):
        copy.wait()
    forward_group(
        step, xn, *(wbuf.at[step, index] for index in range(4)), wb_ref, conv_ref, gain_ref,
        wobuf.at[step], mixed_ref, resid_ref, beta_ref, inv_ref, total,
    )

    @pl.when(step == 0)
    def _():
        row_copy(1).wait()
        out_copy(1).start()
        lefts.middle(0)
        lefts.middle(1)

    @pl.when(step == steps - 1)
    def _():
        stage[...] = total[other_rows, :].astype(BF16)
        row_copy(2).start()
        lefts.far(0)
        lefts.far(1)
        hidden = tokens_ref[...].astype(F32) + total[own_rows, :]
        row_copy(2).wait()
        hidden = hidden + part[...].astype(F32)
        hidden_ref[...] = hidden
        scale = lax.rsqrt(jnp.mean(hidden * hidden, -1, keepdims=True) + norm_eps)
        second = (hidden * scale * norm2_ref[...]).astype(BF16)
        yn[own_rows, :] = second
        row_copy(3).start()
        second_ref[...] = second
        for a in range(2):
            lefts.arrived(a)
            lefts.sent(a)
        row_copy(3).wait()
        out_copy(2).start()
        for index in range(3):
            out_copy(index).wait()


def call_front(tokens, cot, wq, wk, wv, wg, wb, conv, gain, wo, norm1, norm2):
    count, width = tokens.shape
    rows, cols, heads = 2 * count, wq.shape[1], wb.shape[0]
    groups = cols // GROUP
    sds = jax.ShapeDtypeStruct
    whole = lambda *shape: pl.BlockSpec(shape, lambda i: (0,) * len(shape))
    anywhere = pl.BlockSpec(memory_space=pl.ANY)
    sem = pltpu.SemaphoreType.DMA
    low = lambda *shape: pltpu.VMEM(shape, BF16)
    return pl.pallas_call(
        front_kernel,
        grid=(groups,),
        in_specs=[
            whole(count, width), whole(count, width), anywhere, anywhere, anywhere, anywhere,
            whole(heads, width), pl.BlockSpec((3, CONV, GROUP), lambda i: (0, 0, i)),
            whole(1, HEAD), anywhere, whole(1, width), whole(1, width),
        ],
        out_specs=[
            pl.BlockSpec((1, rows, GROUP), lambda i: (i // (groups // 2), 0, i % (groups // 2))),
            pl.BlockSpec((6, rows, GROUP), lambda i: (0, 0, i)), whole(rows, heads),
            pl.BlockSpec((GROUP // HEAD, 2, count, count), lambda i: (i, 0, 0, 0)),
            whole(count, width), whole(count, width), anywhere, anywhere, anywhere, anywhere,
        ],
        out_shape=[
            sds((2, rows, cols // 2), BF16), sds((6, rows, cols), F32), sds((rows, heads), F32),
            sds((heads, 2, count, count), F32), sds((count, width), F32),
            sds((count, width), BF16), sds((rows, width), BF16), sds((rows, width), BF16),
            sds((rows, width), BF16), sds((2, 8 * count, width // 2), BF16),
        ],
        scratch_shapes=[
            pltpu.VMEM((rows, width), F32), low(rows, width), low(rows, width), low(rows, width),
            low(2, 2, count, width // 2), low(count, width), low(count, width),
            low(groups, 4, width, GROUP), low(groups, GROUP, width),
            sem((2, 2, 7)), sem((2, 4)), sem((5,)), sem((groups, 5)),
        ],
        compiler_params=pltpu.CompilerParams(
            vmem_limit_bytes=VMEM_LIMIT, collective_id=2, has_side_effects=True
        ),
        cost_estimate=pl.CostEstimate(flops=2 * 10**10, bytes_accessed=4 * 10**7, transcendentals=0),
        name="front",
    )(tokens, cot, wq, wk, wv, wg, wb, conv, gain, wo, norm1, norm2)


class Refs(typing.NamedTuple):
    hidden: typing.Any
    tokens: typing.Any
    cot: typing.Any
    second: typing.Any
    wb: typing.Any
    conv: typing.Any
    gain: typing.Any
    beta: typing.Any
    norm1: typing.Any
    norm2: typing.Any
    early: typing.Any
    yn: typing.Any
    dy: typing.Any
    xn: typing.Any
    wg: typing.Any
    wu: typing.Any
    wd: typing.Any
    wq: typing.Any
    wk: typing.Any
    wv: typing.Any
    wgo: typing.Any
    wo: typing.Any
    mixed: typing.Any
    resid: typing.Any
    inv: typing.Any
    out: typing.Any
    ingrad: typing.Any
    smalls: typing.Any
    lefts: typing.Any
    gws: typing.Any
    gns: typing.Any
    lows: typing.Any
    paw: typing.Any
    pan: typing.Any
    pbw: typing.Any
    pbn: typing.Any
    own: typing.Any
    wide: typing.Any
    r1w: typing.Any
    r1n: typing.Any
    r2w: typing.Any
    r2n: typing.Any
    rfw: typing.Any
    rfn: typing.Any
    rows: typing.Any
    dh: typing.Any
    state: typing.Any
    small: typing.Any
    first: typing.Any
    smallr: typing.Any
    dconv: typing.Any
    dgain: typing.Any
    bl: typing.Any
    lsem: typing.Any
    rsem: typing.Any
    csem: typing.Any
    qsem: typing.Any
    ssem: typing.Any
    zsem: typing.Any
    fsem: typing.Any
    psem: typing.Any
    msem: typing.Any
    osem: typing.Any


def block_kernel(*refs):
    outs = refs[28 : 28 + COUNT]
    r = Refs(*refs[:28], *refs[28 + COUNT :])
    own, wide, dh, state, small = r.own, r.wide, r.dh, r.state, r.small
    recv1, recv2, recvf = (r.r1w, r.r1n), (r.r2w, r.r2n), (r.rfw, r.rfn)
    landed = (r.gws, r.gns)
    relay = ((r.paw, r.pan), (r.pbw, r.pbn))
    tokens, width = r.second.shape
    place = Place(tokens)
    bit, to, near = place.bit, place.to, place.near
    own_rows, other_rows = place.own_rows, place.other_rows
    quarter, eighth = width // 8, width // 16
    half2, mine2 = bit[GATHER_2], bit[BIT_ZB]
    end = bit[BIT_ZA] == bit[BIT_ZB]
    inner = bit[BIT_ZA] != bit[BIT_ZB]
    place.greet((*to.values(), place.mirror, near))
    lefts = Lefts((2, 3), place, own, r.lefts, r.lsem, r.csem)

    def source(kind, half):
        group, place, _ = KINDS[kind]
        if group == 0:
            return wide.at[half, place]
        return r.mixed.at[half] if place == 0 else r.lows.at[half, place - 1]

    def right_landed(kind, piece):
        group, place, _ = KINDS[kind]
        return landed[group].at[place, piece - 1]

    split = wide.shape[-1] // HEAD // 2 * HEAD + HEAD

    def parts(kind):
        return 2 if KINDS[kind][0] == 0 else 1

    def right_copy(kind, name, part):
        columns = slice(None)
        if parts(kind) == 2:
            columns = slice(0, split) if part == 0 else slice(split, wide.shape[-1])
        view = lambda ref: ref.at[:, columns]
        if name == "one":
            return remote(
                view(source(kind, half2)), view(right_landed(kind, 1)), r.rsem, (kind, 0, part),
                to[GATHER_1[KINDS[kind][2]]],
            )
        if name == "two":
            return remote(
                view(source(kind, 1 - half2)), view(right_landed(kind, 2)), r.rsem,
                (kind, 1, part), to[GATHER_2],
            )
        return remote(
            view(right_landed(kind, 2)), view(right_landed(kind, 3)), r.rsem, (kind, 2, part),
            to[GATHER_1[KINDS[kind][2]]],
        )

    def one(kind, part):
        right_copy(kind, "one", part).start()

    def two(kind, part):
        right_copy(kind, "two", part).start()

    def far(kind, part):
        right_copy(kind, "two", part).wait_recv()
        right_copy(kind, "far", part).start()

    def run(items, actions):
        for item in items:
            digits = (item % 10,) if item >= 1000 else (item // 10 % 10, item % 10)
            actions[item // 100](*digits)

    copy_actions = {0: one, 1: far, 8: two, 11: lefts.middle, 12: lefts.far}

    def run_at(step, table):
        for when, items in table.items():

            @pl.when(step == when)
            def _(items=items):
                run(items, copy_actions)

    def row_copy(index, source_ref):
        target = dh.at[own_rows, :] if index == 3 else r.rows.at[index]
        return remote(source_ref, target, r.qsem, (index,), near)

    def small_lanes(split, flip):
        index = {1: 0, 2: bit[BIT_Y], 4: 2 * bit[BIT_Y] + bit[BIT_X]}[split]
        if flip:
            index = {2: 1 - index, 4: index + 1 - 2 * bit[BIT_X]}[split]
        return pl.ds(pl.multiple_of(index * (width // split), HEAD), width // split)

    def small_copy(stage):
        target = r.smallr.at[stage]
        if stage == len(SMALL_STAGES):
            return remote(
                small.at[SMALL_ROWS - 8 :, :], target.at[:8, :], r.psem, (stage,), near
            )
        mask, split, _ = SMALL_STAGES[stage]
        lanes = small_lanes(split, False)
        return remote(small.at[:, lanes], target.at[:, lanes], r.psem, (stage,), to[mask])

    def small_sum(stage):
        small_copy(stage).wait()
        if stage == len(SMALL_STAGES):
            small[SMALL_ROWS - 8 :, :] += r.smallr[stage, :8, :]
            return
        _, split, add = SMALL_STAGES[stage]
        lanes = small_lanes(split, not add)
        if add:
            small[:, lanes] += r.smallr[stage, :, lanes]
        else:
            small[:, lanes] = r.smallr[stage, :, lanes]

    steps = wide.shape[-1] // HEAD
    pairs = r.wq.shape[1] // PAIR

    def mixer_copies(pair, slot, wbuf, wobuf, resid_buf, inv_buf):
        columns = pl.ds(pl.multiple_of(pair * PAIR, PAIR), PAIR)
        sems = r.msem
        for index, weight in enumerate((r.wq, r.wk, r.wv, r.wgo)):
            yield pltpu.make_async_copy(
                weight.at[:, columns], wbuf.at[slot, index], sems.at[slot, index]
            )
        yield pltpu.make_async_copy(r.wo.at[columns, :], wobuf.at[slot], sems.at[slot, 4])
        yield pltpu.make_async_copy(
            r.resid.at[:, :, columns], resid_buf.at[slot], sems.at[slot, 5]
        )
        yield pltpu.make_async_copy(
            r.inv.at[pl.ds(2 * pair, 2)], inv_buf.at[slot], sems.at[slot, 6]
        )

    def mlp_phase(prefetch, yn, dy, wg_buf, wu_buf, wd_buf, down_total, back_total, stage):
        weights = (r.wg, r.wu, r.wd, wg_buf, wu_buf, wd_buf, r.msem)
        loads = [
            pltpu.make_async_copy(r.yn, yn, r.csem.at[4]),
            pltpu.make_async_copy(r.dy, dy, r.csem.at[5]),
        ]
        for copy in (*loads, *mlp_copies(0, 0, *weights)):
            copy.start()
        lefts.start(0, r.second)
        run(FIRST_STEPS, copy_actions)
        for copy in loads:
            copy.wait()

        @pl.loop(0, steps)
        def _(step):
            columns = pl.ds(pl.multiple_of(step * HEAD, HEAD), HEAD)

            def low_store(half, kind, value):
                wide[half, kind, :, columns] = value

            mlp_tile(step, steps, yn, dy, weights, low_store, down_total, back_total)
            run_at(step, TILE_STEPS)

        run(LAST_TILE_STEPS, copy_actions)
        prefetch()
        for index, total in enumerate((down_total, back_total)):
            stage[index] = total[other_rows, :].astype(BF16)
            row_copy(index, stage.at[index]).start()
        for index in range(2):
            row_copy(index, stage.at[index]).wait()
        hidden = r.hidden[...]
        r.out[...] = (hidden + down_total[own_rows, :] + r.rows[0].astype(F32)).astype(BF16)
        second_grad = back_total[own_rows, :] + r.rows[1].astype(F32)
        scale = lax.rsqrt(jnp.mean(hidden * hidden, -1, keepdims=True) + norm_eps)
        small[...] = jnp.zeros_like(small)
        small[17:18, :] = jnp.sum(second_grad * hidden * scale, 0, keepdims=True)
        grad = r.cot[...].astype(F32) + norm_back(second_grad, hidden, scale, r.norm2[...])
        state[...] = grad
        dh[own_rows, :] = grad.astype(BF16)
        row_copy(3, dh.at[own_rows, :]).start()
        lefts.start(1, dh[own_rows, :])
        row_copy(3, dh.at[own_rows, :]).wait()

    def mixer_phase(buffers, xn, total, beta_total, low_stage):
        wbuf, wobuf, resid_buf, inv_buf = buffers
        load = pltpu.make_async_copy(r.xn, xn, r.csem.at[6])
        load.start()

        def low_copy(pair, slot):
            target = r.lows.at[
                pair // 2, :, :, pl.ds(pl.multiple_of(lax.rem(pair, 2) * PAIR, PAIR), PAIR)
            ]
            return pltpu.make_async_copy(low_stage.at[slot, 0], target, r.osem.at[slot])

        @pl.loop(0, pairs)
        def _(pair):
            slot = lax.rem(pair, 2)

            @pl.when(pair + 1 < pairs)
            def _():
                for copy in mixer_copies(pair + 1, 1 - slot, *buffers):
                    copy.start()

            for copy in mixer_copies(pair, slot, *buffers):
                copy.wait()

            @pl.when(pair >= 2)
            def _():
                low_copy(pair - 2, slot).wait()

            lanes = pl.ds(pl.multiple_of(pair * PAIR, PAIR), PAIR)
            backward_pair(
                pair, pairs, dh, *(wbuf.at[slot, index] for index in range(4)), r.wb,
                r.conv.at[:, :, lanes], r.gain, wobuf.at[slot], resid_buf.at[slot],
                r.beta, inv_buf.at[slot], low_stage.at[slot], r.bl,
                r.dconv.at[:, :, lanes], r.dgain, total, beta_total,
            )
            low_copy(pair, slot).start()
            run_at(pair, PAIR_STEPS)

        for pair in (pairs - 2, pairs - 1):
            low_copy(pair, pair % 2).wait()
        r.rows[0] = total[other_rows, :].astype(BF16)
        row_copy(2, r.rows.at[0]).start()
        r.first[...] = total[own_rows, :]
        load.wait()
        small[0:8, :] = dot(r.bl[...], xn[...], TN)

    def first_norm_back():
        for kind in range(3):
            for offset in range(CONV):
                row = kind * CONV + offset
                lanes = slice(0, width // 2) if row < 8 else slice(width // 2, width)
                small[8 + row % 8 : 9 + row % 8, lanes] = r.dconv[kind, offset : offset + 1, :]
        small[18:19, :HEAD] = r.dgain[...]
        row_copy(2, r.rows.at[0]).wait()
        first_grad = r.first[...] + r.rows[2].astype(F32)
        inputs = r.tokens[...].astype(F32)
        scale = lax.rsqrt(jnp.mean(inputs * inputs, -1, keepdims=True) + norm_eps)
        small[16:17, :] = jnp.sum(first_grad * inputs * scale, 0, keepdims=True)
        small_copy(0).start()
        state[...] += norm_back(first_grad, inputs, scale, r.norm1[...])
        pltpu.make_async_copy(state, r.ingrad, r.csem.at[7]).start()

    def scoped_mixer(wbuf, wobuf, resid_buf, inv_buf):
        buffers = (wbuf, wobuf, resid_buf, inv_buf)

        def prefetch():
            for copy in mixer_copies(0, 0, *buffers):
                copy.start()

        rows = 2 * tokens
        pl.run_scoped(
            functools.partial(mlp_phase, prefetch),
            pltpu.VMEM((rows, width), BF16), pltpu.VMEM((rows, width), BF16),
            pltpu.VMEM((2, width, PAIR), BF16), pltpu.VMEM((2, width, PAIR), BF16),
            pltpu.VMEM((2, PAIR, width), BF16), pltpu.VMEM((rows, width), F32),
            pltpu.VMEM((rows, width), F32), pltpu.VMEM((2, tokens, width), BF16),
        )
        pl.run_scoped(
            functools.partial(mixer_phase, buffers),
            pltpu.VMEM((rows, width), BF16), pltpu.VMEM((rows, width), F32),
            pltpu.VMEM(r.beta.shape, F32), pltpu.VMEM((2, 1, 4, rows, PAIR), BF16),
        )

    pl.run_scoped(
        scoped_mixer, pltpu.VMEM((2, 4, width, PAIR), BF16), pltpu.VMEM((2, PAIR, width), BF16),
        pltpu.VMEM((2, 6, 2 * tokens, PAIR), F32), pltpu.VMEM((2, 2, 2, tokens, tokens), F32),
    )

    def sums_phase(left, gw, gn, s1w, s1n, s2w, s2n, sfw, sfn, ow, on, cw, cn):
        right, send1 = (gw, gn), (s1w, s1n)
        send2, sendf, out_buf, cross_buf = (s2w, s2n), (sfw, sfn), (ow, on), (cw, cn)

        def left_load(a):
            from_ref = r.early.at[a] if a < 2 else r.lefts.at[a - 2]
            return pltpu.make_async_copy(
                from_ref, left.at[LEFT_SLOT[a]], r.csem.at[8 + LEFT_SLOT[a]]
            )

        def right_loads(kind):
            group = KINDS[kind][0]
            rows = 2 * tokens
            for piece in range(4):
                yield pltpu.make_async_copy(
                    right_landed(kind, piece) if piece else source(kind, half2),
                    right[group].at[kind % 2, piece * rows : (piece + 1) * rows, :],
                    r.csem.at[11 + piece],
                )

        in_slot, right_slot = {}, {}

        def load(kind):
            group, _, a = KINDS[kind]
            right_slot[group, kind % 2] = kind
            fresh = in_slot.get(LEFT_SLOT[a]) != a
            if fresh:
                in_slot[LEFT_SLOT[a]] = a
                if a >= 2:
                    lefts.arrived(a - 2)
                left_load(a).start()
            for part in range(parts(kind)):
                right_copy(kind, "one", part).wait_recv()
                right_copy(kind, "far", part).wait_recv()
            for copy in right_loads(kind):
                copy.start()
            if fresh:
                left_load(a).wait()
            for copy in right_loads(kind):
                copy.wait()

        def product(kind, start):
            group, _, a = KINDS[kind]
            assert in_slot[LEFT_SLOT[a]] == a and right_slot[group, kind % 2] == kind
            lanes = pl.ds(pl.multiple_of(start, quarter), quarter)
            return dot(left[LEFT_SLOT[a], :, lanes], right[group][kind % 2], TN)

        def mine1(kind):
            return bit[REDUCE_1[KINDS[kind][2]]]

        def rows_of(which):
            return pl.ds(pl.multiple_of(which * quarter, quarter), quarter)

        last, stored = {}, {}

        def slot_free(kind, stage, wait):
            key = (KINDS[kind][0], kind % 2, stage)
            if key in last:
                wait(last[key])
            last[key] = kind

        def first_copy(kind, part):
            group, at, _ = KINDS[kind]
            rows = rows_of(1 - mine2 if part == 0 else mine2)
            return remote(
                send1[group].at[kind % 2, rows, :], recv1[group].at[at, rows, :], r.ssem,
                (kind, part), to[REDUCE_1[KINDS[kind][2]]],
            )

        def first_sent(kind):
            for part in range(2):
                first_copy(kind, part).wait_send()

        def first_sums(kind, part):
            if part == 0:
                load(kind)
                slot_free(kind, 0, first_sent)
            group = KINDS[kind][0]
            which = 1 - mine2 if part == 0 else mine2
            send1[group][kind % 2, rows_of(which), :] = product(
                kind, (1 - mine1(kind)) * 2 * quarter + which * quarter
            ).astype(BF16)
            first_copy(kind, part).start()

        def second_copy(kind, part, from_end):
            group, at, _ = KINDS[kind]
            rows = slice(part * eighth, (part + 1) * eighth)
            return remote_pair(
                send2[group].at[kind % 2, rows, :],
                relay[0 if from_end else 1][group].at[at, rows, :],
                r.zsem.at[0, kind, part], r.zsem.at[1 if from_end else 2, kind, part],
                to[BIT_ZA] if from_end else place.mirror,
            )

        def second_sent(kind):
            for part in range(2):
                second_copy(kind, part, True).wait_send()

        def pass_copy(kind, part, which):
            group, at, _ = KINDS[kind]
            rows = slice(part * eighth, (part + 1) * eighth)
            return remote_pair(
                relay[which][group].at[at, rows, :], recv2[group].at[at, rows, :],
                r.fsem.at[which, kind, part], r.fsem.at[2, kind, part],
                place.mirror if which == 0 else to[BIT_ZA],
            )

        def pass_on(kind, part, which):
            @pl.when(inner)
            def _():
                second_copy(kind, part, which == 0).wait_recv()
                pass_copy(kind, part, which).start()

        def second_sums(kind, part):
            group, at, _ = KINDS[kind]
            which = mine2 if part else 1 - mine2
            first_copy(kind, part).wait_recv()
            total = product(kind, mine1(kind) * 2 * quarter + which * quarter) + recv1[group][
                at, rows_of(which), :
            ].astype(F32)
            if part:
                recv1[group][at, rows_of(which), :] = total.astype(BF16)
                return
            slot_free(kind, 1, second_sent)
            send2[group][kind % 2] = total.astype(BF16)
            for from_end, here in ((True, end), (False, inner)):

                @pl.when(here)
                def _():
                    for index in range(2):
                        second_copy(kind, index, from_end).start()

        def last_copy(kind):
            group, at, _ = KINDS[kind]
            return remote(
                sendf[group].at[kind % 2], recvf[group].at[at], r.ssem, (kind, 2), to[GATHER_2]
            )

        def last_sent(kind):
            last_copy(kind).wait_send()

        def out_copy(kind):
            group = KINDS[kind][0]
            buffer = cross_buf[group] if kind in CROSSED else out_buf[group].at[kind % 2]
            return pltpu.make_async_copy(buffer, outs[kind], r.osem.at[2 + kind])

        def store(kind, half, value):
            group = KINDS[kind][0]
            count = value.shape[1]
            start = pl.multiple_of(half * count, HEAD)
            if kind in CROSSED:
                cross_buf[group][pl.ds(start, count), :] = value.T
            else:
                out_buf[group][kind % 2, :, pl.ds(start, count)] = value

        finished = []

        def third_sums(kind):
            group, at, _ = KINDS[kind]
            slot_free(kind, 2, last_sent)
            for part in range(2):
                pass_copy(kind, part, 0).wait_recv()

            def total(which):
                rows = pl.ds(pl.multiple_of(which * eighth, eighth), eighth)
                kept = pl.ds(pl.multiple_of(mine2 * quarter + which * eighth, eighth), eighth)
                return recv1[group][at, kept, :].astype(F32) + recv2[group][at, rows, :].astype(F32)

            sendf[group][kind % 2] = total(1 - half2).astype(BF16)
            last_copy(kind).start()
            key = (group, kind % 2, kind in CROSSED)
            if key in stored:
                assert stored[key] in finished
                out_copy(stored[key]).wait()
            stored[key] = kind
            store(kind, half2, total(half2))

        def finish(kind):
            group, at, _ = KINDS[kind]
            last_copy(kind).wait_recv()
            store(kind, 1 - half2, recvf[group][at].astype(F32))
            out_copy(kind).start()
            finished.append(kind)

        stage = 0

        def small_step(kind, part):
            nonlocal stage
            if part == 1:
                first_norm_back()
                return
            small_sum(stage)
            stage += 1
            if stage <= len(SMALL_STAGES):
                small_copy(stage).start()

        actions = {
            **copy_actions, 2: first_sums, 3: second_sums, 4: lambda kind, part: third_sums(kind),
            5: lambda kind, part: finish(kind), 6: lambda kind, part: pass_on(kind, part, 0),
            7: lambda kind, part: pass_on(kind, part, 1), 9: small_step,
        }
        run(SCHEDULE, actions)
        r.smalls[...] = small[...]
        for (_, _, stage), kind in last.items():
            (first_sent, second_sent, last_sent)[stage](kind)

        @pl.when(inner)
        def _():
            for kind in range(COUNT):
                for part in range(2):
                    for which in range(2):
                        pass_copy(kind, part, which).wait_send()

        for kind in stored.values():
            out_copy(kind).wait()

    wide_cols, cols = wide.shape[-1], r.mixed.shape[-1]
    each = lambda count, height, dtype: [
        pltpu.VMEM((*count, height, wide_cols), dtype), pltpu.VMEM((*count, height, cols), dtype)
    ]
    pl.run_scoped(
        sums_phase, pltpu.VMEM((3, 8 * tokens, width // 2), BF16),
        *each((2,), 8 * tokens, BF16), *each((2,), 2 * quarter, BF16),
        *each((2,), quarter, BF16), *each((2,), eighth, BF16),
        pltpu.VMEM((2, HEAD, 2 * wide_cols), F32), pltpu.VMEM((2, HEAD, 2 * cols), F32),
        pltpu.VMEM((2 * wide_cols, HEAD), F32), pltpu.VMEM((2 * cols, HEAD), F32),
    )
    for a in range(2):
        lefts.sent(a)
    for kind in range(COUNT):
        for name in ("one", "two", "far"):
            for part in range(parts(kind)):
                right_copy(kind, name, part).wait_send()
    pltpu.make_async_copy(state, r.ingrad, r.csem.at[7]).wait()


def call_block(
    hidden, tokens, cot, second, wb, conv, gain, beta, norm1, norm2, early,
    yn, dy, xn, wg, wu, wd, wq, wk, wv, wgo, wo, mixed, resid, inv,
):
    count, width = second.shape
    rows, hidden_cols, cols = 2 * count, wg.shape[1] // 2, wq.shape[1] // 2
    vmem = pl.BlockSpec(memory_space=pltpu.VMEM)
    anywhere = pl.BlockSpec(memory_space=pl.ANY)
    columns = lambda kind: 2 * (hidden_cols, cols)[KINDS[kind][0]]
    shape = lambda kind: (columns(kind), HEAD) if kind in CROSSED else (HEAD, columns(kind))
    sds = jax.ShapeDtypeStruct
    each = lambda height: [
        pltpu.VMEM((3, height, hidden_cols), BF16), pltpu.VMEM((5, height, cols), BF16)
    ]
    sem = pltpu.SemaphoreType.DMA
    half = width // 2
    relay = [sds((3, half // 4, hidden_cols), BF16), sds((5, half // 4, cols), BF16)]
    return pl.pallas_call(
        block_kernel,
        in_specs=[vmem] * 10 + [anywhere] * 15,
        out_specs=[vmem, anywhere, vmem] + [anywhere] * 16,
        out_shape=[
            sds((count, width), BF16), sds((count, width), F32), sds((SMALL_ROWS, width), F32),
            *(sds(shape(kind), F32) for kind in range(COUNT)),
            sds((2, 8 * count, half), BF16), sds((3, 3, rows, hidden_cols), BF16),
            sds((5, 3, rows, cols), BF16), sds((2, 4, rows, cols), BF16), *relay, *relay,
        ],
        scratch_shapes=[
            pltpu.VMEM((2, 2, count, half), BF16), pltpu.VMEM((2, 3, rows, hidden_cols), BF16),
            *each(half // 2), *each(half // 4), *each(half // 8),
            pltpu.VMEM((3, count, width), BF16), pltpu.VMEM((rows, width), BF16),
            pltpu.VMEM((count, width), F32), pltpu.VMEM((SMALL_ROWS, width), F32),
            pltpu.VMEM((count, width), F32),
            pltpu.VMEM((len(SMALL_STAGES) + 1, SMALL_ROWS, width), F32), pltpu.VMEM(conv.shape, F32),
            pltpu.VMEM((1, HEAD), F32), pltpu.VMEM(beta.shape, BF16),
            sem((2, 2, 7)), sem((2, COUNT, 3, 2)), sem((15,)), sem((2, 4)), sem((2, COUNT, 3)),
            sem((3, COUNT, 2)), sem((3, COUNT, 2)), sem((2, len(SMALL_STAGES) + 1)), sem((2, 7)),
            sem((2 + COUNT,)),
        ],
        compiler_params=pltpu.CompilerParams(
            vmem_limit_bytes=62 * 1024 * 1024, collective_id=1, has_side_effects=True
        ),
        cost_estimate=pl.CostEstimate(flops=5 * 10**10, bytes_accessed=2 * 10**8, transcendentals=0),
        name="block",
    )(
        hidden, tokens, cot, second, wb, conv, gain, beta, norm1, norm2, early,
        yn, dy, xn, wg, wu, wd, wq, wk, wv, wgo, wo, mixed, resid, inv,
    )


def finish_kernel(*refs):
    count = (len(refs) - 7) // 3
    small, sources = refs[0], refs[1 : 1 + count]
    n1, n2, conv, head, beta = refs[1 + count : 6 + count]
    targets, held, sems = refs[6 + count : 6 + 2 * count], refs[6 + 2 * count : -1], refs[-1]
    loads, stores = (
        [
            pltpu.make_async_copy(source, target, sems.at[way, index])
            for index, (source, target) in enumerate(zip(*pair, strict=True))
        ]
        for way, pair in enumerate(((sources, held), (held, targets)))
    )
    for load in loads:
        load.start()
    n1[...] = small[16:17, :]
    n2[...] = small[17:18, :]
    head[...] = small[18:19, :HEAD]
    cols = conv.shape[-1]
    for kind in range(3):
        for offset in range(CONV):
            row = kind * CONV + offset
            lanes = slice(0, cols) if row < 8 else slice(cols, 2 * cols)
            conv[kind, offset : offset + 1, :] = small[8 + row % 8 : 9 + row % 8, lanes]
    start = pl.multiple_of(lax.axis_index("dp") * HEAD, HEAD)
    beta[...] = small[0:8, pl.ds(start, HEAD)]
    for load, store in zip(loads, stores):
        load.wait()
        store.start()
    for store in stores:
        store.wait()


def call_finish(small, conv, arrays):
    width = small.shape[1]
    vmem = pl.BlockSpec(memory_space=pltpu.VMEM)
    anywhere = pl.BlockSpec(memory_space=pl.ANY)
    sds = jax.ShapeDtypeStruct
    return pl.pallas_call(
        finish_kernel,
        in_specs=[vmem] + [anywhere] * len(arrays),
        out_specs=[vmem] * 5 + [anywhere] * len(arrays),
        out_shape=[
            sds((1, width), F32), sds((1, width), F32), sds(conv.shape, F32), sds((1, HEAD), F32),
            sds((8, HEAD), F32), *(sds(each.shape, each.dtype) for each in arrays),
        ],
        scratch_shapes=[
            *(pltpu.VMEM(each.shape, each.dtype) for each in arrays),
            pltpu.SemaphoreType.DMA((2, len(arrays))),
        ],
        compiler_params=pltpu.CompilerParams(vmem_limit_bytes=VMEM_LIMIT),
        name="finish",
    )(small, *arrays)


def local(
    tokens, norm1_gain, w_query, w_key, w_value, w_beta, w_gate_out, conv_weights, head_gain,
    w_out, norm2_gain, w_gate, w_up, w_down, cotangent, cubic,
):
    gain_row = head_gain.reshape(1, HEAD)
    beta_rows = w_beta.T
    if cubic:
        norm1_row, norm2_row = norm1_gain.reshape(1, -1), norm2_gain.reshape(1, -1)
        mixed, resid, beta, inverses, hidden_state, second_own, xn, dy, yn, early = call_front(
            tokens, cotangent, w_query, w_key, w_value, w_gate_out, beta_rows, conv_weights,
            gain_row, w_out, norm1_row, norm2_row,
        )
        block_out, input_grad, small, *grads = call_block(
            hidden_state, tokens, cotangent, second_own, beta_rows, conv_weights, gain_row, beta,
            norm1_row, norm2_row, early, yn, dy, xn, w_gate, w_up, w_down, w_query, w_key, w_value,
            w_gate_out, w_out, mixed, resid, inverses,
        )
        norm1_sum, norm2_sum, conv_total, head_sum, beta_sum, block_out, input_grad, *grads = (
            call_finish(small, conv_weights, [block_out, input_grad, *grads[:COUNT]])
        )
        grad_down, grad_gate, grad_up, grad_out = grads[:4]
        grad_query, grad_key, grad_value, grad_gate_out = grads[4:]
        return (
            block_out, input_grad, norm1_sum[0], grad_query, grad_key, grad_value, beta_sum.T,
            grad_gate_out, conv_total, head_sum[0], grad_out, norm2_sum[0], grad_gate, grad_up,
            grad_down,
        )

    core = lax.axis_index("tensor")
    inputs = tokens.astype(F32)
    first_scale = lax.rsqrt(jnp.mean(inputs * inputs, -1, keepdims=True) + norm_eps)
    first_own = (inputs * first_scale * norm1_gain).astype(BF16)
    first_normed = both_rows(first_own, sibling(first_own), core)
    out_grad = both_rows(cotangent, sibling(cotangent), core)
    mixed, out_part, resid, beta, inverses = call_mixer_forward(
        first_normed, w_query, w_key, w_value, w_gate_out, beta_rows, conv_weights, gain_row, w_out
    )
    hidden_state = inputs + swap_sum(out_part, core)
    second_scale = lax.rsqrt(jnp.mean(hidden_state * hidden_state, -1, keepdims=True) + norm_eps)
    second_own = (hidden_state * second_scale * norm2_gain).astype(BF16)
    second_normed = both_rows(second_own, sibling(second_own), core)
    wide, down_part, back_part = call_mlp(second_normed, out_grad, w_gate, w_up, w_down)
    block_out = hidden_state + swap_sum(down_part, core)
    second_grad = swap_sum(back_part, core)
    norm2_part = jnp.sum(second_grad * hidden_state * second_scale, 0)
    state_grad = cotangent.astype(F32) + norm_back(
        second_grad, hidden_state, second_scale, norm2_gain
    )
    state_own = state_grad.astype(BF16)
    state_rows = both_rows(state_own, sibling(state_own), core)
    low, beta_low, first_part, conv_grad, head_part = call_mixer_backward(
        state_rows, w_query, w_key, w_value, w_gate_out, beta_rows, conv_weights, gain_row, w_out,
        resid, beta, inverses,
    )
    first_grad = swap_sum(first_part, core)
    norm1_part = jnp.sum(first_grad * inputs * first_scale, 0)
    input_grad = state_grad + norm_back(first_grad, inputs, first_scale, norm1_gain)
    scatter = lambda value, axis: lax.psum_scatter(value, "dp", scatter_dimension=axis, tiled=True)
    whole = lambda value: jnp.concatenate([value[0], value[1]], 1)
    product, gate_grad, up_grad = (whole(wide[:, kind]) for kind in range(3))
    grad_down = scatter(dot(product, out_grad, TN), 1)
    grad_gate = scatter(dot(second_normed, gate_grad, TN), 0)
    grad_up = scatter(dot(second_normed, up_grad, TN), 0)
    grad_out = scatter(dot(whole(mixed), state_rows, TN), 1)
    grad_query, grad_key, grad_value, grad_gate_out = (
        scatter(dot(first_normed, whole(low[:, kind]), TN), 0) for kind in range(4)
    )
    beta_sum = scatter(dot(first_normed, beta_low, TN), 0)
    conv_total = lax.psum(conv_grad, "dp")
    norm1_sum, norm2_sum, head_sum = lax.psum(
        (norm1_part, norm2_part, head_part.reshape(-1)), ("dp", "tensor")
    )
    return (
        block_out.astype(BF16), input_grad, norm1_sum, grad_query, grad_key, grad_value, beta_sum,
        grad_gate_out, conv_total, head_sum, grad_out, norm2_sum, grad_gate, grad_up, grad_down,
    )


def solution(mesh):
    rows = P(("dp", "tensor"), None)
    columns = P(None, "tensor")
    in_specs = (
        rows, P(), columns, columns, columns, columns, columns, P(None, None, "tensor"), P(),
        P("tensor", None), P(), columns, columns, P("tensor", None), rows,
    )
    scattered = P("dp", "tensor")
    crossed = P("tensor", "dp")
    out_specs = (
        rows, rows, P(), scattered, scattered, scattered, scattered, scattered,
        P(None, None, "tensor"), P(), crossed, P(), scattered, scattered, crossed,
    )
    cubic = mesh.shape["dp"] == 16
    return jax.shard_map(
        functools.partial(local, cubic=cubic), mesh=mesh, in_specs=in_specs, out_specs=out_specs,
        check_vma=False,
    )
```

```python
import functools
import typing

import jax
import jax.numpy as jnp
from jax import lax
from jax.experimental import pallas as pl
from jax.experimental.pallas import tpu as pltpu
from jax.sharding import PartitionSpec as P

HEAD = 128
CONV = 4
PAIR = 2 * HEAD
GROUP = 4 * HEAD
F32 = jnp.float32
BF16 = jnp.bfloat16
norm_eps = 1e-06
unit_eps = 1e-06
VMEM_LIMIT = 56 * 1024 * 1024

NN = (((1,), (0,)), ((), ()))
NT = (((1,), (1,)), ((), ()))
TN = (((0,), (0,)), ((), ()))


def dot(left, right, dims=NN):
    return lax.dot_general(left, right, dims, preferred_element_type=F32)


def halves(value):
    high = value.astype(BF16)
    return high, (value - high.astype(F32)).astype(BF16)


def dot3(left, right, dims=NN):
    left_high, left_low = halves(left)
    right_high, right_low = halves(right)
    return (
        dot(left_high, right_low, dims) + dot(left_low, right_high, dims)
    ) + dot(left_high, right_high, dims)


def rows_down(value, shift):
    if shift == 0:
        return value
    row = lax.broadcasted_iota(jnp.int32, value.shape, 0)
    return jnp.where(row >= shift, pltpu.roll(value, shift, 0), 0.0)


def rows_up(value, shift):
    if shift == 0:
        return value
    rows = value.shape[0]
    row = lax.broadcasted_iota(jnp.int32, value.shape, 0)
    return jnp.where(row < rows - shift, pltpu.roll(value, rows - shift, 0), 0.0)


def causal_conv(value, taps):
    total = value * taps[CONV - 1 : CONV]
    for offset in range(CONV - 1):
        total = total + rows_down(value, CONV - 1 - offset) * taps[offset : offset + 1]
    return total


def sigmoid(value):
    return 1.0 / (1.0 + jnp.exp(-value))


def tri_mask(rows, strict):
    row = lax.broadcasted_iota(jnp.int32, (rows, rows), 0)
    col = lax.broadcasted_iota(jnp.int32, (rows, rows), 1)
    return row > col if strict else row >= col


def unit_lower_inverses(lowers):
    size = lowers[0].shape[0]
    row = lax.broadcasted_iota(jnp.int32, (size, size), 0)
    col = lax.broadcasted_iota(jnp.int32, (size, size), 1)
    eye = jnp.where(row == col, 1.0, 0.0)
    lows = [lower.astype(BF16) for lower in lowers]
    level, inverses = 0, None
    while (1 << level) < size:
        mask = (
            ((row >> (level + 1)) == (col >> (level + 1)))
            & (((row >> level) & 1) == 1)
            & (((col >> level) & 1) == 0)
        )
        if inverses is None:
            inverses = [eye - jnp.where(mask, lower, 0.0) for lower in lowers]
        else:
            known = [inverse.astype(BF16) for inverse in inverses]
            parts = [jnp.where(mask, low, jnp.zeros_like(low)) for low in lows]
            inner = [dot(part, each).astype(BF16) for part, each in zip(parts, known)]
            inverses = [
                inverse - dot(each, right)
                for inverse, each, right in zip(inverses, known, inner)
            ]
        level += 1
    lefts = [
        (eye - inverse - dot3(lower, inverse)).astype(BF16)
        for lower, inverse in zip(lowers, inverses)
    ]
    return [
        inverse + dot(inverse.astype(BF16), left) for inverse, left in zip(inverses, lefts)
    ]


def head_column(values, head):
    lane = lax.broadcasted_iota(jnp.int32, values.shape, 1)
    return jnp.sum(jnp.where(lane == head, values, 0.0), -1, keepdims=True)


def forward_group(
    step, xn_ref, wq_ref, wk_ref, wv_ref, wg_ref, wb_ref, conv_ref, gain_ref, wo_ref,
    mixed_ref, resid_ref, beta_ref, inv_ref, total,
):
    xn = xn_ref[...]
    rows = xn.shape[0]
    half = rows // 2

    @pl.when(step == 0)
    def _():
        beta_ref[...] = dot(xn, wb_ref[...], NT)
        total[...] = jnp.zeros_like(total)

    query_in = dot(xn, wq_ref[...])
    key_in = dot(xn, wk_ref[...])
    value_in = dot(xn, wv_ref[...])
    gate_in = dot(xn, wg_ref[...])
    for place, value in enumerate((query_in, key_in, value_in, gate_in)):
        resid_ref[place] = value
    beta_all = sigmoid(beta_ref[...])
    conv_q = causal_conv(query_in, conv_ref[0])
    conv_k = causal_conv(key_in, conv_ref[1])
    conv_v = causal_conv(value_in, conv_ref[2])
    query_act = conv_q * sigmoid(conv_q)
    key_act = conv_k * sigmoid(conv_k)
    value_act = conv_v * sigmoid(conv_v)
    gate_act = gate_in * sigmoid(gate_in)
    strict = tri_mask(rows, True)
    causal = tri_mask(rows, False)
    heads = []
    for head in range(GROUP // HEAD):
        cols = slice(head * HEAD, (head + 1) * HEAD)
        queries = query_act[:, cols]
        queries = queries * lax.rsqrt(jnp.sum(queries * queries, -1, keepdims=True) + unit_eps)
        queries = queries * HEAD**-0.5
        keys = key_act[:, cols]
        keys = keys * lax.rsqrt(jnp.sum(keys * keys, -1, keepdims=True) + unit_eps)
        beta = head_column(beta_all, GROUP // HEAD * step + head)
        lower = jnp.where(strict, dot3(keys, keys, NT) * beta, 0.0)
        scores = jnp.where(causal, dot3(queries, keys, NT), 0.0)
        heads.append((cols, lower, scores, value_act[:, cols] * beta))
    inverses = unit_lower_inverses(
        [lower[part, part] for _, lower, _, _ in heads for part in (slice(0, half), slice(half, rows))]
    )
    upper_u = [dot3(inverses[2 * n], weighted[:half]) for n, (_, _, _, weighted) in enumerate(heads)]
    rest = [
        weighted[half:] - dot3(lower[half:, :half], upper)
        for (_, lower, _, weighted), upper in zip(heads, upper_u)
    ]
    lower_u = [dot3(inverses[2 * n + 1], right) for n, right in enumerate(rest)]
    updates = [jnp.concatenate(pair, 0) for pair in zip(upper_u, lower_u)]
    outputs = [dot3(scores, update) for (_, _, scores, _), update in zip(heads, updates)]
    for head, (cols, _, _, _) in enumerate(heads):
        inv_ref[head, 0] = inverses[2 * head]
        inv_ref[head, 1] = inverses[2 * head + 1]
        resid_ref[4, :, cols] = updates[head]
        output = outputs[head]
        resid_ref[5, :, cols] = output
        normed = output * lax.rsqrt(jnp.mean(output * output, -1, keepdims=True) + norm_eps)
        mixed_ref[0, :, cols] = (normed * gain_ref[...] * gate_act[:, cols]).astype(BF16)
    total[...] += dot(mixed_ref[0], wo_ref[...])


def mixer_forward(
    xn_ref, wq_ref, wk_ref, wv_ref, wg_ref, wb_ref, conv_ref, gain_ref, wo_ref,
    mixed_ref, part_ref, resid_ref, beta_ref, inv_ref, total,
):
    step = pl.program_id(0)
    forward_group(
        step, xn_ref, wq_ref, wk_ref, wv_ref, wg_ref, wb_ref, conv_ref, gain_ref, wo_ref,
        mixed_ref, resid_ref, beta_ref, inv_ref, total,
    )

    @pl.when(step == pl.num_programs(0) - 1)
    def _():
        part_ref[...] = total[...].astype(BF16)


def call_mixer_forward(xn, wq, wk, wv, wg, wb, conv, gain, wo):
    rows, width = xn.shape
    cols = wq.shape[1]
    groups = cols // GROUP
    heads = wb.shape[0]
    whole = lambda *shape: pl.BlockSpec(shape, lambda i: (0,) * len(shape))
    weight = pl.BlockSpec((width, GROUP), lambda i: (0, i))
    return pl.pallas_call(
        mixer_forward,
        grid=(groups,),
        in_specs=[
            whole(rows, width), weight, weight, weight, weight, whole(heads, width),
            pl.BlockSpec((3, CONV, GROUP), lambda i: (0, 0, i)), whole(1, HEAD),
            pl.BlockSpec((GROUP, width), lambda i: (i, 0)),
        ],
        out_specs=[
            pl.BlockSpec((1, rows, GROUP), lambda i: (i // (groups // 2), 0, i % (groups // 2))),
            whole(rows, width), pl.BlockSpec((6, rows, GROUP), lambda i: (0, 0, i)), whole(rows, heads),
            pl.BlockSpec((GROUP // HEAD, 2, rows // 2, rows // 2), lambda i: (i, 0, 0, 0)),
        ],
        out_shape=[
            jax.ShapeDtypeStruct((2, rows, cols // 2), BF16),
            jax.ShapeDtypeStruct((rows, width), BF16),
            jax.ShapeDtypeStruct((6, rows, cols), F32), jax.ShapeDtypeStruct((rows, heads), F32),
            jax.ShapeDtypeStruct((heads, 2, rows // 2, rows // 2), F32),
        ],
        scratch_shapes=[pltpu.VMEM((rows, width), F32)],
        compiler_params=pltpu.CompilerParams(vmem_limit_bytes=VMEM_LIMIT),
        cost_estimate=pl.CostEstimate(
            flops=2 * rows * width * cols * 5 + 10**10, bytes_accessed=5 * width * cols * 2 + 10**7,
            transcendentals=0,
        ),
        name="mixer_forward",
    )(xn, wq, wk, wv, wg, wb, conv, gain, wo)


def silu_slope(value, sig):
    return sig * (1.0 + value * (1.0 - sig))


def backward_pair(
    step, steps, dh_ref, wq_ref, wk_ref, wv_ref, wg_ref, wb_ref, conv_ref, gain_ref, wo_ref,
    resid_ref, beta_ref, inv_ref, low_ref, bl_ref, dconv_ref, dgain_ref, total, beta_total,
):
    rows = dh_ref.shape[0]
    half = rows // 2

    @pl.when(step == 0)
    def _():
        total[...] = jnp.zeros_like(total)
        beta_total[...] = jnp.zeros_like(beta_total)
        dgain_ref[...] = jnp.zeros_like(dgain_ref)

    mixed_grad = dot(dh_ref[...], wo_ref[...], NT)
    query_in, key_in, value_in, gate_in = (resid_ref[place] for place in range(4))
    beta_all = sigmoid(beta_ref[...])
    lane = lax.broadcasted_iota(jnp.int32, beta_all.shape, 1)
    conv_q = causal_conv(query_in, conv_ref[0])
    conv_k = causal_conv(key_in, conv_ref[1])
    conv_v = causal_conv(value_in, conv_ref[2])
    sig_q, sig_k, sig_v = sigmoid(conv_q), sigmoid(conv_k), sigmoid(conv_v)
    sig_g = sigmoid(gate_in)
    query_act = conv_q * sig_q
    key_act = conv_k * sig_k
    value_act = conv_v * sig_v
    gate_act = gate_in * sig_g
    strict = tri_mask(rows, True)
    causal = tri_mask(rows, False)
    gain = gain_ref[...]
    both = range(2)
    cols = [slice(head * HEAD, (head + 1) * HEAD) for head in both]
    raw_q = [query_act[:, each] for each in cols]
    raw_k = [key_act[:, each] for each in cols]
    values = [value_act[:, each] for each in cols]
    scale_q = [lax.rsqrt(jnp.sum(each * each, -1, keepdims=True) + unit_eps) for each in raw_q]
    scale_k = [lax.rsqrt(jnp.sum(each * each, -1, keepdims=True) + unit_eps) for each in raw_k]
    queries = [raw_q[head] * scale_q[head] * HEAD**-0.5 for head in both]
    keys = [raw_k[head] * scale_k[head] for head in both]
    beta = [head_column(beta_all, 2 * step + head) for head in both]
    updates = [resid_ref[4, :, each] for each in cols]
    output = [resid_ref[5, :, each] for each in cols]
    upstream = [mixed_grad[:, each] for each in cols]
    scale_o = [lax.rsqrt(jnp.mean(each * each, -1, keepdims=True) + norm_eps) for each in output]
    unit_out = [output[head] * scale_o[head] for head in both]
    grads_g = [upstream[head] * (unit_out[head] * gain) for head in both]
    d_normed = [upstream[head] * gate_act[:, cols[head]] for head in both]
    for head in both:
        dgain_ref[...] += jnp.sum(d_normed[head] * unit_out[head], 0, keepdims=True)
    d_unit = [each * gain for each in d_normed]
    d_output = [
        scale_o[head]
        * (
            d_unit[head]
            - unit_out[head] * jnp.mean(d_unit[head] * unit_out[head], -1, keepdims=True)
        )
        for head in both
    ]
    inner = [dot3(each, each, NT) for each in keys]
    lower_21 = [inner[head][half:, :half] * beta[head][half:] for head in both]
    scores = [jnp.where(causal, dot3(queries[head], keys[head], NT), 0.0) for head in both]
    d_updates = [dot3(scores[head], d_output[head], TN) for head in both]
    d_right_2 = [dot3(inv_ref[head, 1], d_updates[head][half:], TN) for head in both]
    d_upper = [
        d_updates[head][:half] - dot3(lower_21[head], d_right_2[head], TN) for head in both
    ]
    d_right_1 = [dot3(inv_ref[head, 0], d_upper[head], TN) for head in both]
    d_right = [jnp.concatenate([d_right_1[head], d_right_2[head]], 0) for head in both]
    d_scores = [jnp.where(causal, dot3(d_output[head], updates[head], NT), 0.0) for head in both]
    d_lower = [jnp.where(strict, -dot3(d_right[head], updates[head], NT), 0.0) for head in both]
    d_inner = [d_lower[head] * beta[head] for head in both]
    d_queries = [dot3(d_scores[head], keys[head]) * HEAD**-0.5 for head in both]
    d_keys = [
        dot3(d_scores[head], queries[head], TN)
        + dot3(d_inner[head], keys[head])
        + dot3(d_inner[head], keys[head], TN)
        for head in both
    ]
    grads_v = [d_right[head] * beta[head] for head in both]
    unit_back = lambda grad, raw, scale: scale * (
        grad - raw * (scale * scale) * jnp.sum(grad * raw, -1, keepdims=True)
    )
    grads_q = [unit_back(d_queries[head], raw_q[head], scale_q[head]) for head in both]
    grads_k = [unit_back(d_keys[head], raw_k[head], scale_k[head]) for head in both]
    for head in both:
        d_beta = jnp.sum(d_lower[head] * inner[head], -1, keepdims=True) + jnp.sum(
            d_right[head] * values[head], -1, keepdims=True
        )
        d_beta_in = d_beta * beta[head] * (1.0 - beta[head])
        beta_total[...] += jnp.where(lane == 2 * step + head, d_beta_in, 0.0)
    for kind, (grads, pre, conv, sig) in enumerate(
        (
            (grads_q, query_in, conv_q, sig_q),
            (grads_k, key_in, conv_k, sig_k),
            (grads_v, value_in, conv_v, sig_v),
        )
    ):
        d_conv = jnp.concatenate(grads, 1) * silu_slope(conv, sig)
        taps = conv_ref[kind]
        d_pre = d_conv * taps[CONV - 1 : CONV]
        for offset in range(CONV):
            shift = CONV - 1 - offset
            dconv_ref[kind, offset : offset + 1, :] = jnp.sum(
                d_conv * rows_down(pre, shift), 0, keepdims=True
            )
            if shift:
                d_pre = d_pre + rows_up(d_conv, shift) * taps[offset : offset + 1]
        low_ref[0, kind] = d_pre.astype(BF16)
    low_ref[0, 3] = (jnp.concatenate(grads_g, 1) * silu_slope(gate_in, sig_g)).astype(BF16)
    total[...] += (
        dot(low_ref[0, 0], wq_ref[...], NT)
        + dot(low_ref[0, 1], wk_ref[...], NT)
        + dot(low_ref[0, 2], wv_ref[...], NT)
        + dot(low_ref[0, 3], wg_ref[...], NT)
    )

    @pl.when(step == steps - 1)
    def _():
        bl_ref[...] = beta_total[...].astype(BF16)
        total[...] += dot(bl_ref[...], wb_ref[...])


def mixer_backward(
    dh_ref, wq_ref, wk_ref, wv_ref, wg_ref, wb_ref, conv_ref, gain_ref, wo_ref,
    resid_ref, beta_ref, inv_ref, low_ref, bl_ref, part_ref, dconv_ref, dgain_ref,
    total, beta_total,
):
    step, steps = pl.program_id(0), pl.num_programs(0)
    backward_pair(
        step, steps, dh_ref, wq_ref, wk_ref, wv_ref, wg_ref, wb_ref, conv_ref, gain_ref, wo_ref,
        resid_ref, beta_ref, inv_ref, low_ref, bl_ref, dconv_ref, dgain_ref, total, beta_total,
    )

    @pl.when(step == steps - 1)
    def _():
        part_ref[...] = total[...].astype(BF16)


def call_mixer_backward(dh, wq, wk, wv, wg, wb, conv, gain, wo, resid, beta, inv):
    rows, width = dh.shape
    cols = wq.shape[1]
    pairs = cols // PAIR
    heads = wb.shape[0]
    whole = lambda *shape: pl.BlockSpec(shape, lambda i: (0,) * len(shape))
    weight = pl.BlockSpec((width, PAIR), lambda i: (0, i))
    taps = pl.BlockSpec((3, CONV, PAIR), lambda i: (0, 0, i))
    return pl.pallas_call(
        mixer_backward,
        grid=(pairs,),
        in_specs=[
            whole(rows, width), weight, weight, weight, weight, whole(heads, width), taps,
            whole(1, HEAD), pl.BlockSpec((PAIR, width), lambda i: (i, 0)),
            pl.BlockSpec((6, rows, PAIR), lambda i: (0, 0, i)), whole(rows, heads),
            pl.BlockSpec((2, 2, rows // 2, rows // 2), lambda i: (i, 0, 0, 0)),
        ],
        out_specs=[
            pl.BlockSpec((1, 4, rows, PAIR), lambda i: (i // (pairs // 2), 0, 0, i % (pairs // 2))),
            whole(rows, heads), whole(rows, width), taps, whole(1, HEAD),
        ],
        out_shape=[
            jax.ShapeDtypeStruct((2, 4, rows, cols // 2), BF16),
            jax.ShapeDtypeStruct((rows, heads), BF16),
            jax.ShapeDtypeStruct((rows, width), BF16), jax.ShapeDtypeStruct(conv.shape, F32),
            jax.ShapeDtypeStruct((1, HEAD), F32),
        ],
        scratch_shapes=[pltpu.VMEM((rows, width), F32), pltpu.VMEM((rows, heads), F32)],
        compiler_params=pltpu.CompilerParams(vmem_limit_bytes=VMEM_LIMIT),
        cost_estimate=pl.CostEstimate(
            flops=2 * rows * width * cols * 5 + 2 * 10**10,
            bytes_accessed=5 * width * cols * 2 + 10**7,
            transcendentals=0,
        ),
        name="mixer_backward",
    )(dh, wq, wk, wv, wg, wb, conv, gain, wo, resid, beta, inv)


def mlp_copies(index, slot, wg_ref, wu_ref, wd_ref, wg_buf, wu_buf, wd_buf, sems):
    hidden = wg_ref.shape[1] // 2
    for part in range(2):
        start = pl.multiple_of(part * hidden + index * HEAD, HEAD)
        lanes = pl.ds(part * HEAD, HEAD)
        yield pltpu.make_async_copy(
            wg_ref.at[:, pl.ds(start, HEAD)], wg_buf.at[slot, :, lanes], sems.at[slot, part]
        )
        yield pltpu.make_async_copy(
            wu_ref.at[:, pl.ds(start, HEAD)], wu_buf.at[slot, :, lanes], sems.at[slot, 2 + part]
        )
        yield pltpu.make_async_copy(
            wd_ref.at[pl.ds(start, HEAD), :], wd_buf.at[slot, lanes, :], sems.at[slot, 4 + part]
        )


def mlp_tile(step, steps, yn_ref, dy_ref, weights, low_store, down_total, back_total):
    wg_ref, wu_ref, wd_ref, wg_buf, wu_buf, wd_buf, sems = weights
    slot = lax.rem(step, 2)

    @pl.when(step == 0)
    def _():
        down_total[...] = jnp.zeros_like(down_total)
        back_total[...] = jnp.zeros_like(back_total)

    @pl.when(step + 1 < steps)
    def _():
        for copy in mlp_copies(step + 1, 1 - slot, *weights):
            copy.start()

    for copy in mlp_copies(step, slot, *weights):
        copy.wait()
    yn, dy = yn_ref[...], dy_ref[...]
    w_gate, w_up, w_down = wg_buf[slot], wu_buf[slot], wd_buf[slot]
    gate = dot(yn, w_gate)
    up = dot(yn, w_up)
    d_product = dot(dy, w_down, NT)
    sig = sigmoid(gate)
    act = gate * sig
    product = (act * up).astype(BF16)
    gate_grad = (d_product * up * silu_slope(gate, sig)).astype(BF16)
    up_grad = (d_product * act).astype(BF16)
    down_total[...] += dot(product, w_down)
    back_total[...] += dot(gate_grad, w_gate, NT) + dot(up_grad, w_up, NT)
    for kind, value in enumerate((product, gate_grad, up_grad)):
        low_store(0, kind, value[:, :HEAD])
        low_store(1, kind, value[:, HEAD:])


def mlp_kernel(
    yn_ref, dy_ref, wg_ref, wu_ref, wd_ref, low_ref, down_ref, back_ref,
    wg_buf, wu_buf, wd_buf, down_total, back_total, sems,
):
    step, steps = pl.program_id(0), pl.num_programs(0)
    weights = (wg_ref, wu_ref, wd_ref, wg_buf, wu_buf, wd_buf, sems)

    @pl.when(step == 0)
    def _():
        for copy in mlp_copies(0, 0, *weights):
            copy.start()

    def low_store(half, kind, value):
        low_ref[half, kind] = value

    mlp_tile(step, steps, yn_ref, dy_ref, weights, low_store, down_total, back_total)

    @pl.when(step == steps - 1)
    def _():
        down_ref[...] = down_total[...].astype(BF16)
        back_ref[...] = back_total[...].astype(BF16)


def call_mlp(yn, dy, w_gate, w_up, w_down):
    rows, width = yn.shape
    hidden = w_gate.shape[1] // 2
    whole = lambda *shape: pl.BlockSpec(shape, lambda i: (0,) * len(shape))
    anywhere = pl.BlockSpec(memory_space=pl.ANY)
    tile = pl.BlockSpec((2, 3, rows, HEAD), lambda i: (0, 0, 0, i))
    return pl.pallas_call(
        mlp_kernel,
        grid=(hidden // HEAD,),
        in_specs=[whole(rows, width), whole(rows, width), anywhere, anywhere, anywhere],
        out_specs=[tile, whole(rows, width), whole(rows, width)],
        out_shape=[
            jax.ShapeDtypeStruct((2, 3, rows, hidden), BF16),
            jax.ShapeDtypeStruct((rows, width), BF16),
            jax.ShapeDtypeStruct((rows, width), BF16),
        ],
        scratch_shapes=[
            pltpu.VMEM((2, width, PAIR), BF16), pltpu.VMEM((2, width, PAIR), BF16),
            pltpu.VMEM((2, PAIR, width), BF16), pltpu.VMEM((rows, width), F32),
            pltpu.VMEM((rows, width), F32), pltpu.SemaphoreType.DMA((2, 6)),
        ],
        compiler_params=pltpu.CompilerParams(vmem_limit_bytes=VMEM_LIMIT),
        cost_estimate=pl.CostEstimate(
            flops=12 * rows * width * w_gate.shape[1], bytes_accessed=6 * width * w_gate.shape[1],
            transcendentals=0,
        ),
        name="mlp",
    )(yn, dy, w_gate, w_up, w_down)


def norm_back(upstream, inputs, scale_rows, gain_row):
    scaled_grad = upstream * gain_row
    return scale_rows * (
        scaled_grad
        - inputs * scale_rows * scale_rows * jnp.mean(scaled_grad * inputs, -1, keepdims=True)
    )


def take(value, axis, index):
    return lax.dynamic_index_in_dim(value, index, axis, keepdims=False)


def sibling(value):
    return lax.ppermute(value, "tensor", [(0, 1), (1, 0)])


def both_rows(mine, other, core):
    axis = mine.ndim - 2
    return jnp.where(
        core == 0, jnp.concatenate([mine, other], axis), jnp.concatenate([other, mine], axis)
    )


def swap_sum(partial, core):
    parts = partial.reshape(2, -1, partial.shape[-1])
    received = sibling(take(parts, 0, 1 - core))
    return take(parts, 0, core).astype(F32) + received.astype(F32)


BIT_X, BIT_Y, BIT_ZA, BIT_ZB = 1, 2, 4, 8
GATHER_2 = BIT_ZA
BITS = (1, 2, 4, 8)
SMALL_STAGES = ((1, 1, True), (2, 1, True), (4, 4, True), (8, 4, True), (1, 4, False), (2, 2, False))
CHIPS = 16
MESH = pl.DeviceIdType.MESH
KINDS = ((0, 0, 0), (0, 1, 2), (0, 2, 2), (1, 0, 3), (1, 1, 1), (1, 2, 1), (1, 3, 1), (1, 4, 1))
COUNT = len(KINDS)
CROSSED = (0, 3)
GATHER_1 = (BIT_Y, BIT_Y, BIT_X, BIT_Y)
REDUCE_1 = tuple(BIT_X + BIT_Y - bit for bit in GATHER_1)
LEFT_SLOT = (0, 0, 2, 1)
SMALL_ROWS = 24
FIRST_STEPS = (
    830,
)
TILE_STEPS = {2: (1100,), 3: (130,), 5: (10, 20, 810, 0,), 8: (800,)}
LAST_TILE_STEPS = (
    811, 1, 21, 11, 801, 30,
)
PAIR_STEPS = {0: (110,), 1: (1200, 1101, 101, 821, 100, 820,), 2: (111, 1201,)}
SCHEDULE = (
    230, 40, 850, 50, 200, 60, 901, 231, 330, 201, 840, 630,
    210, 211, 631, 870, 300, 140, 860, 310, 600, 120, 701, 121,
    900, 150, 601, 301, 331, 731, 70, 730, 430, 220, 700, 170,
    250, 610, 240, 900, 400, 711, 611, 221, 241, 340, 160, 710,
    251, 350, 351, 640, 270, 900, 271, 341, 320, 641, 311, 410,
    720, 721, 620, 900, 621, 510, 321, 751, 651, 750, 530, 650,
    370, 260, 741, 261, 670, 900, 360, 660, 740, 420, 770, 450,
    520, 771, 671, 900, 550, 661, 440, 760, 761, 900, 371, 470,
    500, 540, 361, 460, 570, 560,
)


def block_place(block, left):
    bit = lambda mask: int((block & mask) != 0)
    return bit(GATHER_1[left]), bit(REDUCE_1[left]) * 4 + bit(BIT_ZB) * 2 + bit(GATHER_2)


class Place:
    def __init__(self, tokens):
        self.chip, self.core = lax.axis_index("dp"), lax.axis_index("tensor")
        self.bit = {mask: lax.rem(self.chip // mask, 2) for mask in BITS}
        step = {mask: mask * (1 - 2 * self.bit[mask]) for mask in BITS}
        self.to = {mask: (self.chip + step[mask], self.core) for mask in BITS}
        self.mirror = (self.chip + step[BIT_ZA] + step[BIT_ZB], self.core)
        self.near = (self.chip, 1 - self.core)
        self.own_rows = pl.ds(pl.multiple_of(self.core * tokens, tokens), tokens)
        self.other_rows = pl.ds(pl.multiple_of((1 - self.core) * tokens, tokens), tokens)
        self.tokens = tokens

    def greet(self, partners):
        barrier = pltpu.get_barrier_semaphore()
        for target in partners:
            pl.semaphore_signal(barrier, inc=1, device_id=target, device_id_type=MESH)
        pl.semaphore_wait(barrier, len(partners))


def remote_pair(source, target, send_sem, recv_sem, device):
    return pltpu.make_async_remote_copy(
        src_ref=source, dst_ref=target, send_sem=send_sem, recv_sem=recv_sem,
        device_id=device, device_id_type=MESH,
    )


def remote(source, target, sems, index, device):
    return remote_pair(source, target, sems.at[(0, *index)], sems.at[(1, *index)], device)


class Lefts:
    def __init__(self, lefts, place, own, landed, sems, local_sems):
        self.place, self.own, self.landed, self.sems, self.local = place, own, landed, sems, local_sems
        self.lefts = lefts

    def rows(self, a, piece):
        tokens = self.place.tokens
        start = pl.multiple_of((2 * piece + self.place.core) * tokens, tokens)
        return self.landed.at[a, pl.ds(start, tokens), :]

    def copy(self, a, name):
        place, own, sems = self.place, self.own, self.sems
        first = GATHER_1[self.lefts[a]]
        half = place.bit[first]
        if name == "one":
            return remote(own.at[a, 1 - half], self.rows(a, 1), sems, (a, 0), place.to[first])
        if name == "two":
            return remote(own.at[a, half], self.rows(a, 2), sems, (a, 1), place.to[GATHER_2])
        if name == "far":
            return remote(self.rows(a, 1), self.rows(a, 3), sems, (a, 2), place.to[GATHER_2])
        if name == 0:
            return remote(own.at[a, half], self.rows(a, 0), sems, (a, 3), place.near)
        return remote(self.rows(a, name), self.rows(a, name), sems, (a, 3 + name), place.near)

    def own_copy(self, a):
        half = self.place.bit[GATHER_1[self.lefts[a]]]
        return pltpu.make_async_copy(self.own.at[a, half], self.rows(a, 0), self.local.at[a])

    def start(self, a, natural):
        for block in range(CHIPS):
            half, place = block_place(block, self.lefts[a])
            self.own[a, half, :, place * HEAD : (place + 1) * HEAD] = natural[
                :, block * HEAD : (block + 1) * HEAD
            ]
        for name in ("one", "two", 0):
            self.copy(a, name).start()
        self.own_copy(a).start()

    def middle(self, a):
        self.copy(a, "one").wait_recv()
        self.copy(a, "far").start()
        self.copy(a, 1).start()
        self.copy(a, "two").wait_recv()
        self.copy(a, 2).start()

    def far(self, a):
        self.copy(a, "far").wait_recv()
        self.copy(a, 3).start()

    def arrived(self, a):
        for piece in range(4):
            self.copy(a, piece).wait_recv()
        self.own_copy(a).wait()

    def sent(self, a):
        for name in ("one", "two", "far", 0, 1, 2, 3):
            self.copy(a, name).wait_send()


def front_kernel(
    tokens_ref, cot_ref, wq_ref, wk_ref, wv_ref, wg_ref, wb_ref, conv_ref, gain_ref, wo_ref,
    norm1_ref, norm2_ref,
    mixed_ref, resid_ref, beta_ref, inv_ref, hidden_ref, second_ref, xn_out, dy_out, yn_out,
    landed,
    total, xn, dy, yn, own, stage, part, wbuf, wobuf, lsem, qsem, csem, wsem,
):
    step, steps = pl.program_id(0), pl.num_programs(0)
    place = Place(tokens_ref.shape[0])
    own_rows, other_rows = place.own_rows, place.other_rows
    lefts = Lefts((0, 1), place, own, landed, lsem, csem)

    def row_copy(index):
        source = stage if index == 2 else (xn, dy, None, yn)[index].at[own_rows, :]
        target = part if index == 2 else source
        return remote(source, target, qsem, (index,), place.near)

    def out_copy(index):
        source, target = ((xn, xn_out), (dy, dy_out), (yn, yn_out))[index]
        return pltpu.make_async_copy(source, target, csem.at[2 + index])

    def weight_copies(group):
        columns = pl.ds(pl.multiple_of(group * GROUP, GROUP), GROUP)
        for index, weight in enumerate((wq_ref, wk_ref, wv_ref, wg_ref)):
            yield pltpu.make_async_copy(
                weight.at[:, columns], wbuf.at[group, index], wsem.at[group, index]
            )
        yield pltpu.make_async_copy(wo_ref.at[columns, :], wobuf.at[group], wsem.at[group, 4])

    @pl.when(step == 0)
    def _():
        for group in range(wbuf.shape[0]):
            for copy in weight_copies(group):
                copy.start()
        place.greet((place.to[BIT_X], place.to[BIT_Y], place.to[GATHER_2], place.near))
        inputs = tokens_ref[...].astype(F32)
        scale = lax.rsqrt(jnp.mean(inputs * inputs, -1, keepdims=True) + norm_eps)
        xn[own_rows, :] = (inputs * scale * norm1_ref[...]).astype(BF16)
        row_copy(0).start()
        dy[own_rows, :] = cot_ref[...]
        row_copy(1).start()
        lefts.start(0, cot_ref)
        lefts.start(1, xn[own_rows, :])
        row_copy(0).wait()
        out_copy(0).start()

    for copy in weight_copies(step):
        copy.wait()
    forward_group(
        step, xn, *(wbuf.at[step, index] for index in range(4)), wb_ref, conv_ref, gain_ref,
        wobuf.at[step], mixed_ref, resid_ref, beta_ref, inv_ref, total,
    )

    @pl.when(step == 0)
    def _():
        row_copy(1).wait()
        out_copy(1).start()
        lefts.middle(0)
        lefts.middle(1)

    @pl.when(step == steps - 1)
    def _():
        stage[...] = total[other_rows, :].astype(BF16)
        row_copy(2).start()
        lefts.far(0)
        lefts.far(1)
        hidden = tokens_ref[...].astype(F32) + total[own_rows, :]
        row_copy(2).wait()
        hidden = hidden + part[...].astype(F32)
        hidden_ref[...] = hidden
        scale = lax.rsqrt(jnp.mean(hidden * hidden, -1, keepdims=True) + norm_eps)
        second = (hidden * scale * norm2_ref[...]).astype(BF16)
        yn[own_rows, :] = second
        row_copy(3).start()
        second_ref[...] = second
        for a in range(2):
            lefts.arrived(a)
            lefts.sent(a)
        row_copy(3).wait()
        out_copy(2).start()
        for index in range(3):
            out_copy(index).wait()


def call_front(tokens, cot, wq, wk, wv, wg, wb, conv, gain, wo, norm1, norm2):
    count, width = tokens.shape
    rows, cols, heads = 2 * count, wq.shape[1], wb.shape[0]
    groups = cols // GROUP
    sds = jax.ShapeDtypeStruct
    whole = lambda *shape: pl.BlockSpec(shape, lambda i: (0,) * len(shape))
    anywhere = pl.BlockSpec(memory_space=pl.ANY)
    sem = pltpu.SemaphoreType.DMA
    low = lambda *shape: pltpu.VMEM(shape, BF16)
    return pl.pallas_call(
        front_kernel,
        grid=(groups,),
        in_specs=[
            whole(count, width), whole(count, width), anywhere, anywhere, anywhere, anywhere,
            whole(heads, width), pl.BlockSpec((3, CONV, GROUP), lambda i: (0, 0, i)),
            whole(1, HEAD), anywhere, whole(1, width), whole(1, width),
        ],
        out_specs=[
            pl.BlockSpec((1, rows, GROUP), lambda i: (i // (groups // 2), 0, i % (groups // 2))),
            pl.BlockSpec((6, rows, GROUP), lambda i: (0, 0, i)), whole(rows, heads),
            pl.BlockSpec((GROUP // HEAD, 2, count, count), lambda i: (i, 0, 0, 0)),
            whole(count, width), whole(count, width), anywhere, anywhere, anywhere, anywhere,
        ],
        out_shape=[
            sds((2, rows, cols // 2), BF16), sds((6, rows, cols), F32), sds((rows, heads), F32),
            sds((heads, 2, count, count), F32), sds((count, width), F32),
            sds((count, width), BF16), sds((rows, width), BF16), sds((rows, width), BF16),
            sds((rows, width), BF16), sds((2, 8 * count, width // 2), BF16),
        ],
        scratch_shapes=[
            pltpu.VMEM((rows, width), F32), low(rows, width), low(rows, width), low(rows, width),
            low(2, 2, count, width // 2), low(count, width), low(count, width),
            low(groups, 4, width, GROUP), low(groups, GROUP, width),
            sem((2, 2, 7)), sem((2, 4)), sem((5,)), sem((groups, 5)),
        ],
        compiler_params=pltpu.CompilerParams(
            vmem_limit_bytes=VMEM_LIMIT, collective_id=2, has_side_effects=True
        ),
        cost_estimate=pl.CostEstimate(flops=2 * 10**10, bytes_accessed=4 * 10**7, transcendentals=0),
        name="front",
    )(tokens, cot, wq, wk, wv, wg, wb, conv, gain, wo, norm1, norm2)


class Refs(typing.NamedTuple):
    hidden: typing.Any
    tokens: typing.Any
    cot: typing.Any
    second: typing.Any
    wb: typing.Any
    conv: typing.Any
    gain: typing.Any
    beta: typing.Any
    norm1: typing.Any
    norm2: typing.Any
    early: typing.Any
    yn: typing.Any
    dy: typing.Any
    xn: typing.Any
    wg: typing.Any
    wu: typing.Any
    wd: typing.Any
    wq: typing.Any
    wk: typing.Any
    wv: typing.Any
    wgo: typing.Any
    wo: typing.Any
    mixed: typing.Any
    resid: typing.Any
    inv: typing.Any
    out: typing.Any
    ingrad: typing.Any
    smalls: typing.Any
    lefts: typing.Any
    gws: typing.Any
    gns: typing.Any
    lows: typing.Any
    paw: typing.Any
    pan: typing.Any
    pbw: typing.Any
    pbn: typing.Any
    own: typing.Any
    wide: typing.Any
    r1w: typing.Any
    r1n: typing.Any
    r2w: typing.Any
    r2n: typing.Any
    rfw: typing.Any
    rfn: typing.Any
    rows: typing.Any
    dh: typing.Any
    state: typing.Any
    small: typing.Any
    first: typing.Any
    smallr: typing.Any
    dconv: typing.Any
    dgain: typing.Any
    bl: typing.Any
    lsem: typing.Any
    rsem: typing.Any
    csem: typing.Any
    qsem: typing.Any
    ssem: typing.Any
    zsem: typing.Any
    fsem: typing.Any
    psem: typing.Any
    msem: typing.Any
    osem: typing.Any


def block_kernel(*refs):
    outs = refs[28 : 28 + COUNT]
    r = Refs(*refs[:28], *refs[28 + COUNT :])
    own, wide, dh, state, small = r.own, r.wide, r.dh, r.state, r.small
    recv1, recv2, recvf = (r.r1w, r.r1n), (r.r2w, r.r2n), (r.rfw, r.rfn)
    landed = (r.gws, r.gns)
    relay = ((r.paw, r.pan), (r.pbw, r.pbn))
    tokens, width = r.second.shape
    place = Place(tokens)
    bit, to, near = place.bit, place.to, place.near
    own_rows, other_rows = place.own_rows, place.other_rows
    quarter, eighth = width // 8, width // 16
    half2, mine2 = bit[GATHER_2], bit[BIT_ZB]
    end = bit[BIT_ZA] == bit[BIT_ZB]
    inner = bit[BIT_ZA] != bit[BIT_ZB]
    lefts = Lefts((2, 3), place, own, r.lefts, r.lsem, r.csem)

    def source(kind, half):
        group, place, _ = KINDS[kind]
        if group == 0:
            return wide.at[half, place]
        return r.mixed.at[half] if place == 0 else r.lows.at[half, place - 1]

    def right_landed(kind, piece):
        group, place, _ = KINDS[kind]
        return landed[group].at[place, piece - 1]

    split = wide.shape[-1] // HEAD // 2 * HEAD + HEAD

    def parts(kind):
        return 2 if KINDS[kind][0] == 0 else 1

    def right_copy(kind, name, part):
        columns = slice(None)
        if parts(kind) == 2:
            columns = slice(0, split) if part == 0 else slice(split, wide.shape[-1])
        view = lambda ref: ref.at[:, columns]
        if name == "one":
            return remote(
                view(source(kind, half2)), view(right_landed(kind, 1)), r.rsem, (kind, 0, part),
                to[GATHER_1[KINDS[kind][2]]],
            )
        if name == "two":
            return remote(
                view(source(kind, 1 - half2)), view(right_landed(kind, 2)), r.rsem,
                (kind, 1, part), to[GATHER_2],
            )
        return remote(
            view(right_landed(kind, 2)), view(right_landed(kind, 3)), r.rsem, (kind, 2, part),
            to[GATHER_1[KINDS[kind][2]]],
        )

    def one(kind, part):
        right_copy(kind, "one", part).start()

    def two(kind, part):
        right_copy(kind, "two", part).start()

    def far(kind, part):
        right_copy(kind, "two", part).wait_recv()
        right_copy(kind, "far", part).start()

    def run(items, actions):
        for item in items:
            digits = (item % 10,) if item >= 1000 else (item // 10 % 10, item % 10)
            actions[item // 100](*digits)

    copy_actions = {0: one, 1: far, 8: two, 11: lefts.middle, 12: lefts.far}

    def run_at(step, table):
        for when, items in table.items():

            @pl.when(step == when)
            def _(items=items):
                run(items, copy_actions)

    def row_copy(index, source_ref):
        target = dh.at[own_rows, :] if index == 3 else r.rows.at[index]
        return remote(source_ref, target, r.qsem, (index,), near)

    def small_lanes(split, flip):
        index = {1: 0, 2: bit[BIT_Y], 4: 2 * bit[BIT_Y] + bit[BIT_X]}[split]
        if flip:
            index = {2: 1 - index, 4: index + 1 - 2 * bit[BIT_X]}[split]
        return pl.ds(pl.multiple_of(index * (width // split), HEAD), width // split)

    def small_copy(stage):
        target = r.smallr.at[stage]
        if stage == len(SMALL_STAGES):
            return remote(
                small.at[SMALL_ROWS - 8 :, :], target.at[:8, :], r.psem, (stage,), near
            )
        mask, split, _ = SMALL_STAGES[stage]
        lanes = small_lanes(split, False)
        return remote(small.at[:, lanes], target.at[:, lanes], r.psem, (stage,), to[mask])

    def small_sum(stage):
        small_copy(stage).wait()
        if stage == len(SMALL_STAGES):
            small[SMALL_ROWS - 8 :, :] += r.smallr[stage, :8, :]
            return
        _, split, add = SMALL_STAGES[stage]
        lanes = small_lanes(split, not add)
        if add:
            small[:, lanes] += r.smallr[stage, :, lanes]
        else:
            small[:, lanes] = r.smallr[stage, :, lanes]

    steps = wide.shape[-1] // HEAD
    pairs = r.wq.shape[1] // PAIR

    def mixer_copies(pair, slot, wbuf, wobuf, resid_buf, inv_buf):
        columns = pl.ds(pl.multiple_of(pair * PAIR, PAIR), PAIR)
        sems = r.msem
        for index, weight in enumerate((r.wq, r.wk, r.wv, r.wgo)):
            yield pltpu.make_async_copy(
                weight.at[:, columns], wbuf.at[slot, index], sems.at[slot, index]
            )
        yield pltpu.make_async_copy(r.wo.at[columns, :], wobuf.at[slot], sems.at[slot, 4])
        yield pltpu.make_async_copy(
            r.resid.at[:, :, columns], resid_buf.at[slot], sems.at[slot, 5]
        )
        yield pltpu.make_async_copy(
            r.inv.at[pl.ds(2 * pair, 2)], inv_buf.at[slot], sems.at[slot, 6]
        )

    def mlp_phase(prefetch, yn, dy, wg_buf, wu_buf, wd_buf, down_total, back_total, stage):
        weights = (r.wg, r.wu, r.wd, wg_buf, wu_buf, wd_buf, r.msem)
        loads = [
            pltpu.make_async_copy(r.yn, yn, r.csem.at[4]),
            pltpu.make_async_copy(r.dy, dy, r.csem.at[5]),
        ]
        for copy in (*loads, *mlp_copies(0, 0, *weights)):
            copy.start()
        place.greet((*to.values(), place.mirror, near))
        lefts.start(0, r.second)
        run(FIRST_STEPS, copy_actions)
        for copy in loads:
            copy.wait()

        @pl.loop(0, steps)
        def _(step):
            columns = pl.ds(pl.multiple_of(step * HEAD, HEAD), HEAD)

            def low_store(half, kind, value):
                wide[half, kind, :, columns] = value

            mlp_tile(step, steps, yn, dy, weights, low_store, down_total, back_total)
            run_at(step, TILE_STEPS)

        run(LAST_TILE_STEPS, copy_actions)
        prefetch()
        for index, total in enumerate((down_total, back_total)):
            stage[index] = total[other_rows, :].astype(BF16)
            row_copy(index, stage.at[index]).start()
        for index in range(2):
            row_copy(index, stage.at[index]).wait()
        hidden = r.hidden[...]
        r.out[...] = (hidden + down_total[own_rows, :] + r.rows[0].astype(F32)).astype(BF16)
        second_grad = back_total[own_rows, :] + r.rows[1].astype(F32)
        scale = lax.rsqrt(jnp.mean(hidden * hidden, -1, keepdims=True) + norm_eps)
        small[...] = jnp.zeros_like(small)
        small[17:18, :] = jnp.sum(second_grad * hidden * scale, 0, keepdims=True)
        grad = r.cot[...].astype(F32) + norm_back(second_grad, hidden, scale, r.norm2[...])
        state[...] = grad
        dh[own_rows, :] = grad.astype(BF16)
        row_copy(3, dh.at[own_rows, :]).start()
        lefts.start(1, dh[own_rows, :])
        row_copy(3, dh.at[own_rows, :]).wait()

    def mixer_phase(buffers, xn, total, beta_total, low_stage):
        wbuf, wobuf, resid_buf, inv_buf = buffers
        load = pltpu.make_async_copy(r.xn, xn, r.csem.at[6])
        load.start()

        def low_copy(pair, slot):
            target = r.lows.at[
                pair // 2, :, :, pl.ds(pl.multiple_of(lax.rem(pair, 2) * PAIR, PAIR), PAIR)
            ]
            return pltpu.make_async_copy(low_stage.at[slot, 0], target, r.osem.at[slot])

        @pl.loop(0, pairs)
        def _(pair):
            slot = lax.rem(pair, 2)

            @pl.when(pair + 1 < pairs)
            def _():
                for copy in mixer_copies(pair + 1, 1 - slot, *buffers):
                    copy.start()

            for copy in mixer_copies(pair, slot, *buffers):
                copy.wait()

            @pl.when(pair >= 2)
            def _():
                low_copy(pair - 2, slot).wait()

            lanes = pl.ds(pl.multiple_of(pair * PAIR, PAIR), PAIR)
            backward_pair(
                pair, pairs, dh, *(wbuf.at[slot, index] for index in range(4)), r.wb,
                r.conv.at[:, :, lanes], r.gain, wobuf.at[slot], resid_buf.at[slot],
                r.beta, inv_buf.at[slot], low_stage.at[slot], r.bl,
                r.dconv.at[:, :, lanes], r.dgain, total, beta_total,
            )
            low_copy(pair, slot).start()
            run_at(pair, PAIR_STEPS)

        for pair in (pairs - 2, pairs - 1):
            low_copy(pair, pair % 2).wait()
        r.rows[0] = total[other_rows, :].astype(BF16)
        row_copy(2, r.rows.at[0]).start()
        r.first[...] = total[own_rows, :]
        load.wait()
        small[0:8, :] = dot(r.bl[...], xn[...], TN)

    def first_norm_back():
        for kind in range(3):
            for offset in range(CONV):
                row = kind * CONV + offset
                lanes = slice(0, width // 2) if row < 8 else slice(width // 2, width)
                small[8 + row % 8 : 9 + row % 8, lanes] = r.dconv[kind, offset : offset + 1, :]
        small[18:19, :HEAD] = r.dgain[...]
        row_copy(2, r.rows.at[0]).wait()
        first_grad = r.first[...] + r.rows[2].astype(F32)
        inputs = r.tokens[...].astype(F32)
        scale = lax.rsqrt(jnp.mean(inputs * inputs, -1, keepdims=True) + norm_eps)
        small[16:17, :] = jnp.sum(first_grad * inputs * scale, 0, keepdims=True)
        small_copy(0).start()
        state[...] += norm_back(first_grad, inputs, scale, r.norm1[...])
        pltpu.make_async_copy(state, r.ingrad, r.csem.at[7]).start()

    def scoped_mixer(wbuf, wobuf, resid_buf, inv_buf):
        buffers = (wbuf, wobuf, resid_buf, inv_buf)

        def prefetch():
            for copy in mixer_copies(0, 0, *buffers):
                copy.start()

        rows = 2 * tokens
        pl.run_scoped(
            functools.partial(mlp_phase, prefetch),
            pltpu.VMEM((rows, width), BF16), pltpu.VMEM((rows, width), BF16),
            pltpu.VMEM((2, width, PAIR), BF16), pltpu.VMEM((2, width, PAIR), BF16),
            pltpu.VMEM((2, PAIR, width), BF16), pltpu.VMEM((rows, width), F32),
            pltpu.VMEM((rows, width), F32), pltpu.VMEM((2, tokens, width), BF16),
        )
        pl.run_scoped(
            functools.partial(mixer_phase, buffers),
            pltpu.VMEM((rows, width), BF16), pltpu.VMEM((rows, width), F32),
            pltpu.VMEM(r.beta.shape, F32), pltpu.VMEM((2, 1, 4, rows, PAIR), BF16),
        )

    pl.run_scoped(
        scoped_mixer, pltpu.VMEM((2, 4, width, PAIR), BF16), pltpu.VMEM((2, PAIR, width), BF16),
        pltpu.VMEM((2, 6, 2 * tokens, PAIR), F32), pltpu.VMEM((2, 2, 2, tokens, tokens), F32),
    )

    def sums_phase(left, gw, gn, s1w, s1n, s2w, s2n, sfw, sfn, ow, on, cw, cn):
        right, send1 = (gw, gn), (s1w, s1n)
        send2, sendf, out_buf, cross_buf = (s2w, s2n), (sfw, sfn), (ow, on), (cw, cn)

        def left_load(a):
            from_ref = r.early.at[a] if a < 2 else r.lefts.at[a - 2]
            return pltpu.make_async_copy(
                from_ref, left.at[LEFT_SLOT[a]], r.csem.at[8 + LEFT_SLOT[a]]
            )

        def right_loads(kind):
            group = KINDS[kind][0]
            rows = 2 * tokens
            for piece in range(4):
                yield pltpu.make_async_copy(
                    right_landed(kind, piece) if piece else source(kind, half2),
                    right[group].at[kind % 2, piece * rows : (piece + 1) * rows, :],
                    r.csem.at[11 + piece],
                )

        in_slot, right_slot = {}, {}

        def load(kind):
            group, _, a = KINDS[kind]
            right_slot[group, kind % 2] = kind
            fresh = in_slot.get(LEFT_SLOT[a]) != a
            if fresh:
                in_slot[LEFT_SLOT[a]] = a
                if a >= 2:
                    lefts.arrived(a - 2)
                left_load(a).start()
            for part in range(parts(kind)):
                right_copy(kind, "one", part).wait_recv()
                right_copy(kind, "far", part).wait_recv()
            for copy in right_loads(kind):
                copy.start()
            if fresh:
                left_load(a).wait()
            for copy in right_loads(kind):
                copy.wait()

        def product(kind, start):
            group, _, a = KINDS[kind]
            assert in_slot[LEFT_SLOT[a]] == a and right_slot[group, kind % 2] == kind
            lanes = pl.ds(pl.multiple_of(start, quarter), quarter)
            return dot(left[LEFT_SLOT[a], :, lanes], right[group][kind % 2], TN)

        def mine1(kind):
            return bit[REDUCE_1[KINDS[kind][2]]]

        def rows_of(which):
            return pl.ds(pl.multiple_of(which * quarter, quarter), quarter)

        last, stored = {}, {}

        def slot_free(kind, stage, wait):
            key = (KINDS[kind][0], kind % 2, stage)
            if key in last:
                wait(last[key])
            last[key] = kind

        def first_copy(kind, part):
            group, at, _ = KINDS[kind]
            rows = rows_of(1 - mine2 if part == 0 else mine2)
            return remote(
                send1[group].at[kind % 2, rows, :], recv1[group].at[at, rows, :], r.ssem,
                (kind, part), to[REDUCE_1[KINDS[kind][2]]],
            )

        def first_sent(kind):
            for part in range(2):
                first_copy(kind, part).wait_send()

        def first_sums(kind, part):
            if part == 0:
                load(kind)
                slot_free(kind, 0, first_sent)
            group = KINDS[kind][0]
            which = 1 - mine2 if part == 0 else mine2
            send1[group][kind % 2, rows_of(which), :] = product(
                kind, (1 - mine1(kind)) * 2 * quarter + which * quarter
            ).astype(BF16)
            first_copy(kind, part).start()

        def second_copy(kind, part, from_end):
            group, at, _ = KINDS[kind]
            rows = slice(part * eighth, (part + 1) * eighth)
            return remote_pair(
                send2[group].at[kind % 2, rows, :],
                relay[0 if from_end else 1][group].at[at, rows, :],
                r.zsem.at[0, kind, part], r.zsem.at[1 if from_end else 2, kind, part],
                to[BIT_ZA] if from_end else place.mirror,
            )

        def second_sent(kind):
            for part in range(2):
                second_copy(kind, part, True).wait_send()

        def pass_copy(kind, part, which):
            group, at, _ = KINDS[kind]
            rows = slice(part * eighth, (part + 1) * eighth)
            return remote_pair(
                relay[which][group].at[at, rows, :], recv2[group].at[at, rows, :],
                r.fsem.at[which, kind, part], r.fsem.at[2, kind, part],
                place.mirror if which == 0 else to[BIT_ZA],
            )

        def pass_on(kind, part, which):
            @pl.when(inner)
            def _():
                second_copy(kind, part, which == 0).wait_recv()
                pass_copy(kind, part, which).start()

        def second_sums(kind, part):
            group, at, _ = KINDS[kind]
            which = mine2 if part else 1 - mine2
            first_copy(kind, part).wait_recv()
            total = product(kind, mine1(kind) * 2 * quarter + which * quarter) + recv1[group][
                at, rows_of(which), :
            ].astype(F32)
            if part:
                recv1[group][at, rows_of(which), :] = total.astype(BF16)
                return
            slot_free(kind, 1, second_sent)
            send2[group][kind % 2] = total.astype(BF16)
            for from_end, here in ((True, end), (False, inner)):

                @pl.when(here)
                def _():
                    for index in range(2):
                        second_copy(kind, index, from_end).start()

        def last_copy(kind):
            group, at, _ = KINDS[kind]
            return remote(
                sendf[group].at[kind % 2], recvf[group].at[at], r.ssem, (kind, 2), to[GATHER_2]
            )

        def last_sent(kind):
            last_copy(kind).wait_send()

        def out_copy(kind):
            group = KINDS[kind][0]
            buffer = cross_buf[group] if kind in CROSSED else out_buf[group].at[kind % 2]
            return pltpu.make_async_copy(buffer, outs[kind], r.osem.at[2 + kind])

        def store(kind, half, value):
            group = KINDS[kind][0]
            count = value.shape[1]
            start = pl.multiple_of(half * count, HEAD)
            if kind in CROSSED:
                cross_buf[group][pl.ds(start, count), :] = value.T
            else:
                out_buf[group][kind % 2, :, pl.ds(start, count)] = value

        finished = []

        def third_sums(kind):
            group, at, _ = KINDS[kind]
            slot_free(kind, 2, last_sent)
            for part in range(2):
                pass_copy(kind, part, 0).wait_recv()

            def total(which):
                rows = pl.ds(pl.multiple_of(which * eighth, eighth), eighth)
                kept = pl.ds(pl.multiple_of(mine2 * quarter + which * eighth, eighth), eighth)
                return recv1[group][at, kept, :].astype(F32) + recv2[group][at, rows, :].astype(F32)

            sendf[group][kind % 2] = total(1 - half2).astype(BF16)
            last_copy(kind).start()
            key = (group, kind % 2, kind in CROSSED)
            if key in stored:
                assert stored[key] in finished
                out_copy(stored[key]).wait()
            stored[key] = kind
            store(kind, half2, total(half2))

        def finish(kind):
            group, at, _ = KINDS[kind]
            last_copy(kind).wait_recv()
            store(kind, 1 - half2, recvf[group][at].astype(F32))
            out_copy(kind).start()
            finished.append(kind)

        stage = 0

        def small_step(kind, part):
            nonlocal stage
            if part == 1:
                first_norm_back()
                return
            small_sum(stage)
            stage += 1
            if stage <= len(SMALL_STAGES):
                small_copy(stage).start()

        actions = {
            **copy_actions, 2: first_sums, 3: second_sums, 4: lambda kind, part: third_sums(kind),
            5: lambda kind, part: finish(kind), 6: lambda kind, part: pass_on(kind, part, 0),
            7: lambda kind, part: pass_on(kind, part, 1), 9: small_step,
        }
        run(SCHEDULE, actions)
        r.smalls[...] = small[...]
        for (_, _, stage), kind in last.items():
            (first_sent, second_sent, last_sent)[stage](kind)

        @pl.when(inner)
        def _():
            for kind in range(COUNT):
                for part in range(2):
                    for which in range(2):
                        pass_copy(kind, part, which).wait_send()

        for kind in stored.values():
            out_copy(kind).wait()

    wide_cols, cols = wide.shape[-1], r.mixed.shape[-1]
    each = lambda count, height, dtype: [
        pltpu.VMEM((*count, height, wide_cols), dtype), pltpu.VMEM((*count, height, cols), dtype)
    ]
    pl.run_scoped(
        sums_phase, pltpu.VMEM((3, 8 * tokens, width // 2), BF16),
        *each((2,), 8 * tokens, BF16), *each((2,), 2 * quarter, BF16),
        *each((2,), quarter, BF16), *each((2,), eighth, BF16),
        pltpu.VMEM((2, HEAD, 2 * wide_cols), F32), pltpu.VMEM((2, HEAD, 2 * cols), F32),
        pltpu.VMEM((2 * wide_cols, HEAD), F32), pltpu.VMEM((2 * cols, HEAD), F32),
    )
    for a in range(2):
        lefts.sent(a)
    for kind in range(COUNT):
        for name in ("one", "two", "far"):
            for part in range(parts(kind)):
                right_copy(kind, name, part).wait_send()
    pltpu.make_async_copy(state, r.ingrad, r.csem.at[7]).wait()


def call_block(
    hidden, tokens, cot, second, wb, conv, gain, beta, norm1, norm2, early,
    yn, dy, xn, wg, wu, wd, wq, wk, wv, wgo, wo, mixed, resid, inv,
):
    count, width = second.shape
    rows, hidden_cols, cols = 2 * count, wg.shape[1] // 2, wq.shape[1] // 2
    vmem = pl.BlockSpec(memory_space=pltpu.VMEM)
    anywhere = pl.BlockSpec(memory_space=pl.ANY)
    columns = lambda kind: 2 * (hidden_cols, cols)[KINDS[kind][0]]
    shape = lambda kind: (columns(kind), HEAD) if kind in CROSSED else (HEAD, columns(kind))
    sds = jax.ShapeDtypeStruct
    each = lambda height: [
        pltpu.VMEM((3, height, hidden_cols), BF16), pltpu.VMEM((5, height, cols), BF16)
    ]
    sem = pltpu.SemaphoreType.DMA
    half = width // 2
    relay = [sds((3, half // 4, hidden_cols), BF16), sds((5, half // 4, cols), BF16)]
    return pl.pallas_call(
        block_kernel,
        in_specs=[vmem] * 10 + [anywhere] * 15,
        out_specs=[vmem, anywhere, vmem] + [anywhere] * 16,
        out_shape=[
            sds((count, width), BF16), sds((count, width), F32), sds((SMALL_ROWS, width), F32),
            *(sds(shape(kind), F32) for kind in range(COUNT)),
            sds((2, 8 * count, half), BF16), sds((3, 3, rows, hidden_cols), BF16),
            sds((5, 3, rows, cols), BF16), sds((2, 4, rows, cols), BF16), *relay, *relay,
        ],
        scratch_shapes=[
            pltpu.VMEM((2, 2, count, half), BF16), pltpu.VMEM((2, 3, rows, hidden_cols), BF16),
            *each(half // 2), *each(half // 4), *each(half // 8),
            pltpu.VMEM((3, count, width), BF16), pltpu.VMEM((rows, width), BF16),
            pltpu.VMEM((count, width), F32), pltpu.VMEM((SMALL_ROWS, width), F32),
            pltpu.VMEM((count, width), F32),
            pltpu.VMEM((len(SMALL_STAGES) + 1, SMALL_ROWS, width), F32), pltpu.VMEM(conv.shape, F32),
            pltpu.VMEM((1, HEAD), F32), pltpu.VMEM(beta.shape, BF16),
            sem((2, 2, 7)), sem((2, COUNT, 3, 2)), sem((15,)), sem((2, 4)), sem((2, COUNT, 3)),
            sem((3, COUNT, 2)), sem((3, COUNT, 2)), sem((2, len(SMALL_STAGES) + 1)), sem((2, 7)),
            sem((2 + COUNT,)),
        ],
        compiler_params=pltpu.CompilerParams(
            vmem_limit_bytes=62 * 1024 * 1024, collective_id=1, has_side_effects=True
        ),
        cost_estimate=pl.CostEstimate(flops=5 * 10**10, bytes_accessed=2 * 10**8, transcendentals=0),
        name="block",
    )(
        hidden, tokens, cot, second, wb, conv, gain, beta, norm1, norm2, early,
        yn, dy, xn, wg, wu, wd, wq, wk, wv, wgo, wo, mixed, resid, inv,
    )


def finish_kernel(*refs):
    count = (len(refs) - 7) // 3
    small, sources = refs[0], refs[1 : 1 + count]
    n1, n2, conv, head, beta = refs[1 + count : 6 + count]
    targets, held, sems = refs[6 + count : 6 + 2 * count], refs[6 + 2 * count : -1], refs[-1]
    loads, stores = (
        [
            pltpu.make_async_copy(source, target, sems.at[way, index])
            for index, (source, target) in enumerate(zip(*pair, strict=True))
        ]
        for way, pair in enumerate(((sources, held), (held, targets)))
    )
    for load in loads:
        load.start()
    n1[...] = small[16:17, :]
    n2[...] = small[17:18, :]
    head[...] = small[18:19, :HEAD]
    cols = conv.shape[-1]
    for kind in range(3):
        for offset in range(CONV):
            row = kind * CONV + offset
            lanes = slice(0, cols) if row < 8 else slice(cols, 2 * cols)
            conv[kind, offset : offset + 1, :] = small[8 + row % 8 : 9 + row % 8, lanes]
    start = pl.multiple_of(lax.axis_index("dp") * HEAD, HEAD)
    beta[...] = small[0:8, pl.ds(start, HEAD)]
    for load, store in zip(loads, stores):
        load.wait()
        store.start()
    for store in stores:
        store.wait()


def call_finish(small, conv, arrays):
    width = small.shape[1]
    vmem = pl.BlockSpec(memory_space=pltpu.VMEM)
    anywhere = pl.BlockSpec(memory_space=pl.ANY)
    sds = jax.ShapeDtypeStruct
    return pl.pallas_call(
        finish_kernel,
        in_specs=[vmem] + [anywhere] * len(arrays),
        out_specs=[vmem] * 5 + [anywhere] * len(arrays),
        out_shape=[
            sds((1, width), F32), sds((1, width), F32), sds(conv.shape, F32), sds((1, HEAD), F32),
            sds((8, HEAD), F32), *(sds(each.shape, each.dtype) for each in arrays),
        ],
        scratch_shapes=[
            *(pltpu.VMEM(each.shape, each.dtype) for each in arrays),
            pltpu.SemaphoreType.DMA((2, len(arrays))),
        ],
        compiler_params=pltpu.CompilerParams(vmem_limit_bytes=VMEM_LIMIT),
        name="finish",
    )(small, *arrays)


def local(
    tokens, norm1_gain, w_query, w_key, w_value, w_beta, w_gate_out, conv_weights, head_gain,
    w_out, norm2_gain, w_gate, w_up, w_down, cotangent, cubic,
):
    gain_row = head_gain.reshape(1, HEAD)
    beta_rows = w_beta.T
    if cubic:
        norm1_row, norm2_row = norm1_gain.reshape(1, -1), norm2_gain.reshape(1, -1)
        mixed, resid, beta, inverses, hidden_state, second_own, xn, dy, yn, early = call_front(
            tokens, cotangent, w_query, w_key, w_value, w_gate_out, beta_rows, conv_weights,
            gain_row, w_out, norm1_row, norm2_row,
        )
        block_out, input_grad, small, *grads = call_block(
            hidden_state, tokens, cotangent, second_own, beta_rows, conv_weights, gain_row, beta,
            norm1_row, norm2_row, early, yn, dy, xn, w_gate, w_up, w_down, w_query, w_key, w_value,
            w_gate_out, w_out, mixed, resid, inverses,
        )
        norm1_sum, norm2_sum, conv_total, head_sum, beta_sum, block_out, input_grad, *grads = (
            call_finish(small, conv_weights, [block_out, input_grad, *grads[:COUNT]])
        )
        grad_down, grad_gate, grad_up, grad_out = grads[:4]
        grad_query, grad_key, grad_value, grad_gate_out = grads[4:]
        return (
            block_out, input_grad, norm1_sum[0], grad_query, grad_key, grad_value, beta_sum.T,
            grad_gate_out, conv_total, head_sum[0], grad_out, norm2_sum[0], grad_gate, grad_up,
            grad_down,
        )

    core = lax.axis_index("tensor")
    inputs = tokens.astype(F32)
    first_scale = lax.rsqrt(jnp.mean(inputs * inputs, -1, keepdims=True) + norm_eps)
    first_own = (inputs * first_scale * norm1_gain).astype(BF16)
    first_normed = both_rows(first_own, sibling(first_own), core)
    out_grad = both_rows(cotangent, sibling(cotangent), core)
    mixed, out_part, resid, beta, inverses = call_mixer_forward(
        first_normed, w_query, w_key, w_value, w_gate_out, beta_rows, conv_weights, gain_row, w_out
    )
    hidden_state = inputs + swap_sum(out_part, core)
    second_scale = lax.rsqrt(jnp.mean(hidden_state * hidden_state, -1, keepdims=True) + norm_eps)
    second_own = (hidden_state * second_scale * norm2_gain).astype(BF16)
    second_normed = both_rows(second_own, sibling(second_own), core)
    wide, down_part, back_part = call_mlp(second_normed, out_grad, w_gate, w_up, w_down)
    block_out = hidden_state + swap_sum(down_part, core)
    second_grad = swap_sum(back_part, core)
    norm2_part = jnp.sum(second_grad * hidden_state * second_scale, 0)
    state_grad = cotangent.astype(F32) + norm_back(
        second_grad, hidden_state, second_scale, norm2_gain
    )
    state_own = state_grad.astype(BF16)
    state_rows = both_rows(state_own, sibling(state_own), core)
    low, beta_low, first_part, conv_grad, head_part = call_mixer_backward(
        state_rows, w_query, w_key, w_value, w_gate_out, beta_rows, conv_weights, gain_row, w_out,
        resid, beta, inverses,
    )
    first_grad = swap_sum(first_part, core)
    norm1_part = jnp.sum(first_grad * inputs * first_scale, 0)
    input_grad = state_grad + norm_back(first_grad, inputs, first_scale, norm1_gain)
    scatter = lambda value, axis: lax.psum_scatter(value, "dp", scatter_dimension=axis, tiled=True)
    whole = lambda value: jnp.concatenate([value[0], value[1]], 1)
    product, gate_grad, up_grad = (whole(wide[:, kind]) for kind in range(3))
    grad_down = scatter(dot(product, out_grad, TN), 1)
    grad_gate = scatter(dot(second_normed, gate_grad, TN), 0)
    grad_up = scatter(dot(second_normed, up_grad, TN), 0)
    grad_out = scatter(dot(whole(mixed), state_rows, TN), 1)
    grad_query, grad_key, grad_value, grad_gate_out = (
        scatter(dot(first_normed, whole(low[:, kind]), TN), 0) for kind in range(4)
    )
    beta_sum = scatter(dot(first_normed, beta_low, TN), 0)
    conv_total = lax.psum(conv_grad, "dp")
    norm1_sum, norm2_sum, head_sum = lax.psum(
        (norm1_part, norm2_part, head_part.reshape(-1)), ("dp", "tensor")
    )
    return (
        block_out.astype(BF16), input_grad, norm1_sum, grad_query, grad_key, grad_value, beta_sum,
        grad_gate_out, conv_total, head_sum, grad_out, norm2_sum, grad_gate, grad_up, grad_down,
    )


def solution(mesh):
    rows = P(("dp", "tensor"), None)
    columns = P(None, "tensor")
    in_specs = (
        rows, P(), columns, columns, columns, columns, columns, P(None, None, "tensor"), P(),
        P("tensor", None), P(), columns, columns, P("tensor", None), rows,
    )
    scattered = P("dp", "tensor")
    crossed = P("tensor", "dp")
    out_specs = (
        rows, rows, P(), scattered, scattered, scattered, scattered, scattered,
        P(None, None, "tensor"), P(), crossed, P(), scattered, scattered, crossed,
    )
    cubic = mesh.shape["dp"] == 16
    return jax.shard_map(
        functools.partial(local, cubic=cubic), mesh=mesh, in_specs=in_specs, out_specs=out_specs,
        check_vma=False,
    )
```
